32 devices in a mesh: groups: 2 (over y), tensor: 16 (over z, x, core).
Axes of the slice: x: 2, y: 2, z: 4, core: 2. Of those that a mesh axis runs over, the one named last changes fastest.
Arguments:
- tokens: bfloat16 [2048, 8192], P(('groups', 'tensor')), parts along dimension 0, may hold values from -6 to 6
- gate_matrix: bfloat16 [8192, 28672], P(None, 'tensor'), may hold values from -0.0625 to 0.0625
- up_matrix: bfloat16 [8192, 28672], P(None, 'tensor'), may hold values from -0.0625 to 0.0625
- lowrank_down: bfloat16 [16, 64, 8192], P('tensor'), may hold values from -0.0625 to 0.0625
- lowrank_up: bfloat16 [16, 64, 28672], P(None, None, 'tensor'), may hold values from -0.75 to 0.75
- tenant: int32 [16], P('groups'), parts along dimension 0, may hold values from 0 to 15, as said below
- adapter_storage_slot: int32 [16], replicated, may hold values from 0 to 15, each once
- live_count: int32 [16], P('groups'), parts along dimension 0, may hold values from 1 to 128
Outputs:
- hidden: bfloat16 [2048, 28672], P('groups', 'tensor'), parts along dimension 0
The draws below stay inside these ranges and needn't reach their ends.
There are 2 independent parts, one for each index of `groups`. The reference program is written for one: setup_inputs(seed, part) draws one part's arguments, and reference() takes and returns one part's arrays. A program takes and returns all parts, laid end to end along the dimension named above; an argument that names none is the same for every part. Nothing has to cross between parts.
Inputs may be any that keep to these rules, and one draw needn't show every extreme that they name: `tenant`: not all blocks name the same adapter. `adapter_storage_slot`: each storage slot holds exactly one adapter.
All inputs are finite; a program needn't handle non-finite values.
Results may differ from the reference program's by a relative error of at most 0.0046.
Values may be sent and summed in bfloat16 or wider, within the bound.
No kernel may reach another device: no remote copies, remote signals or barrier semaphores. Data moves between devices by JAX's collectives and lax.ppermute only.
A program may use at most 192 MiB of HBM per device.

```python
import jax
import jax.numpy as jnp

MODEL_WIDTH = 8192
HIDDEN_UNITS = 28672
ADAPTER_RANK = 64
BLOCK = 128
BLOCKS = 8
TOKEN_SLOTS = 1024
ADAPTER_COUNT = 16


def draw_tenant(key, part):
    key = jax.random.fold_in(key, 7)
    key_popular, key_pick, key_other, key_last = jax.random.split(key, 4)
    popular = jax.random.randint(key_popular, (), 0, ADAPTER_COUNT, dtype=jnp.int32)
    picked = jax.random.randint(key_pick, (BLOCKS,), 0, 2, dtype=jnp.int32)
    others = jax.random.randint(key_other, (BLOCKS,), 0, ADAPTER_COUNT, dtype=jnp.int32)
    chosen = jnp.where(picked == 1, popular, others).astype(jnp.int32)
    step_away = jax.random.randint(key_last, (), 1, ADAPTER_COUNT, dtype=jnp.int32)
    last_value = ((chosen[0] + step_away) % ADAPTER_COUNT).astype(jnp.int32)
    return chosen.at[BLOCKS - 1].set(last_value)


def touch_ends(entries, stream_key, least, top_value):
    spot = [jax.random.randint(jax.random.fold_in(stream_key, axis), (), 0, length) for axis, length in enumerate(entries.shape)]
    main_axis = entries.shape.index(max(entries.shape))
    beside = spot[:main_axis] + [(spot[main_axis] + 1) % entries.shape[main_axis]] + spot[main_axis + 1:]
    return entries.at[tuple(spot)].set(least).at[tuple(beside)].set(top_value)


def shard_levels(key, extent, cuts, low, largest):
    loudness, own = 1.0, jax.random.fold_in(key, 6)
    for axis_at, blocks in cuts:
        heights = jnp.exp(jax.random.uniform(jax.random.fold_in(own, axis_at), (blocks,), jnp.float32, low / len(cuts), largest / len(cuts)))
        loudness = loudness * jnp.repeat(heights, extent[axis_at] // blocks).reshape([-1 if axis == axis_at else 1 for axis in range(len(extent))])
    return loudness


def centred(rng, shape, width, bound, pieces=(), kind=jnp.bfloat16):
    array = width * jax.random.normal(rng, shape, jnp.float32)
    if pieces:
        array = array * shard_levels(rng, shape, pieces, -0.22, 0.18)
    return jnp.clip(array, -bound, bound).astype(kind)


def setup_inputs(seed: int = 0, part: int = 0) -> dict:
    streams_of = jax.random.split(jax.random.key(seed), 9)
    own_keys = jax.random.split(jax.random.fold_in(streams_of[8], part), 9)
    tokens = centred(own_keys[0], (TOKEN_SLOTS, MODEL_WIDTH), 1.0, 6.0, ((0, 16),))
    gate_matrix = centred(streams_of[1], (MODEL_WIDTH, HIDDEN_UNITS), MODEL_WIDTH ** -0.5, 0.0625, ((1, 16),))
    up_matrix = centred(streams_of[2], (MODEL_WIDTH, HIDDEN_UNITS), MODEL_WIDTH ** -0.5, 0.0625, ((1, 16),))
    lowrank_down = centred(streams_of[3], (ADAPTER_COUNT, ADAPTER_RANK, MODEL_WIDTH), MODEL_WIDTH ** -0.5, 0.0625, ((0, 16),))
    lowrank_up = centred(streams_of[4], (ADAPTER_COUNT, ADAPTER_RANK, HIDDEN_UNITS), ADAPTER_RANK ** -0.5, 0.75, ((2, 16),))
    tenant = draw_tenant(jax.random.fold_in(jax.random.fold_in(streams_of[8], part), 71), part)
    adapter_storage_slot = jax.random.permutation(streams_of[6], ADAPTER_COUNT).astype(jnp.int32)
    live_count = touch_ends(jax.random.randint(own_keys[7], (BLOCKS,), 1, BLOCK + 1), jax.random.fold_in(own_keys[7], 1), 1, BLOCK).astype(jnp.int32)
    return dict(tokens=tokens, gate_matrix=gate_matrix, up_matrix=up_matrix, lowrank_down=lowrank_down, lowrank_up=lowrank_up, tenant=tenant, adapter_storage_slot=adapter_storage_slot, live_count=live_count)


lowrank_scale = 2.0


def reference(tokens, gate_matrix, up_matrix, lowrank_down, lowrank_up, tenant, adapter_storage_slot, live_count):
    gate_out = jnp.dot(tokens, gate_matrix, preferred_element_type=jnp.float32)
    up_output = jnp.dot(tokens, up_matrix, preferred_element_type=jnp.float32)
    slot_numbers = adapter_storage_slot[tenant]
    rows_block = tokens.reshape(BLOCKS, BLOCK, MODEL_WIDTH).astype(jnp.float32)
    adapter_down = lowrank_down[slot_numbers].astype(jnp.float32)
    reduced_output = jnp.einsum("bsd,brd->bsr", rows_block, adapter_down).astype(jnp.bfloat16)
    adapter_up = lowrank_up[slot_numbers].astype(jnp.float32)
    lowrank_term = jnp.einsum("who,wok->whk", reduced_output.astype(jnp.float32), adapter_up)
    up_output = up_output + lowrank_scale * lowrank_term.reshape(TOKEN_SLOTS, HIDDEN_UNITS)
    positions = jnp.arange(BLOCK, dtype=jnp.int32)
    live_rows = (positions[None, :] < live_count[:, None]).reshape(TOKEN_SLOTS, 1)
    hidden = jnp.where(live_rows, jax.nn.silu(gate_out) * up_output, 0.0)
    return hidden.astype(jnp.bfloat16)
```

```python
import jax
import jax.numpy as jnp
from jax import lax
from jax.experimental import pallas as pl
from jax.experimental.pallas import tpu as pltpu
from jax.sharding import PartitionSpec as P

lowrank_scale = 2.0
TILE = 256
VMEM_LIMIT = 48 * 1024 * 1024


def chip_at(place, chips):
    half = chips // 2
    if place < half:
        return 2 * place
    return 2 * (chips - 1 - place) + 1


def ring_pairs(chips, step):
    pairs = []
    for place in range(chips):
        for core in range(2):
            pairs.append((2 * chip_at(place, chips) + core, 2 * chip_at((place + step) % chips, chips) + core))
    return pairs


def pass_call(meta, blocks, down, gate_matrix, up_matrix, earlier, first_tile, tiles, block_len, want_reduced):
    width, columns = gate_matrix.shape
    rank = down.shape[0]
    row_total = earlier[0].shape[0] if not isinstance(earlier[0], tuple) else earlier[0][0]
    fresh = isinstance(earlier[0], tuple)
    count = len(blocks)
    rows = count * block_len
    half = block_len // 2
    flat = []
    places = []
    for number, pieces in enumerate(blocks):
        for piece, sibling, offset in pieces:
            places.append((number * block_len, sibling, offset, piece.shape[0]))
            flat.append(piece)
    n_pieces = len(flat)

    def kernel(*refs):
        meta_ref = refs[0]
        piece_refs = refs[1:1 + n_pieces]
        rest = refs[1 + n_pieces:]
        down_ref, gate_ref, up_ref = rest[:3]
        rest = rest[3:]
        if not fresh:
            rest = rest[2:]
        prod_ref, act_ref = rest[:2]
        rest = rest[2:]
        if want_reduced:
            reduced_ref = rest[0]
            rest = rest[1:]
        held, prod_tile, act_tile, in_sem, out_sem = rest
        step = pl.program_id(0)
        slot = lax.rem(step, 2)

        @pl.when(step == 0)
        def _():
            copies = []
            for k in range(n_pieces):
                base, sibling, offset, length = places[k]
                core = meta_ref[0]
                side = (1 - core) if sibling else core
                start = pl.multiple_of(base + side * half + offset, 32)
                copies.append(pltpu.make_async_copy(piece_refs[k], held.at[pl.ds(start, length)], in_sem.at[k]))
            for copy in copies:
                copy.start()
            for copy in copies:
                copy.wait()
            if want_reduced:
                found = lax.dot_general(held[...], down_ref[...], (((1,), (1,)), ((), ())), preferred_element_type=jnp.float32)
                for b in range(count):
                    part = found[b * block_len:(b + 1) * block_len]
                    reduced_ref[b * block_len:(b + 1) * block_len, :] = jnp.where(meta_ref[1 + 3 * b + 2] == 1, part, 0.0).astype(jnp.bfloat16)

        def out_copies(at_step, at_slot):
            made = []
            for b in range(count):
                block_row = pl.multiple_of(meta_ref[1 + 3 * b] * block_len, block_len)
                col = pl.multiple_of((at_step + first_tile) * TILE, TILE)
                for n, (tile, out) in enumerate(((prod_tile, prod_ref), (act_tile, act_ref))):
                    made.append(pltpu.make_async_copy(
                        tile.at[at_slot, pl.ds(b * block_len, block_len)],
                        out.at[pl.ds(block_row, block_len), pl.ds(col, TILE)],
                        out_sem.at[at_slot, 2 * b + n]))
            return made

        @pl.when(step >= 2)
        def _():
            for copy in out_copies(step - 2, slot):
                copy.wait()

        rows_in = held[...]
        gate_out = jnp.dot(rows_in, gate_ref[...], preferred_element_type=jnp.float32)
        up_out = jnp.dot(rows_in, up_ref[...], preferred_element_type=jnp.float32)
        for b in range(count):
            at = slice(b * block_len, (b + 1) * block_len)
            gate_part = gate_out[at]
            act = gate_part / (1.0 + jnp.exp(-gate_part))
            live = lax.broadcasted_iota(jnp.int32, act.shape, 0) < meta_ref[1 + 3 * b + 1]
            act = jnp.where(live, act, 0.0)
            prod = jnp.where(live, act * up_out[at], 0.0)
            act_tile[slot, at, :] = act.astype(jnp.bfloat16)
            prod_tile[slot, at, :] = prod.astype(jnp.bfloat16)
        for copy in out_copies(step, slot):
            copy.start()

        @pl.when(step == tiles - 1)
        def _():
            if tiles > 1:
                for copy in out_copies(step - 1, 1 - slot):
                    copy.wait()
            for copy in out_copies(step, slot):
                copy.wait()

    weight_spec = pl.BlockSpec((width, TILE), lambda j, m: (0, first_tile + j))
    any_spec = pl.BlockSpec(memory_space=pl.ANY)
    in_specs = [any_spec] * n_pieces + [pl.BlockSpec((rank, width), lambda j, m: (0, 0)), weight_spec, weight_spec]
    operands = [meta] + flat + [down, gate_matrix, up_matrix]
    aliases = {}
    if not fresh:
        in_specs += [any_spec, any_spec]
        aliases = {len(operands): 0, len(operands) + 1: 1}
        operands += list(earlier)
    out_specs = [any_spec, any_spec]
    out_shape = [jax.ShapeDtypeStruct((row_total, columns), jnp.bfloat16)] * 2
    if want_reduced:
        out_specs.append(pl.BlockSpec((rows, rank), lambda j, m: (0, 0)))
        out_shape.append(jax.ShapeDtypeStruct((rows, rank), jnp.bfloat16))
    return pl.pallas_call(
        kernel,
        grid_spec=pltpu.PrefetchScalarGridSpec(
            num_scalar_prefetch=1,
            grid=(tiles,),
            in_specs=in_specs,
            out_specs=out_specs,
            scratch_shapes=[
                pltpu.VMEM((rows, width), jnp.bfloat16),
                pltpu.VMEM((2, rows, TILE), jnp.bfloat16),
                pltpu.VMEM((2, rows, TILE), jnp.bfloat16),
                pltpu.SemaphoreType.DMA((n_pieces,)),
                pltpu.SemaphoreType.DMA((2, 2 * count)),
            ],
        ),
        out_shape=out_shape,
        input_output_aliases=aliases,
        compiler_params=pltpu.CompilerParams(dimension_semantics=("arbitrary",), vmem_limit_bytes=VMEM_LIMIT),
        cost_estimate=pl.CostEstimate(
            flops=4 * rows * width * TILE * tiles, bytes_accessed=4 * width * TILE * tiles, transcendentals=0),
    )(*operands)


def table_call(meta, pieces, down, owned, row_total, block_len):
    rank, width = down.shape
    half = block_len // 2
    n_pieces = len(pieces)
    n_owned = len(owned)

    def kernel(*refs):
        meta_ref = refs[0]
        piece_refs = refs[1:1 + n_pieces]
        down_ref = refs[1 + n_pieces]
        owned_refs = refs[2 + n_pieces:2 + n_pieces + n_owned]
        table_ref, held, in_sem = refs[2 + n_pieces + n_owned:]
        copies = []
        for k, (piece, sibling, offset) in enumerate(pieces):
            core = meta_ref[0]
            side = (1 - core) if sibling else core
            start = pl.multiple_of(side * half + offset, 32)
            copies.append(pltpu.make_async_copy(piece_refs[k], held.at[pl.ds(start, piece.shape[0])], in_sem.at[k]))
        for copy in copies:
            copy.start()
        number = 0
        for ref in owned_refs:
            for b in range(ref.shape[0] // block_len):
                row = pl.multiple_of(meta_ref[1 + 3 * number] * block_len, block_len)
                table_ref[pl.ds(row, block_len), :] = ref[b * block_len:(b + 1) * block_len, :]
                number += 1
        for copy in copies:
            copy.wait()
        found = lax.dot_general(held[...], down_ref[...], (((1,), (1,)), ((), ())), preferred_element_type=jnp.float32)
        row = pl.multiple_of(meta_ref[1 + 3 * number] * block_len, block_len)
        table_ref[pl.ds(row, block_len), :] = jnp.where(meta_ref[1 + 3 * number + 2] == 1, found, 0.0).astype(jnp.bfloat16)

    whole = pl.BlockSpec(memory_space=pltpu.VMEM)
    return pl.pallas_call(
        kernel,
        in_specs=[pl.BlockSpec(memory_space=pltpu.SMEM)] + [pl.BlockSpec(memory_space=pl.ANY)] * n_pieces + [whole] * (1 + n_owned),
        out_specs=whole,
        out_shape=jax.ShapeDtypeStruct((row_total, rank), jnp.bfloat16),
        scratch_shapes=[pltpu.VMEM((block_len, width), jnp.bfloat16), pltpu.SemaphoreType.DMA((n_pieces,))],
        compiler_params=pltpu.CompilerParams(vmem_limit_bytes=VMEM_LIMIT),
        cost_estimate=pl.CostEstimate(flops=2 * block_len * width * 256, bytes_accessed=4 * 1024 * 1024, transcendentals=0),
    )(meta, *[piece for piece, _, _ in pieces], down, *owned)


def finish_call(slots, table, lowrank_up, prod, act, block_len):
    row_total, columns = prod.shape
    rank = table.shape[1]

    def kernel(slots_ref, table_ref, map_ref, prod_ref, act_ref, out_ref):
        term = jnp.dot(table_ref[...], map_ref[0], preferred_element_type=jnp.float32)
        total = prod_ref[...].astype(jnp.float32) + act_ref[...].astype(jnp.float32) * (lowrank_scale * term)
        out_ref[...] = total.astype(jnp.bfloat16)

    row_spec = pl.BlockSpec((block_len, columns), lambda b, s: (b, 0))
    return pl.pallas_call(
        kernel,
        grid_spec=pltpu.PrefetchScalarGridSpec(
            num_scalar_prefetch=1,
            grid=(row_total // block_len,),
            in_specs=[
                pl.BlockSpec((block_len, rank), lambda b, s: (b, 0)),
                pl.BlockSpec((1, rank, columns), lambda b, s: (s[b], 0, 0)),
                row_spec,
                row_spec,
            ],
            out_specs=row_spec,
        ),
        out_shape=jax.ShapeDtypeStruct((row_total, columns), jnp.bfloat16),
        input_output_aliases={3: 0},
        compiler_params=pltpu.CompilerParams(dimension_semantics=("arbitrary",), vmem_limit_bytes=VMEM_LIMIT),
        cost_estimate=pl.CostEstimate(
            flops=2 * row_total * columns * 256, bytes_accessed=6 * row_total * columns, transcendentals=0),
    )(slots, table, lowrank_up, prod, act)


def on_ring(tokens, gate_matrix, up_matrix, lowrank_down, lowrank_up, tenant, adapter_storage_slot, live_count):
    block_count = tenant.shape[0]
    rows_here, width = tokens.shape
    chips = block_count
    block_len = 2 * rows_here
    row_total = block_count * block_len
    columns = gate_matrix.shape[1]
    me = lax.axis_index("tensor")
    core = lax.rem(me, 2)
    chip = me // 2
    place = jnp.where(lax.rem(chip, 2) == 0, chip // 2, chips - 1 - chip // 2)
    order = jnp.array([0, -1, 1, -2, 2, -3, 3, -4], jnp.int32)
    at = lax.rem(place + order + chips, chips)
    numbers = jnp.where(at < chips // 2, 2 * at, 2 * (chips - 1 - at) + 1)
    slots = adapter_storage_slot[tenant]
    here = (slots == me).astype(jnp.int32)
    fields = jnp.stack([numbers, live_count[numbers], here[numbers]], axis=1).astype(jnp.int32)

    def meta_of(first, count):
        return jnp.concatenate([core[None].astype(jnp.int32), fields[first:first + count].reshape(-1)])

    right, left = ring_pairs(chips, 1), ring_pairs(chips, -1)
    swap = [(d, d ^ 1) for d in range(2 * chips)]

    def send(value, pairs):
        return lax.ppermute(value, "tensor", pairs)

    down = lowrank_down[0]
    rest = (gate_matrix, up_matrix)
    n_tiles = columns // TILE
    from_left, from_right = tokens, tokens
    other = send(tokens, swap)
    blocks = [[(tokens, False, 0), (other, True, 0)]]
    state = ((row_total, columns), (row_total, columns))
    owned = []
    first = 0
    for step in range(3):
        from_left = send(from_left, right)
        from_right = send(from_right, left)
        prod, act, part = pass_call(meta_of(first, len(blocks)), blocks, down, *rest, state, 0, n_tiles, block_len, True)
        state = (prod, act)
        owned.append(part)
        first += len(blocks)
        blocks = [[(v, False, 0), (send(v, swap), True, 0)] for v in (from_left, from_right)]
    cut = rows_here // 2
    last_low = send(from_left[:cut], right)
    last_high = send(from_right[cut:], left)
    prod, act, part = pass_call(meta_of(first, 2), blocks, down, *rest, state, 0, n_tiles, block_len, True)
    state = (prod, act)
    owned.append(part)
    first += 2
    pieces = [
        (last_low, False, 0), (send(last_low, swap), True, 0),
        (last_high, False, cut), (send(last_high, swap), True, cut),
    ]
    table = table_call(meta_of(0, block_count), pieces, down, owned, row_total, block_len)
    for bit in (1, 2, 4, 8):
        table = table + send(table, [(d, d ^ bit) for d in range(2 * chips)])
    start = 0
    for count in (2, 2, 2, 1):
        state = pass_call(meta_of(first, 1), [pieces], down, *rest, state, start, count, block_len, False)
        start += count
    return finish_call(slots, table, lowrank_up, *state, block_len)


def on_device(
    tokens,
    gate_matrix,
    up_matrix,
    lowrank_down,
    lowrank_up,
    tenant,
    adapter_storage_slot,
    live_count,
):
    my_index = lax.axis_index("tensor")
    gathered = lax.all_gather(tokens, "tensor", axis=0, tiled=True)
    row_total = gathered.shape[0]
    width = gathered.shape[1]
    block_count = tenant.shape[0]
    block_len = row_total // block_count
    hidden_columns = gate_matrix.shape[1]
    gate_out = jnp.dot(gathered, gate_matrix, preferred_element_type=jnp.float32)
    up_output = jnp.dot(gathered, up_matrix, preferred_element_type=jnp.float32)
    slot_numbers = adapter_storage_slot[tenant]
    rows_block = gathered.reshape(block_count, block_len, width)
    per_replica = lowrank_down.shape[0]
    rank_width = lowrank_down.shape[1]
    first_slot = my_index * per_replica
    pieces = []
    for block in range(block_count):
        slot_here = slot_numbers[block]
        mine = jnp.logical_and(slot_here >= first_slot, slot_here < first_slot + per_replica)
        resident_slot = jnp.clip(slot_here - first_slot, 0, per_replica - 1)
        down_matrix = lax.dynamic_index_in_dim(lowrank_down, resident_slot, 0, keepdims=False)
        block_rows = rows_block[block]

        def product_fn(rows_in=block_rows, map_in=down_matrix):
            return lax.dot_general(
                rows_in, map_in, (((1,), (1,)), ((), ())), preferred_element_type=jnp.float32
            )

        def empty_fn():
            return jnp.zeros((block_len, rank_width), jnp.float32)

        pieces.append(lax.cond(mine, product_fn, empty_fn))
    partial_value = jnp.stack(pieces, axis=0)
    reduced_output = lax.psum(partial_value, "tensor").astype(jnp.bfloat16)
    every_slot = jnp.arange(lowrank_up.shape[0], dtype=jnp.int32)
    slot_indicator = (slot_numbers[:, None] == every_slot[None, :]).astype(jnp.bfloat16)
    adapter_up = jnp.einsum(
        "oe,exz->oxz", slot_indicator, lowrank_up, preferred_element_type=jnp.float32
    ).astype(jnp.bfloat16)
    lowrank_term = jnp.einsum(
        "who,wok->whk", reduced_output, adapter_up, preferred_element_type=jnp.float32
    )
    up_output = up_output + lowrank_scale * lowrank_term.reshape(row_total, hidden_columns)
    positions = jnp.arange(block_len, dtype=jnp.int32)
    live_rows = (positions[None, :] < live_count[:, None]).reshape(row_total, 1)
    hidden = jnp.where(live_rows, jax.nn.silu(gate_out) * up_output, 0.0)
    return hidden.astype(jnp.bfloat16)


def solution(mesh):
    placed = (
        P(("groups", "tensor"), None),
        P(None, "tensor"),
        P(None, "tensor"),
        P("tensor", None, None),
        P(None, None, "tensor"),
        P("groups"),
        P(),
        P("groups"),
    )
    run = on_ring if mesh.shape["tensor"] == 16 else on_device
    return jax.shard_map(
        run, mesh=mesh, in_specs=placed, out_specs=P("groups", "tensor"), check_vma=False
    )
```

```python
import jax
import jax.numpy as jnp
from jax import lax
from jax.experimental import pallas as pl
from jax.experimental.pallas import tpu as pltpu
from jax.sharding import PartitionSpec as P

lowrank_scale = 2.0
TILE = 256
KEPT = 3
VMEM_LIMIT = 30 * 1024 * 1024


def chip_at(place, chips):
    half = chips // 2
    if place < half:
        return 2 * place
    return 2 * (chips - 1 - place) + 1


def ring_pairs(chips, step):
    pairs = []
    for place in range(chips):
        for core in range(2):
            pairs.append((2 * chip_at(place, chips) + core, 2 * chip_at((place + step) % chips, chips) + core))
    return pairs


def pass_call(meta, first, blocks, down, gate_matrix, up_matrix, kept, earlier, tiles, block_len, want_reduced):
    width, columns = gate_matrix.shape
    rank = down.shape[0]
    fresh = kept is None
    row_total = earlier[0] if fresh else earlier[0].shape[0]
    count = len(blocks)
    rows = count * block_len
    half = block_len // 2
    n_kept = len([t for t in tiles if t < KEPT])
    n_streamed = len(tiles) - n_kept
    first_streamed = KEPT
    flat = []
    places = []
    for number, pieces in enumerate(blocks):
        for piece, sibling, offset in pieces:
            places.append((number * block_len, sibling, offset, piece.shape[0]))
            flat.append(piece)
    n_pieces = len(flat)

    def kernel(*refs):
        meta_ref = refs[0]
        piece_refs = refs[1:1 + n_pieces]
        rest = refs[1 + n_pieces:]
        if want_reduced:
            down_ref = rest[0]
            rest = rest[1:]
        gate_ref, up_ref = rest[:2]
        rest = rest[2:]
        if fresh:
            prod_ref, act_ref, kept_gate, kept_up = rest[:4]
            rest = rest[4:]
        else:
            prod_ref, act_ref, kept_gate, kept_up = rest[4:8]
            rest = rest[8:]
        if want_reduced:
            reduced_ref = rest[0]
            rest = rest[1:]
        held, gate_in, up_in, prod_tile, act_tile, in_sem, kept_sem, stream_sem, out_sem = rest

        def kept_copies(t):
            col = pl.multiple_of(t * TILE, TILE)
            return [
                pltpu.make_async_copy(gate_ref.at[:, pl.ds(col, TILE)], kept_gate.at[t], kept_sem.at[0, t]),
                pltpu.make_async_copy(up_ref.at[:, pl.ds(col, TILE)], kept_up.at[t], kept_sem.at[1, t]),
            ]

        def stream_copies(s):
            col = pl.multiple_of((first_streamed + s) * TILE, TILE)
            slot = lax.rem(s, 2)
            return [
                pltpu.make_async_copy(gate_ref.at[:, pl.ds(col, TILE)], gate_in.at[slot], stream_sem.at[0, slot]),
                pltpu.make_async_copy(up_ref.at[:, pl.ds(col, TILE)], up_in.at[slot], stream_sem.at[1, slot]),
            ]

        def start(copies):
            for copy in copies:
                copy.start()

        def wait(copies):
            for copy in copies:
                copy.wait()

        core = meta_ref[0]
        arrivals = []
        for k in range(n_pieces):
            base, sibling, offset, length = places[k]
            side = (1 - core) if sibling else core
            row = pl.multiple_of(base + side * half + offset, 32)
            arrivals.append(pltpu.make_async_copy(piece_refs[k], held.at[pl.ds(row, length)], in_sem.at[k]))
        start(arrivals)
        if fresh:
            for t in range(n_kept):
                start(kept_copies(t))
        for s in range(min(2, n_streamed)):
            start(stream_copies(s))
        wait(arrivals)
        if want_reduced:
            found = lax.dot_general(held[...], down_ref[...], (((1,), (1,)), ((), ())), preferred_element_type=jnp.float32)
            for b in range(count):
                at = slice(b * block_len, (b + 1) * block_len)
                reduced_ref[at, :] = jnp.where(meta_ref[1 + 3 * (first + b) + 2] == 1, found[at], 0.0).astype(jnp.bfloat16)

        def out_copies(done, tile_at):
            slot = lax.rem(done, 2)
            col = pl.multiple_of(tile_at * TILE, TILE)
            made = []
            for b in range(count):
                block_row = pl.multiple_of(meta_ref[1 + 3 * (first + b)] * block_len, block_len)
                for n, (tile, out) in enumerate(((prod_tile, prod_ref), (act_tile, act_ref))):
                    made.append(pltpu.make_async_copy(
                        tile.at[slot, pl.ds(b * block_len, block_len)],
                        out.at[pl.ds(block_row, block_len), pl.ds(col, TILE)],
                        out_sem.at[slot, 2 * b + n]))
            return made

        def compute(done, tile_at, gate_tile, up_tile):
            @pl.when(done >= 2)
            def _():
                wait(out_copies(done - 2, tile_at))

            slot = lax.rem(done, 2)
            rows_in = held[...]
            gate_out = jnp.dot(rows_in, gate_tile, preferred_element_type=jnp.float32)
            up_out = jnp.dot(rows_in, up_tile, preferred_element_type=jnp.float32)
            for b in range(count):
                at = slice(b * block_len, (b + 1) * block_len)
                gate_part = gate_out[at]
                act = gate_part / (1.0 + jnp.exp(-gate_part))
                live = lax.broadcasted_iota(jnp.int32, act.shape, 0) < meta_ref[1 + 3 * (first + b) + 1]
                act_tile[slot, at, :] = jnp.where(live, act, 0.0).astype(jnp.bfloat16)
                prod_tile[slot, at, :] = jnp.where(live, act * up_out[at], 0.0).astype(jnp.bfloat16)
            start(out_copies(done, tile_at))

        if n_kept:
            def on_kept(t, carry):
                if fresh:
                    wait(kept_copies(t))
                compute(t, t, kept_gate[t], kept_up[t])
                return carry

            lax.fori_loop(0, n_kept, on_kept, 0)
        if n_streamed:
            def on_streamed(s, carry):
                wait(stream_copies(s))
                slot = lax.rem(s, 2)
                compute(n_kept + s, first_streamed + s, gate_in[slot], up_in[slot])

                @pl.when(s + 2 < n_streamed)
                def _():
                    start(stream_copies(s + 2))
                return carry

            lax.fori_loop(0, n_streamed, on_streamed, 0)
        total = n_kept + n_streamed
        for done in range(max(0, total - 2), total):
            wait(out_copies(done, 0))

    any_spec = pl.BlockSpec(memory_space=pl.ANY)
    vmem_spec = pl.BlockSpec(memory_space=pltpu.VMEM)
    in_specs = [any_spec] * n_pieces
    operands = [meta] + flat
    if want_reduced:
        in_specs.append(vmem_spec)
        operands.append(down)
    in_specs += [any_spec, any_spec]
    operands += [gate_matrix, up_matrix]
    result = jax.ShapeDtypeStruct((row_total, columns), jnp.bfloat16)
    out_specs = [any_spec, any_spec, vmem_spec, vmem_spec]
    out_shape = [result, result] + [pltpu.VMEM((KEPT, width, TILE), jnp.bfloat16)] * 2
    aliases = {}
    if not fresh:
        in_specs += [any_spec, any_spec, vmem_spec, vmem_spec]
        aliases = {len(operands) + k: k for k in range(4)}
        operands += list(earlier) + list(kept)
    if want_reduced:
        out_specs.append(vmem_spec)
        out_shape.append(jax.ShapeDtypeStruct((rows, rank), jnp.bfloat16))
    buffers = min(2, n_streamed) or 1
    stream_shape = (buffers, width, TILE) if n_streamed else (1, 16, 128)
    return pl.pallas_call(
        kernel,
        grid_spec=pltpu.PrefetchScalarGridSpec(
            num_scalar_prefetch=1,
            grid=(1,),
            in_specs=in_specs,
            out_specs=out_specs,
            scratch_shapes=[
                pltpu.VMEM((rows, width), jnp.bfloat16),
                pltpu.VMEM(stream_shape, jnp.bfloat16),
                pltpu.VMEM(stream_shape, jnp.bfloat16),
                pltpu.VMEM((2, rows, TILE), jnp.bfloat16),
                pltpu.VMEM((2, rows, TILE), jnp.bfloat16),
                pltpu.SemaphoreType.DMA((n_pieces,)),
                pltpu.SemaphoreType.DMA((2, KEPT)),
                pltpu.SemaphoreType.DMA((2, 2)),
                pltpu.SemaphoreType.DMA((2, 2 * count)),
            ],
        ),
        out_shape=out_shape,
        input_output_aliases=aliases,
        compiler_params=pltpu.CompilerParams(dimension_semantics=("arbitrary",), vmem_limit_bytes=VMEM_LIMIT),
        cost_estimate=pl.CostEstimate(
            flops=4 * rows * width * TILE * len(tiles),
            bytes_accessed=4 * width * TILE * (len(tiles) if fresh else n_streamed), transcendentals=0),
    )(*operands)


def place_call(meta, owned, row_total, block_len):
    rank = owned[0].shape[1]

    def kernel(*refs):
        meta_ref, table_ref = refs[0], refs[-1]
        table_ref[...] = jnp.zeros_like(table_ref)
        number = 0
        for ref in refs[1:-1]:
            for b in range(ref.shape[0] // block_len):
                row = pl.multiple_of(meta_ref[1 + 3 * number] * block_len, block_len)
                table_ref[pl.ds(row, block_len), :] = ref[b * block_len:(b + 1) * block_len, :]
                number += 1

    whole = pl.BlockSpec(memory_space=pltpu.VMEM)
    return pl.pallas_call(
        kernel,
        in_specs=[pl.BlockSpec(memory_space=pltpu.SMEM)] + [whole] * len(owned),
        out_specs=whole,
        out_shape=jax.ShapeDtypeStruct((row_total, rank), jnp.bfloat16),
        compiler_params=pltpu.CompilerParams(vmem_limit_bytes=4 * 1024 * 1024),
        cost_estimate=pl.CostEstimate(flops=0, bytes_accessed=1024 * 1024, transcendentals=0),
    )(meta, *owned)


def late_call(meta, first, pieces, down, owned, block_len):
    rank, width = down.shape
    half = block_len // 2
    n_pieces = len(pieces)

    def kernel(*refs):
        meta_ref = refs[0]
        piece_refs = refs[1:1 + n_pieces]
        down_ref, owned_ref, late_ref, held, in_sem = refs[1 + n_pieces:]
        core = meta_ref[0]
        copies = []
        for k, (piece, sibling, offset) in enumerate(pieces):
            side = (1 - core) if sibling else core
            row = pl.multiple_of(side * half + offset, 32)
            copies.append(pltpu.make_async_copy(piece_refs[k], held.at[pl.ds(row, piece.shape[0])], in_sem.at[k]))
        for copy in copies:
            copy.start()
        late_ref[:2 * block_len, :] = owned_ref[...]
        for copy in copies:
            copy.wait()
        found = lax.dot_general(held[...], down_ref[...], (((1,), (1,)), ((), ())), preferred_element_type=jnp.float32)
        late_ref[2 * block_len:, :] = jnp.where(meta_ref[1 + 3 * first + 2] == 1, found, 0.0).astype(jnp.bfloat16)

    whole = pl.BlockSpec(memory_space=pltpu.VMEM)
    return pl.pallas_call(
        kernel,
        in_specs=[pl.BlockSpec(memory_space=pltpu.SMEM)] + [pl.BlockSpec(memory_space=pl.ANY)] * n_pieces + [whole] * 2,
        out_specs=whole,
        out_shape=jax.ShapeDtypeStruct((3 * block_len, rank), jnp.bfloat16),
        scratch_shapes=[pltpu.VMEM((block_len, width), jnp.bfloat16), pltpu.SemaphoreType.DMA((n_pieces,))],
        compiler_params=pltpu.CompilerParams(vmem_limit_bytes=12 * 1024 * 1024),
        cost_estimate=pl.CostEstimate(flops=2 * block_len * width * 256, bytes_accessed=4 * 1024 * 1024, transcendentals=0),
    )(meta, *[piece for piece, _, _ in pieces], down, owned)


def finish_call(numbers, base, early, late, lowrank_up, prod, act, block_len):
    row_total, columns = prod.shape
    rank = early.shape[1]
    n_late = len(late)

    def kernel(*refs):
        numbers_ref, early_ref = refs[:2]
        late_refs = refs[2:2 + n_late]
        map_ref, prod_ref, act_ref, out_ref, entries = refs[2 + n_late:]
        b = pl.program_id(0)

        @pl.when(b == 0)
        def _():
            at = 0
            for ref in late_refs:
                entries[at:at + ref.shape[0], :] = ref[...]
                at += ref.shape[0]

        reduced = early_ref[...]
        for kind in range(3):
            row = pl.multiple_of(numbers_ref[base + 5 * b + 2 + kind] * block_len, block_len)
            reduced = reduced + entries[pl.ds(row, block_len), :]
        term = jnp.dot(reduced, map_ref[0], preferred_element_type=jnp.float32)
        total = prod_ref[...].astype(jnp.float32) + act_ref[...].astype(jnp.float32) * (lowrank_scale * term)
        live = lax.broadcasted_iota(jnp.int32, total.shape, 0) < numbers_ref[base + 5 * b + 1]
        out_ref[...] = jnp.where(live, total, 0.0).astype(jnp.bfloat16)

    row_spec = pl.BlockSpec((block_len, columns), lambda b, s: (b, 0))
    return pl.pallas_call(
        kernel,
        grid_spec=pltpu.PrefetchScalarGridSpec(
            num_scalar_prefetch=1,
            grid=(row_total // block_len,),
            in_specs=[pl.BlockSpec((block_len, rank), lambda b, s: (b, 0))]
            + [pl.BlockSpec(part.shape, lambda b, s: (0, 0)) for part in late]
            + [pl.BlockSpec((1, rank, columns), lambda b, s: (s[base + 5 * b], 0, 0)), row_spec, row_spec],
            out_specs=row_spec,
            scratch_shapes=[pltpu.VMEM((sum(part.shape[0] for part in late), rank), jnp.bfloat16)],
        ),
        out_shape=jax.ShapeDtypeStruct((row_total, columns), jnp.bfloat16),
        input_output_aliases={3 + n_late: 0},
        compiler_params=pltpu.CompilerParams(dimension_semantics=("arbitrary",), vmem_limit_bytes=16 * 1024 * 1024),
        cost_estimate=pl.CostEstimate(
            flops=2 * row_total * columns * 256, bytes_accessed=6 * row_total * columns, transcendentals=0),
    )(numbers, early, *late, lowrank_up, prod, act)


def on_ring(tokens, gate_matrix, up_matrix, lowrank_down, lowrank_up, tenant, adapter_storage_slot, live_count):
    block_count = tenant.shape[0]
    rows_here, width = tokens.shape
    chips = block_count
    block_len = 2 * rows_here
    row_total = block_count * block_len
    columns = gate_matrix.shape[1]
    me = lax.axis_index("tensor")
    core = lax.rem(me, 2)
    chip = me // 2

    def place_of(number):
        return jnp.where(lax.rem(number, 2) == 0, number // 2, chips - 1 - number // 2)

    def number_at(place):
        at = lax.rem(place + chips, chips)
        return jnp.where(at < chips // 2, 2 * at, 2 * (chips - 1 - at) + 1)

    order = jnp.array([0, -1, 1, -2, 2, -3, 3, -4], jnp.int32)
    numbers = number_at(place_of(chip) + order)
    slots = adapter_storage_slot[tenant]
    here = (slots == me).astype(jnp.int32)
    fields = jnp.stack([numbers, live_count[numbers], here[numbers]], axis=1).astype(jnp.int32)
    every = jnp.arange(block_count, dtype=jnp.int32)
    entry_of = [(number_at(place_of(every) + away) ^ chip) * 3 + kind for kind, away in enumerate((3, -3, 4))]
    last_fields = jnp.stack([slots, live_count] + entry_of, axis=1).astype(jnp.int32).reshape(-1)

    meta = jnp.concatenate([core[None].astype(jnp.int32), fields.reshape(-1), last_fields])
    last_at = 1 + fields.size

    right, left = ring_pairs(chips, 1), ring_pairs(chips, -1)

    def send(value, pairs):
        return lax.ppermute(value, "tensor", pairs)

    def flip(value, bits):
        return lax.ppermute(value, "tensor", [(d, d ^ bits) for d in range(2 * chips)])

    down = lowrank_down[0]
    weights = (gate_matrix, up_matrix)
    n_tiles = columns // TILE
    all_tiles = list(range(n_tiles))
    from_left, from_right = tokens, tokens
    blocks = [[(tokens, False, 0), (flip(tokens, 1), True, 0)]]
    state = (row_total, row_total)
    kept = None
    owned = []
    first = 0
    for step in range(3):
        from_left = send(from_left, right)
        from_right = send(from_right, left)
        out = pass_call(meta, first, blocks, down, *weights, kept, state, all_tiles, block_len, True)
        state = out[:2]
        kept = out[2:4]
        owned.append(out[-1])
        first += len(blocks)
        blocks = [[(v, False, 0), (flip(v, 1), True, 0)] for v in (from_left, from_right)]
    cut = rows_here // 2
    last_low = send(from_left[:cut], right)
    last_high = send(from_right[cut:], left)
    early = place_call(meta, owned, row_total, block_len)
    for bits in (1, 2, 4, 8):
        early = early + flip(early, bits)
    *state, kept_gate, kept_up, part = pass_call(
        meta, first, blocks, down, *weights, kept, state, all_tiles, block_len, True)
    kept = (kept_gate, kept_up)
    first += 2
    pieces = [
        (last_low, False, 0), (flip(last_low, 1), True, 0),
        (last_high, False, cut), (flip(last_high, 1), True, cut),
    ]
    mine = late_call(meta, first, pieces, down, part, block_len)
    on_chip = mine + flip(mine, 1)
    across = flip(mine, 2) + flip(mine, 3)
    both = jnp.concatenate([on_chip, across], axis=0)
    late = [both] + [flip(both, 4 * k) for k in range(1, chips // 2)]
    for tiles in (all_tiles[KEPT:], all_tiles[:KEPT]):
        out = pass_call(meta, first, [pieces], down, *weights, kept, state, tiles, block_len, False)
        state, kept = out[:2], out[2:]
    return finish_call(meta, last_at, early, late, lowrank_up, *state, block_len)


def on_device(
    tokens,
    gate_matrix,
    up_matrix,
    lowrank_down,
    lowrank_up,
    tenant,
    adapter_storage_slot,
    live_count,
):
    my_index = lax.axis_index("tensor")
    gathered = lax.all_gather(tokens, "tensor", axis=0, tiled=True)
    row_total = gathered.shape[0]
    width = gathered.shape[1]
    block_count = tenant.shape[0]
    block_len = row_total // block_count
    hidden_columns = gate_matrix.shape[1]
    gate_out = jnp.dot(gathered, gate_matrix, preferred_element_type=jnp.float32)
    up_output = jnp.dot(gathered, up_matrix, preferred_element_type=jnp.float32)
    slot_numbers = adapter_storage_slot[tenant]
    rows_block = gathered.reshape(block_count, block_len, width)
    per_replica = lowrank_down.shape[0]
    rank_width = lowrank_down.shape[1]
    first_slot = my_index * per_replica
    pieces = []
    for block in range(block_count):
        slot_here = slot_numbers[block]
        mine = jnp.logical_and(slot_here >= first_slot, slot_here < first_slot + per_replica)
        resident_slot = jnp.clip(slot_here - first_slot, 0, per_replica - 1)
        down_matrix = lax.dynamic_index_in_dim(lowrank_down, resident_slot, 0, keepdims=False)
        block_rows = rows_block[block]

        def product_fn(rows_in=block_rows, map_in=down_matrix):
            return lax.dot_general(
                rows_in, map_in, (((1,), (1,)), ((), ())), preferred_element_type=jnp.float32
            )

        def empty_fn():
            return jnp.zeros((block_len, rank_width), jnp.float32)

        pieces.append(lax.cond(mine, product_fn, empty_fn))
    partial_value = jnp.stack(pieces, axis=0)
    reduced_output = lax.psum(partial_value, "tensor").astype(jnp.bfloat16)
    every_slot = jnp.arange(lowrank_up.shape[0], dtype=jnp.int32)
    slot_indicator = (slot_numbers[:, None] == every_slot[None, :]).astype(jnp.bfloat16)
    adapter_up = jnp.einsum(
        "oe,exz->oxz", slot_indicator, lowrank_up, preferred_element_type=jnp.float32
    ).astype(jnp.bfloat16)
    lowrank_term = jnp.einsum(
        "who,wok->whk", reduced_output, adapter_up, preferred_element_type=jnp.float32
    )
    up_output = up_output + lowrank_scale * lowrank_term.reshape(row_total, hidden_columns)
    positions = jnp.arange(block_len, dtype=jnp.int32)
    live_rows = (positions[None, :] < live_count[:, None]).reshape(row_total, 1)
    hidden = jnp.where(live_rows, jax.nn.silu(gate_out) * up_output, 0.0)
    return hidden.astype(jnp.bfloat16)


def solution(mesh):
    placed = (
        P(("groups", "tensor"), None),
        P(None, "tensor"),
        P(None, "tensor"),
        P("tensor", None, None),
        P(None, None, "tensor"),
        P("groups"),
        P(),
        P("groups"),
    )
    run = on_ring if mesh.shape["tensor"] == 16 else on_device
    return jax.shard_map(
        run, mesh=mesh, in_specs=placed, out_specs=P("groups", "tensor"), check_vma=False
    )
```

```python
import jax
import jax.numpy as jnp
from jax import lax
from jax.experimental import pallas as pl
from jax.experimental.pallas import tpu as pltpu
from jax.sharding import PartitionSpec as P

lowrank_scale = 2.0
TILE = 256
KEPT = 4
PIECE = 512
MIDDLE = 0.0
VMEM_LIMIT = 23 * 1024 * 1024


def chip_at(place, chips):
    half = chips // 2
    if place < half:
        return 2 * place
    return 2 * (chips - 1 - place) + 1


def ring_pairs(chips, step):
    pairs = []
    for place in range(chips):
        for core in range(2):
            pairs.append((2 * chip_at(place, chips) + core, 2 * chip_at((place + step) % chips, chips) + core))
    return pairs


def pass_call(meta, first, blocks, down, gate_matrix, up_matrix, kept, earlier, tiles, block_len, want_reduced, threaded=(), share=0.0):
    width, columns = gate_matrix.shape
    rank = down.shape[0]
    fresh = kept is None
    row_total = earlier[0] if fresh else earlier[0].shape[0]
    count = len(blocks)
    rows = count * block_len
    half = block_len // 2
    n_kept = len([t for t in tiles if t < KEPT])
    n_streamed = len(tiles) - n_kept
    first_streamed = KEPT
    flat = []
    places = []
    for number, pieces in enumerate(blocks):
        for piece, sibling, offset in pieces:
            places.append((number * block_len, sibling, offset, piece.shape[0]))
            flat.append(piece)
    n_pieces = len(flat)

    def kernel(*refs):
        meta_ref = refs[0]
        piece_refs = refs[1:1 + n_pieces]
        rest = refs[1 + n_pieces:]
        if want_reduced:
            down_ref = rest[0]
            rest = rest[1:]
        gate_ref, up_ref = rest[:2]
        rest = rest[2:]
        if fresh:
            prod_ref, act_ref, kept_gate, kept_up = rest[:4]
            rest = rest[4:]
        else:
            rest = rest[4 + len(threaded):]
            prod_ref, act_ref, kept_gate, kept_up = rest[:4]
            rest = rest[4 + len(threaded):]
        if want_reduced:
            reduced_ref = rest[0]
            rest = rest[1:]
        held, gate_in, up_in, prod_tile, act_tile, in_sem, kept_sem, stream_sem, out_sem = rest

        def kept_copies(t):
            col = pl.multiple_of(t * TILE, TILE)
            return [
                pltpu.make_async_copy(gate_ref.at[:, pl.ds(col, TILE)], kept_gate.at[t], kept_sem.at[0, t]),
                pltpu.make_async_copy(up_ref.at[:, pl.ds(col, TILE)], kept_up.at[t], kept_sem.at[1, t]),
            ]

        def stream_copies(s):
            col = pl.multiple_of((first_streamed + s) * TILE, TILE)
            slot = lax.rem(s, 2)
            return [
                pltpu.make_async_copy(gate_ref.at[:, pl.ds(col, TILE)], gate_in.at[slot], stream_sem.at[0, slot]),
                pltpu.make_async_copy(up_ref.at[:, pl.ds(col, TILE)], up_in.at[slot], stream_sem.at[1, slot]),
            ]

        def start(copies):
            for copy in copies:
                copy.start()

        def wait(copies):
            for copy in copies:
                copy.wait()

        core = meta_ref[0]
        arrivals = []
        for k in range(n_pieces):
            base, sibling, offset, length = places[k]
            side = (1 - core) if sibling else core
            row = pl.multiple_of(base + side * half + offset, 32)
            arrivals.append(pltpu.make_async_copy(piece_refs[k], held.at[pl.ds(row, length)], in_sem.at[k]))
        start(arrivals)
        if fresh:
            for t in range(n_kept):
                start(kept_copies(t))
        for s in range(min(2, n_streamed)):
            start(stream_copies(s))
        wait(arrivals)
        if want_reduced:
            found = lax.dot_general(held[...], down_ref[...], (((1,), (1,)), ((), ())), preferred_element_type=jnp.float32)
            for b in range(count):
                at = slice(b * block_len, (b + 1) * block_len)
                reduced_ref[at, :] = jnp.where(meta_ref[1 + 3 * (first + b) + 2] == 1, found[at], 0.0).astype(jnp.bfloat16)

        def out_copies(done, tile_at):
            slot = lax.rem(done, 2)
            col = pl.multiple_of(tile_at * TILE, TILE)
            made = []
            for b in range(count):
                block_row = pl.multiple_of(meta_ref[1 + 3 * (first + b)] * block_len, block_len)
                for n, (tile, out) in enumerate(((prod_tile, prod_ref), (act_tile, act_ref))):
                    made.append(pltpu.make_async_copy(
                        tile.at[slot, pl.ds(b * block_len, block_len)],
                        out.at[pl.ds(block_row, block_len), pl.ds(col, TILE)],
                        out_sem.at[slot, 2 * b + n]))
            return made

        def compute(done, tile_at, gate_tiles, up_tiles, which):
            @pl.when(done >= 2)
            def _():
                wait(out_copies(done - 2, tile_at))

            slot = lax.rem(done, 2)
            gate_out = jnp.zeros((rows, TILE), jnp.float32)
            up_out = gate_out
            for k in range(0, width, PIECE):
                rows_in = held[:, k:k + PIECE]
                gate_out += jnp.dot(rows_in, gate_tiles[which, k:k + PIECE, :], preferred_element_type=jnp.float32)
                up_out += jnp.dot(rows_in, up_tiles[which, k:k + PIECE, :], preferred_element_type=jnp.float32)
            for b in range(count):
                at = slice(b * block_len, (b + 1) * block_len)
                gate_part = gate_out[at]
                act = gate_part / (1.0 + jnp.exp(-gate_part))
                live = lax.broadcasted_iota(jnp.int32, act.shape, 0) < meta_ref[1 + 3 * (first + b) + 1]
                act_tile[slot, at, :] = jnp.where(live, act, 0.0).astype(jnp.bfloat16)
                prod_tile[slot, at, :] = jnp.where(live, act * up_out[at], 0.0).astype(jnp.bfloat16)
            start(out_copies(done, tile_at))

        if n_kept:
            def on_kept(t, carry):
                if fresh:
                    wait(kept_copies(t))
                compute(t, t, kept_gate, kept_up, t)
                return carry

            lax.fori_loop(0, n_kept, on_kept, 0)
        if n_streamed:
            def on_streamed(s, carry):
                wait(stream_copies(s))
                slot = lax.rem(s, 2)
                compute(n_kept + s, first_streamed + s, gate_in, up_in, slot)

                @pl.when(s + 2 < n_streamed)
                def _():
                    start(stream_copies(s + 2))
                return carry

            lax.fori_loop(0, n_streamed, on_streamed, 0)
        total = n_kept + n_streamed
        for done in range(max(0, total - 2), total):
            wait(out_copies(done, 0))

    any_spec = pl.BlockSpec(memory_space=pl.ANY)
    vmem_spec = pl.BlockSpec(memory_space=pltpu.VMEM)
    in_specs = [any_spec] * n_pieces
    operands = [meta] + flat
    if want_reduced:
        in_specs.append(vmem_spec)
        operands.append(down)
    in_specs += [any_spec, any_spec]
    operands += [gate_matrix, up_matrix]
    result = jax.ShapeDtypeStruct((row_total, columns), jnp.bfloat16)
    out_specs = [any_spec, any_spec, vmem_spec, vmem_spec]
    out_shape = [result, result] + [pltpu.VMEM((KEPT, width, TILE), jnp.bfloat16)] * 2
    aliases = {}
    if not fresh:
        in_specs += [any_spec, any_spec, vmem_spec, vmem_spec]
        in_specs += [any_spec] * len(threaded)
        aliases = {len(operands) + k: k for k in range(4 + len(threaded))}
        operands += list(earlier) + list(kept) + list(threaded)
        out_specs += [any_spec] * len(threaded)
        out_shape += [jax.ShapeDtypeStruct(v.shape, v.dtype) for v in threaded]
    if want_reduced:
        out_specs.append(vmem_spec)
        out_shape.append(jax.ShapeDtypeStruct((rows, rank), jnp.bfloat16))
    buffers = min(2, n_streamed) or 1
    stream_shape = (buffers, width, TILE) if n_streamed else (1, 16, 128)
    return pl.pallas_call(
        kernel,
        grid_spec=pltpu.PrefetchScalarGridSpec(
            num_scalar_prefetch=1,
            grid=(1,),
            in_specs=in_specs,
            out_specs=out_specs,
            scratch_shapes=[
                pltpu.VMEM((rows, width), jnp.bfloat16),
                pltpu.VMEM(stream_shape, jnp.bfloat16),
                pltpu.VMEM(stream_shape, jnp.bfloat16),
                pltpu.VMEM((2, rows, TILE), jnp.bfloat16),
                pltpu.VMEM((2, rows, TILE), jnp.bfloat16),
                pltpu.SemaphoreType.DMA((n_pieces,)),
                pltpu.SemaphoreType.DMA((2, KEPT)),
                pltpu.SemaphoreType.DMA((2, 2)),
                pltpu.SemaphoreType.DMA((2, 2 * count)),
            ],
        ),
        out_shape=out_shape,
        input_output_aliases=aliases,
        compiler_params=pltpu.CompilerParams(dimension_semantics=("arbitrary",), vmem_limit_bytes=VMEM_LIMIT),
        cost_estimate=pl.CostEstimate(
            flops=int(share * 4 * rows * width * TILE * len(tiles)), bytes_accessed=1024 + int(share * 4 * width * TILE * len(tiles)), transcendentals=0),
    )(*operands)


def after_call(values, other):
    any_spec = pl.BlockSpec(memory_space=pl.ANY)

    def kernel(*refs):
        pass

    return pl.pallas_call(
        kernel,
        in_specs=[any_spec] * (len(values) + 1),
        out_specs=[any_spec] * len(values),
        out_shape=[jax.ShapeDtypeStruct(v.shape, v.dtype) for v in values],
        input_output_aliases={k: k for k in range(len(values))},
        compiler_params=pltpu.CompilerParams(vmem_limit_bytes=1024 * 1024),
        cost_estimate=pl.CostEstimate(flops=0, bytes_accessed=0, transcendentals=0),
    )(*values, other)


def place_call(meta, owned, row_total, block_len):
    rank = owned[0].shape[1]

    def kernel(*refs):
        meta_ref, table_ref = refs[0], refs[-1]
        table_ref[...] = jnp.zeros_like(table_ref)
        number = 0
        for ref in refs[1:-1]:
            for b in range(ref.shape[0] // block_len):
                row = pl.multiple_of(meta_ref[1 + 3 * number] * block_len, block_len)
                table_ref[pl.ds(row, block_len), :] = ref[b * block_len:(b + 1) * block_len, :]
                number += 1

    whole = pl.BlockSpec(memory_space=pltpu.VMEM)
    return pl.pallas_call(
        kernel,
        in_specs=[pl.BlockSpec(memory_space=pltpu.SMEM)] + [whole] * len(owned),
        out_specs=whole,
        out_shape=jax.ShapeDtypeStruct((row_total, rank), jnp.bfloat16),
        compiler_params=pltpu.CompilerParams(vmem_limit_bytes=4 * 1024 * 1024),
        cost_estimate=pl.CostEstimate(flops=0, bytes_accessed=1024 * 1024, transcendentals=0),
    )(meta, *owned)


def late_call(meta, first, pieces, down, owned, block_len):
    rank, width = down.shape
    half = block_len // 2
    n_pieces = len(pieces)

    def kernel(*refs):
        meta_ref = refs[0]
        piece_refs = refs[1:1 + n_pieces]
        down_ref, owned_ref, late_ref, held, in_sem = refs[1 + n_pieces:]
        core = meta_ref[0]
        copies = []
        for k, (piece, sibling, offset) in enumerate(pieces):
            side = (1 - core) if sibling else core
            row = pl.multiple_of(side * half + offset, 32)
            copies.append(pltpu.make_async_copy(piece_refs[k], held.at[pl.ds(row, piece.shape[0])], in_sem.at[k]))
        for copy in copies:
            copy.start()
        late_ref[:2 * block_len, :] = owned_ref[...]
        for copy in copies:
            copy.wait()
        found = lax.dot_general(held[...], down_ref[...], (((1,), (1,)), ((), ())), preferred_element_type=jnp.float32)
        late_ref[2 * block_len:, :] = jnp.where(meta_ref[1 + 3 * first + 2] == 1, found, 0.0).astype(jnp.bfloat16)

    whole = pl.BlockSpec(memory_space=pltpu.VMEM)
    return pl.pallas_call(
        kernel,
        in_specs=[pl.BlockSpec(memory_space=pltpu.SMEM)] + [pl.BlockSpec(memory_space=pl.ANY)] * n_pieces + [whole] * 2,
        out_specs=whole,
        out_shape=jax.ShapeDtypeStruct((3 * block_len, rank), jnp.bfloat16),
        scratch_shapes=[pltpu.VMEM((block_len, width), jnp.bfloat16), pltpu.SemaphoreType.DMA((n_pieces,))],
        compiler_params=pltpu.CompilerParams(vmem_limit_bytes=12 * 1024 * 1024),
        cost_estimate=pl.CostEstimate(flops=2 * block_len * width * 256, bytes_accessed=4 * 1024 * 1024, transcendentals=0),
    )(meta, *[piece for piece, _, _ in pieces], down, owned)


def finish_call(numbers, base, early, late, lowrank_up, prod, act, block_len):
    row_total, columns = prod.shape
    rank = early.shape[1]
    n_late = len(late)

    def kernel(*refs):
        numbers_ref, early_ref = refs[:2]
        late_refs = refs[2:2 + n_late]
        map_ref, prod_ref, act_ref, out_ref, entries = refs[2 + n_late:]
        b = pl.program_id(0)

        @pl.when(b == 0)
        def _():
            at = 0
            for ref in late_refs:
                entries[at:at + ref.shape[0], :] = ref[...]
                at += ref.shape[0]

        reduced = early_ref[...]
        for kind in range(3):
            row = pl.multiple_of(numbers_ref[base + 5 * b + 2 + kind] * block_len, block_len)
            reduced = reduced + entries[pl.ds(row, block_len), :]
        term = jnp.dot(reduced, map_ref[0], preferred_element_type=jnp.float32)
        total = prod_ref[...].astype(jnp.float32) + act_ref[...].astype(jnp.float32) * (lowrank_scale * term)
        live = lax.broadcasted_iota(jnp.int32, total.shape, 0) < numbers_ref[base + 5 * b + 1]
        out_ref[...] = jnp.where(live, total, 0.0).astype(jnp.bfloat16)

    row_spec = pl.BlockSpec((block_len, columns), lambda b, s: (b, 0))
    return pl.pallas_call(
        kernel,
        grid_spec=pltpu.PrefetchScalarGridSpec(
            num_scalar_prefetch=1,
            grid=(row_total // block_len,),
            in_specs=[pl.BlockSpec((block_len, rank), lambda b, s: (b, 0))]
            + [pl.BlockSpec(part.shape, lambda b, s: (0, 0)) for part in late]
            + [pl.BlockSpec((1, rank, columns), lambda b, s: (s[base + 5 * b], 0, 0)), row_spec, row_spec],
            out_specs=row_spec,
            scratch_shapes=[pltpu.VMEM((sum(part.shape[0] for part in late), rank), jnp.bfloat16)],
        ),
        out_shape=jax.ShapeDtypeStruct((row_total, columns), jnp.bfloat16),
        input_output_aliases={3 + n_late: 0},
        compiler_params=pltpu.CompilerParams(dimension_semantics=("arbitrary",), vmem_limit_bytes=16 * 1024 * 1024),
        cost_estimate=pl.CostEstimate(
            flops=2 * row_total * columns * 256, bytes_accessed=6 * row_total * columns, transcendentals=0),
    )(numbers, early, *late, lowrank_up, prod, act)


def on_ring(tokens, gate_matrix, up_matrix, lowrank_down, lowrank_up, tenant, adapter_storage_slot, live_count):
    block_count = tenant.shape[0]
    rows_here, width = tokens.shape
    chips = block_count
    block_len = 2 * rows_here
    row_total = block_count * block_len
    columns = gate_matrix.shape[1]
    me = lax.axis_index("tensor")
    core = lax.rem(me, 2)
    chip = me // 2

    def place_of(number):
        return jnp.where(lax.rem(number, 2) == 0, number // 2, chips - 1 - number // 2)

    def number_at(place):
        at = lax.rem(place + chips, chips)
        return jnp.where(at < chips // 2, 2 * at, 2 * (chips - 1 - at) + 1)

    order = jnp.array([0, -1, 1, -2, 2, -3, 3, -4], jnp.int32)
    numbers = number_at(place_of(chip) + order)
    slots = adapter_storage_slot[tenant]
    here = (slots == me).astype(jnp.int32)
    fields = jnp.stack([numbers, live_count[numbers], here[numbers]], axis=1).astype(jnp.int32)
    every = jnp.arange(block_count, dtype=jnp.int32)
    entry_of = [(number_at(place_of(every) + away) ^ chip) * 3 + kind for kind, away in enumerate((3, -3, 4))]
    last_fields = jnp.stack([slots, live_count] + entry_of, axis=1).astype(jnp.int32).reshape(-1)

    meta = jnp.concatenate([core[None].astype(jnp.int32), fields.reshape(-1), last_fields])
    last_at = 1 + fields.size

    right, left = ring_pairs(chips, 1), ring_pairs(chips, -1)

    def send(value, pairs):
        return lax.ppermute(value, "tensor", pairs)

    def flip(value, bits):
        return lax.ppermute(value, "tensor", [(d, d ^ bits) for d in range(2 * chips)])

    down = lowrank_down[0]
    weights = (gate_matrix, up_matrix)
    n_tiles = columns // TILE
    all_tiles = list(range(n_tiles))
    from_left, from_right = tokens, tokens
    blocks = [[(tokens, False, 0), (flip(tokens, 1), True, 0)]]
    state = (row_total, row_total)
    kept = None
    owned = []
    first = 0
    for step in range(3):
        from_left = send(from_left, right)
        from_right = send(from_right, left)
        out = pass_call(meta, first, blocks, down, *weights, kept, state, all_tiles, block_len, True)
        state = out[:2]
        kept = out[2:4]
        owned.append(out[-1])
        first += len(blocks)
        from_left, from_right = after_call((from_left, from_right), out[-1])
        blocks = [[(v, False, 0), (flip(v, 1), True, 0)] for v in (from_left, from_right)]
    cut = rows_here // 2
    last_low = send(from_left[:cut], right)
    last_high = send(from_right[cut:], left)
    early = place_call(meta, owned, row_total, block_len)
    early = early + flip(early, 1)
    met = flip(early, 2)
    *state, kept_gate, kept_up, early, part = pass_call(
        meta, first, blocks, down, *weights, kept, state, all_tiles[:KEPT], block_len, True, (early,))
    early = early + met
    met = flip(early, 4)
    *state, kept_gate, kept_up, early, part = pass_call(
        meta, first, blocks, down, *weights, (kept_gate, kept_up), state, all_tiles[KEPT:], block_len, False, (early, part), MIDDLE)
    early = early + met
    met = flip(early, 8)
    first += 2
    last_low, last_high = after_call((last_low, last_high), part)
    pieces = [
        (last_low, False, 0), (flip(last_low, 1), True, 0),
        (last_high, False, cut), (flip(last_high, 1), True, cut),
    ]
    mine = late_call(meta, first, pieces, down, part, block_len)
    near = [flip(mine, bits) for bits in (1, 2, 3)]
    *state, kept_gate, kept_up, early, mine = pass_call(
        meta, first, [pieces], down, *weights, (kept_gate, kept_up), state, all_tiles[:KEPT], block_len, False, (early, mine), 1.0)
    early = early + met
    both = jnp.concatenate([mine + near[0], near[1] + near[2]], axis=0)
    far = [flip(both, 4 * k) for k in range(1, chips // 2)]
    *state, kept_gate, kept_up, both = pass_call(
        meta, first, [pieces], down, *weights, (kept_gate, kept_up), state, all_tiles[KEPT:], block_len, False, (both,), 1.0)
    return finish_call(meta, last_at, early, [both] + far, lowrank_up, *state, block_len)


def on_device(
    tokens,
    gate_matrix,
    up_matrix,
    lowrank_down,
    lowrank_up,
    tenant,
    adapter_storage_slot,
    live_count,
):
    my_index = lax.axis_index("tensor")
    gathered = lax.all_gather(tokens, "tensor", axis=0, tiled=True)
    row_total = gathered.shape[0]
    width = gathered.shape[1]
    block_count = tenant.shape[0]
    block_len = row_total // block_count
    hidden_columns = gate_matrix.shape[1]
    gate_out = jnp.dot(gathered, gate_matrix, preferred_element_type=jnp.float32)
    up_output = jnp.dot(gathered, up_matrix, preferred_element_type=jnp.float32)
    slot_numbers = adapter_storage_slot[tenant]
    rows_block = gathered.reshape(block_count, block_len, width)
    per_replica = lowrank_down.shape[0]
    rank_width = lowrank_down.shape[1]
    first_slot = my_index * per_replica
    pieces = []
    for block in range(block_count):
        slot_here = slot_numbers[block]
        mine = jnp.logical_and(slot_here >= first_slot, slot_here < first_slot + per_replica)
        resident_slot = jnp.clip(slot_here - first_slot, 0, per_replica - 1)
        down_matrix = lax.dynamic_index_in_dim(lowrank_down, resident_slot, 0, keepdims=False)
        block_rows = rows_block[block]

        def product_fn(rows_in=block_rows, map_in=down_matrix):
            return lax.dot_general(
                rows_in, map_in, (((1,), (1,)), ((), ())), preferred_element_type=jnp.float32
            )

        def empty_fn():
            return jnp.zeros((block_len, rank_width), jnp.float32)

        pieces.append(lax.cond(mine, product_fn, empty_fn))
    partial_value = jnp.stack(pieces, axis=0)
    reduced_output = lax.psum(partial_value, "tensor").astype(jnp.bfloat16)
    every_slot = jnp.arange(lowrank_up.shape[0], dtype=jnp.int32)
    slot_indicator = (slot_numbers[:, None] == every_slot[None, :]).astype(jnp.bfloat16)
    adapter_up = jnp.einsum(
        "oe,exz->oxz", slot_indicator, lowrank_up, preferred_element_type=jnp.float32
    ).astype(jnp.bfloat16)
    lowrank_term = jnp.einsum(
        "who,wok->whk", reduced_output, adapter_up, preferred_element_type=jnp.float32
    )
    up_output = up_output + lowrank_scale * lowrank_term.reshape(row_total, hidden_columns)
    positions = jnp.arange(block_len, dtype=jnp.int32)
    live_rows = (positions[None, :] < live_count[:, None]).reshape(row_total, 1)
    hidden = jnp.where(live_rows, jax.nn.silu(gate_out) * up_output, 0.0)
    return hidden.astype(jnp.bfloat16)


def solution(mesh):
    placed = (
        P(("groups", "tensor"), None),
        P(None, "tensor"),
        P(None, "tensor"),
        P("tensor", None, None),
        P(None, None, "tensor"),
        P("groups"),
        P(),
        P("groups"),
    )
    run = on_ring if mesh.shape["tensor"] == 16 else on_device
    return jax.shard_map(
        run, mesh=mesh, in_specs=placed, out_specs=P("groups", "tensor"), check_vma=False
    )
```

```python
import jax
import jax.numpy as jnp
from jax import lax
from jax.experimental import pallas as pl
from jax.experimental.pallas import tpu as pltpu
from jax.sharding import PartitionSpec as P

lowrank_scale = 2.0
TILE = 256
CHUNK = 16
VMEM_LIMIT = 36 * 1024 * 1024


def last_tiles(tiles):
    third = tiles // 3
    return (tiles - 2 * third, third, third)


def chip_at(place, chips):
    half = chips // 2
    if place < half:
        return 2 * place
    return 2 * (chips - 1 - place) + 1


def ring_pairs(chips, step):
    pairs = []
    for place in range(chips):
        for core in range(2):
            pairs.append((2 * chip_at(place, chips) + core, 2 * chip_at((place + step) % chips, chips) + core))
    return pairs


FIELDS = 4


def chunks_of(meta_ref, block):
    return (meta_ref[1 + FIELDS * block + 1] + CHUNK - 1) // CHUNK


def packed_copies(meta_ref, first, places, piece_refs, held, sems, half):
    core = meta_ref[0]
    made = []
    at = 0
    for k, (number, sibling, offset, length) in enumerate(places):
        base = 0
        for before in range(number):
            base = base + chunks_of(meta_ref, first + before)
        live = chunks_of(meta_ref, first + number)
        side = (1 - core) if sibling else core
        for i in range(length // CHUNK):
            chunk = side * (half // CHUNK) + offset // CHUNK + i
            row = pl.multiple_of((base + chunk) * CHUNK, CHUNK)
            copy = pltpu.make_async_copy(
                piece_refs[k].at[pl.ds(i * CHUNK, CHUNK)], held.at[pl.ds(jnp.minimum(row, held.shape[0] - CHUNK), CHUNK)], sems.at[at])
            made.append((chunk < live, copy))
            at += 1
    return made


def flatten(blocks):
    flat, places = [], []
    for number, pieces in enumerate(blocks):
        for piece, sibling, offset in pieces:
            places.append((number, sibling, offset, piece.shape[0]))
            flat.append(piece)
    return flat, places


def pass_call(meta, first, blocks, down, gate_matrix, up_matrix, first_tile, tiles, block_len, want_reduced, share):
    width = gate_matrix.shape[0]
    rank = down.shape[0]
    count = len(blocks)
    rows = count * block_len
    half = block_len // 2
    flat, places = flatten(blocks)
    n_pieces = len(flat)
    n_copies = rows // CHUNK
    sizes = [m for m in range(block_len, rows + 1, block_len // 2)]

    def kernel(*refs):
        meta_ref = refs[0]
        piece_refs = refs[1:1 + n_pieces]
        rest = refs[1 + n_pieces:]
        if want_reduced:
            down_ref = rest[0]
            rest = rest[1:]
        gate_ref, up_ref, prod_ref, act_ref = rest[:4]
        rest = rest[4:]
        if want_reduced:
            reduced_ref, held, in_sem, found_ref = rest
        else:
            held, in_sem = rest
        total = 0
        for b in range(count):
            total = total + chunks_of(meta_ref, first + b)
        used = total * CHUNK

        @pl.when(pl.program_id(0) == 0)
        def _():
            copies = packed_copies(meta_ref, first, places, piece_refs, held, in_sem, half)
            for live, copy in copies:
                pl.when(live)(copy.start)
            for live, copy in copies:
                pl.when(live)(copy.wait)
            if want_reduced:
                found_ref[...] = lax.dot_general(
                    held[...], down_ref[...], (((1,), (1,)), ((), ())), preferred_element_type=jnp.float32)
                base = 0
                for b in range(count):
                    row = pl.multiple_of(base * CHUNK, CHUNK)
                    part = found_ref[pl.ds(row, block_len), :]
                    mine = meta_ref[1 + FIELDS * (first + b) + 2] == 1
                    reduced_ref[b * block_len:(b + 1) * block_len, :] = jnp.where(mine, part, 0.0).astype(jnp.bfloat16)
                    base = base + chunks_of(meta_ref, first + b)

        below = 0
        for size in sizes:
            def run(size=size):
                rows_in = held[:size, :]
                gate_out = jnp.dot(rows_in, gate_ref[...], preferred_element_type=jnp.float32)
                up_out = jnp.dot(rows_in, up_ref[...], preferred_element_type=jnp.float32)
                act = gate_out * (0.5 * jnp.tanh(0.5 * gate_out) + 0.5)
                act_ref[:size, :] = act.astype(jnp.bfloat16)
                prod_ref[:size, :] = (act * up_out).astype(jnp.bfloat16)

            pl.when(jnp.logical_and(used > below, used <= size))(run)
            below = size

    weight_spec = pl.BlockSpec((width, TILE), lambda j, m: (0, first_tile + j))
    any_spec = pl.BlockSpec(memory_space=pl.ANY)
    in_specs = [any_spec] * n_pieces
    operands = [meta] + flat
    if want_reduced:
        in_specs.append(pl.BlockSpec((rank, width), lambda j, m: (0, 0)))
        operands.append(down)
    in_specs += [weight_spec, weight_spec]
    operands += [gate_matrix, up_matrix]
    out_specs = [pl.BlockSpec((rows, TILE), lambda j, m: (0, j))] * 2
    out_shape = [jax.ShapeDtypeStruct((rows, tiles * TILE), jnp.bfloat16)] * 2
    scratch = [pltpu.VMEM((rows, width), jnp.bfloat16), pltpu.SemaphoreType.DMA((n_copies,))]
    if want_reduced:
        out_specs.append(pl.BlockSpec((rows, rank), lambda j, m: (0, 0)))
        out_shape.append(jax.ShapeDtypeStruct((rows, rank), jnp.bfloat16))
        scratch.append(pltpu.VMEM((rows, rank), jnp.float32))
    return pl.pallas_call(
        kernel,
        grid_spec=pltpu.PrefetchScalarGridSpec(
            num_scalar_prefetch=1, grid=(tiles,), in_specs=in_specs, out_specs=out_specs, scratch_shapes=scratch),
        out_shape=out_shape,
        compiler_params=pltpu.CompilerParams(dimension_semantics=("arbitrary",), vmem_limit_bytes=VMEM_LIMIT),
        cost_estimate=pl.CostEstimate(
            flops=int(share * 4 * rows * width * TILE * tiles),
            bytes_accessed=1024 + int(share * 4 * width * TILE * tiles), transcendentals=0),
    )(*operands)


def after_call(values, other):
    any_spec = pl.BlockSpec(memory_space=pl.ANY)

    def kernel(*refs):
        pass

    return pl.pallas_call(
        kernel,
        in_specs=[any_spec] * (len(values) + 1),
        out_specs=[any_spec] * len(values),
        out_shape=[jax.ShapeDtypeStruct(v.shape, v.dtype) for v in values],
        input_output_aliases={k: k for k in range(len(values))},
        compiler_params=pltpu.CompilerParams(vmem_limit_bytes=1024 * 1024),
        cost_estimate=pl.CostEstimate(flops=0, bytes_accessed=0, transcendentals=0),
    )(*values, other)


def reduce_call(meta, first, blocks, down, owned, row_total, block_len):
    rank, width = down.shape
    half = block_len // 2
    count = len(blocks)
    rows = count * block_len
    flat, places = flatten(blocks)
    n_pieces = len(flat)
    n_owned = len(owned)

    def kernel(*refs):
        meta_ref = refs[0]
        piece_refs = refs[1:1 + n_pieces]
        down_ref = refs[1 + n_pieces]
        owned_refs = refs[2 + n_pieces:2 + n_pieces + n_owned]
        out_ref, held, in_sem = refs[2 + n_pieces + n_owned:]
        core = meta_ref[0]
        copies = []
        for k, (number, sibling, offset, length) in enumerate(places):
            side = (1 - core) if sibling else core
            row = pl.multiple_of(number * block_len + side * half + offset, 32)
            copies.append(pltpu.make_async_copy(piece_refs[k], held.at[pl.ds(row, length)], in_sem.at[k]))
        for copy in copies:
            copy.start()

        def put(number, value):
            row = pl.multiple_of(meta_ref[1 + FIELDS * number] * block_len, block_len)
            out_ref[pl.ds(row, block_len), :] = value

        number = 0
        for ref in owned_refs:
            for b in range(ref.shape[0] // block_len):
                put(number, ref[b * block_len:(b + 1) * block_len, :])
                number += 1
        for copy in copies:
            copy.wait()
        found = lax.dot_general(held[...], down_ref[...], (((1,), (1,)), ((), ())), preferred_element_type=jnp.float32)
        for b in range(count):
            at = slice(b * block_len, (b + 1) * block_len)
            value = jnp.where(meta_ref[1 + FIELDS * (first + b) + 2] == 1, found[at], 0.0).astype(jnp.bfloat16)
            if owned:
                put(first + b, value)
            else:
                out_ref[at, :] = value

    whole = pl.BlockSpec(memory_space=pltpu.VMEM)
    return pl.pallas_call(
        kernel,
        in_specs=[pl.BlockSpec(memory_space=pltpu.SMEM)] + [pl.BlockSpec(memory_space=pl.ANY)] * n_pieces + [whole] * (1 + n_owned),
        out_specs=whole,
        out_shape=jax.ShapeDtypeStruct((row_total if owned else rows, rank), jnp.bfloat16),
        scratch_shapes=[pltpu.VMEM((rows, width), jnp.bfloat16), pltpu.SemaphoreType.DMA((n_pieces,))],
        compiler_params=pltpu.CompilerParams(vmem_limit_bytes=16 * 1024 * 1024),
        cost_estimate=pl.CostEstimate(flops=0, bytes_accessed=1024 * 1024, transcendentals=0),
    )(meta, *flat, down, *owned)


def finish_call(meta, table, lowrank_up, passes, row_total, block_len):
    rank, columns = lowrank_up.shape[1:]
    total_blocks = row_total // block_len
    flat = []
    for _, results in passes:
        for _, prod, act in results:
            flat += [prod, act]
    n_flat = len(flat)

    def kernel(*refs):
        meta_ref, table_ref, map_ref = refs[:3]
        result_refs = refs[3:3 + n_flat]
        out_ref = refs[3 + n_flat]
        k = pl.program_id(0)
        row = pl.multiple_of(meta_ref[1 + FIELDS * k] * block_len, block_len)
        reduced = table_ref[pl.ds(row, block_len), :]
        live = meta_ref[1 + FIELDS * k + 1]
        used = 0
        begun = 0
        for count, results in passes:
            mine = result_refs[used:used + 2 * len(results)]
            used += 2 * len(results)

            def run(begun=begun, count=count, results=results, mine=mine):
                base = 0
                for b in range(begun, begun + count - 1):
                    base = base + jnp.where(b < k, chunks_of(meta_ref, b), 0)
                at = pl.ds(pl.multiple_of(base * CHUNK, CHUNK), block_len)
                for n, (column, prod, _) in enumerate(results):
                    for c in range(0, prod.shape[1], TILE):
                        cols = slice(column + c, column + c + TILE)
                        term = jnp.dot(reduced, map_ref[0, :, cols], preferred_element_type=jnp.float32)
                        sum_of = mine[2 * n][at, c:c + TILE].astype(jnp.float32) + mine[2 * n + 1][at, c:c + TILE].astype(jnp.float32) * (
                            lowrank_scale * term)
                        shown = lax.broadcasted_iota(jnp.int32, sum_of.shape, 0) < live
                        out_ref[:, cols] = jnp.where(shown, sum_of, 0.0).astype(jnp.bfloat16)

            pl.when(jnp.logical_and(k >= begun, k < begun + count))(run)
            begun += count

    return pl.pallas_call(
        kernel,
        grid_spec=pltpu.PrefetchScalarGridSpec(
            num_scalar_prefetch=1,
            grid=(total_blocks,),
            in_specs=[
                pl.BlockSpec(memory_space=pltpu.VMEM),
                pl.BlockSpec((1, rank, columns), lambda k, m: (m[1 + FIELDS * k + 3], 0, 0)),
            ] + [pl.BlockSpec(memory_space=pltpu.VMEM)] * n_flat,
            out_specs=pl.BlockSpec((block_len, columns), lambda k, m: (m[1 + FIELDS * k], 0)),
        ),
        out_shape=jax.ShapeDtypeStruct((row_total, columns), jnp.bfloat16),
        compiler_params=pltpu.CompilerParams(dimension_semantics=("arbitrary",), vmem_limit_bytes=16 * 1024 * 1024),
        cost_estimate=pl.CostEstimate(
            flops=2 * row_total * columns * 256, bytes_accessed=6 * row_total * columns, transcendentals=0),
    )(meta, table, lowrank_up, *flat)


def on_ring(tokens, gate_matrix, up_matrix, lowrank_down, lowrank_up, tenant, adapter_storage_slot, live_count):
    block_count = tenant.shape[0]
    rows_here, width = tokens.shape
    chips = block_count
    block_len = 2 * rows_here
    row_total = block_count * block_len
    columns = gate_matrix.shape[1]
    me = lax.axis_index("tensor")
    core = lax.rem(me, 2)
    chip = me // 2
    place = jnp.where(lax.rem(chip, 2) == 0, chip // 2, chips - 1 - chip // 2)
    order = jnp.array([0, -1, 1, -2, 2, -3, 3, -4], jnp.int32)
    at = lax.rem(place + order + chips, chips)
    numbers = jnp.where(at < chips // 2, 2 * at, 2 * (chips - 1 - at) + 1)
    slots = adapter_storage_slot[tenant][numbers]
    here = (slots == me).astype(jnp.int32)
    fields = jnp.stack([numbers, live_count[numbers], here, slots], axis=1).astype(jnp.int32)
    meta = jnp.concatenate([core[None].astype(jnp.int32), fields.reshape(-1)])

    right, left = ring_pairs(chips, 1), ring_pairs(chips, -1)

    def send(value, pairs):
        return lax.ppermute(value, "tensor", pairs)

    def flip(value, bits):
        return lax.ppermute(value, "tensor", [(d, d ^ bits) for d in range(2 * chips)])

    down = lowrank_down[0]
    weights = (gate_matrix, up_matrix)
    n_tiles = columns // TILE
    from_left, from_right = tokens, tokens
    blocks = [[(tokens, False, 0), (flip(tokens, 1), True, 0)]]
    owned = []
    passes = []
    first = 0
    for step in range(3):
        from_left = send(from_left, right)
        from_right = send(from_right, left)
        prod, act, part = pass_call(meta, first, blocks, down, *weights, 0, n_tiles, block_len, True, 0.0)
        passes.append((len(blocks), [(0, prod, act)]))
        owned.append(part)
        first += len(blocks)
        from_left, from_right = after_call((from_left, from_right), part)
        blocks = [[(v, False, 0), (flip(v, 1), True, 0)] for v in (from_left, from_right)]
    cut = rows_here // 2
    last_low = send(from_left[:cut], right)
    last_high = send(from_right[cut:], left)
    part = reduce_call(meta, first, blocks, down, (), row_total, block_len)
    owned.append(part)
    last_low, last_high = after_call((last_low, last_high), part)
    blocks.append([
        (last_low, False, 0), (flip(last_low, 1), True, 0),
        (last_high, False, cut), (flip(last_high, 1), True, cut),
    ])
    table = reduce_call(meta, first + 2, blocks[2:], down, owned, row_total, block_len)
    for bits in (1, 2, 4, 8):
        table = table + flip(table, bits)
    results = []
    start = 0
    for tiles in last_tiles(n_tiles):
        prod, act = pass_call(meta, first, blocks, down, *weights, start, tiles, block_len, False, 1.0)
        results.append((start * TILE, prod, act))
        start += tiles
    passes.append((3, results))
    return finish_call(meta, table, lowrank_up, passes, row_total, block_len)


def on_device(
    tokens,
    gate_matrix,
    up_matrix,
    lowrank_down,
    lowrank_up,
    tenant,
    adapter_storage_slot,
    live_count,
):
    my_index = lax.axis_index("tensor")
    gathered = lax.all_gather(tokens, "tensor", axis=0, tiled=True)
    row_total = gathered.shape[0]
    width = gathered.shape[1]
    block_count = tenant.shape[0]
    block_len = row_total // block_count
    hidden_columns = gate_matrix.shape[1]
    gate_out = jnp.dot(gathered, gate_matrix, preferred_element_type=jnp.float32)
    up_output = jnp.dot(gathered, up_matrix, preferred_element_type=jnp.float32)
    slot_numbers = adapter_storage_slot[tenant]
    rows_block = gathered.reshape(block_count, block_len, width)
    per_replica = lowrank_down.shape[0]
    rank_width = lowrank_down.shape[1]
    first_slot = my_index * per_replica
    pieces = []
    for block in range(block_count):
        slot_here = slot_numbers[block]
        mine = jnp.logical_and(slot_here >= first_slot, slot_here < first_slot + per_replica)
        resident_slot = jnp.clip(slot_here - first_slot, 0, per_replica - 1)
        down_matrix = lax.dynamic_index_in_dim(lowrank_down, resident_slot, 0, keepdims=False)
        block_rows = rows_block[block]

        def product_fn(rows_in=block_rows, map_in=down_matrix):
            return lax.dot_general(
                rows_in, map_in, (((1,), (1,)), ((), ())), preferred_element_type=jnp.float32
            )

        def empty_fn():
            return jnp.zeros((block_len, rank_width), jnp.float32)

        pieces.append(lax.cond(mine, product_fn, empty_fn))
    partial_value = jnp.stack(pieces, axis=0)
    reduced_output = lax.psum(partial_value, "tensor").astype(jnp.bfloat16)
    every_slot = jnp.arange(lowrank_up.shape[0], dtype=jnp.int32)
    slot_indicator = (slot_numbers[:, None] == every_slot[None, :]).astype(jnp.bfloat16)
    adapter_up = jnp.einsum(
        "oe,exz->oxz", slot_indicator, lowrank_up, preferred_element_type=jnp.float32
    ).astype(jnp.bfloat16)
    lowrank_term = jnp.einsum(
        "who,wok->whk", reduced_output, adapter_up, preferred_element_type=jnp.float32
    )
    up_output = up_output + lowrank_scale * lowrank_term.reshape(row_total, hidden_columns)
    positions = jnp.arange(block_len, dtype=jnp.int32)
    live_rows = (positions[None, :] < live_count[:, None]).reshape(row_total, 1)
    hidden = jnp.where(live_rows, jax.nn.silu(gate_out) * up_output, 0.0)
    return hidden.astype(jnp.bfloat16)


def solution(mesh):
    placed = (
        P(("groups", "tensor"), None),
        P(None, "tensor"),
        P(None, "tensor"),
        P("tensor", None, None),
        P(None, None, "tensor"),
        P("groups"),
        P(),
        P("groups"),
    )
    run = on_ring if mesh.shape["tensor"] == 16 else on_device
    return jax.shard_map(
        run, mesh=mesh, in_specs=placed, out_specs=P("groups", "tensor"), check_vma=False
    )
```

```python
import jax
import jax.numpy as jnp
from jax import lax
from jax.experimental import pallas as pl
from jax.experimental.pallas import tpu as pltpu
from jax.sharding import PartitionSpec as P

lowrank_scale = 2.0
TILE = 256
CHUNK = 16
KEPT = 4
KEPT_LIMIT = 16 * 1024 * 1024
VMEM_LIMIT = 36 * 1024 * 1024


def last_tiles(tiles):
    return (tiles - tiles // 2, tiles // 2)


def chip_at(place, chips):
    half = chips // 2
    if place < half:
        return 2 * place
    return 2 * (chips - 1 - place) + 1


def ring_pairs(chips, step):
    pairs = []
    for place in range(chips):
        for core in range(2):
            pairs.append((2 * chip_at(place, chips) + core, 2 * chip_at((place + step) % chips, chips) + core))
    return pairs


FIELDS = 4


def chunks_of(meta_ref, block):
    return (meta_ref[1 + FIELDS * block + 1] + CHUNK - 1) // CHUNK


def packed_copies(meta_ref, first, places, piece_refs, held, sems, half):
    core = meta_ref[0]
    made = []
    at = 0
    for k, (number, sibling, offset, length) in enumerate(places):
        base = 0
        for before in range(number):
            base = base + chunks_of(meta_ref, first + before)
        live = chunks_of(meta_ref, first + number)
        side = (1 - core) if sibling else core
        for i in range(length // CHUNK):
            chunk = side * (half // CHUNK) + offset // CHUNK + i
            row = pl.multiple_of((base + chunk) * CHUNK, CHUNK)
            copy = pltpu.make_async_copy(
                piece_refs[k].at[pl.ds(i * CHUNK, CHUNK)], held.at[pl.ds(jnp.minimum(row, held.shape[0] - CHUNK), CHUNK)], sems.at[at])
            made.append((chunk < live, copy))
            at += 1
    return made


def flatten(blocks):
    flat, places = [], []
    for number, pieces in enumerate(blocks):
        for piece, sibling, offset in pieces:
            places.append((number, sibling, offset, piece.shape[0]))
            flat.append(piece)
    return flat, places


def pass_call(meta, first, blocks, down, gate_matrix, up_matrix, first_tile, tiles, block_len, want_reduced, share, after=()):
    width = gate_matrix.shape[0]
    rank = down.shape[0]
    count = len(blocks)
    rows = count * block_len
    half = block_len // 2
    flat, places = flatten(blocks)
    n_pieces = len(flat)
    n_copies = rows // CHUNK
    sizes = [m for m in range(block_len, rows + 1, block_len // 2)]

    def kernel(*refs):
        meta_ref = refs[0]
        piece_refs = refs[1:1 + n_pieces]
        rest = refs[1 + n_pieces:]
        if want_reduced:
            down_ref = rest[0]
            rest = rest[1:]
        gate_ref, up_ref = rest[:2]
        prod_ref, act_ref = rest[2 + len(after):4 + len(after)]
        rest = rest[4 + len(after):]
        if want_reduced:
            reduced_ref, held, in_sem, found_ref = rest
        else:
            held, in_sem = rest
        total = 0
        for b in range(count):
            total = total + chunks_of(meta_ref, first + b)
        used = total * CHUNK

        @pl.when(pl.program_id(0) == 0)
        def _():
            copies = packed_copies(meta_ref, first, places, piece_refs, held, in_sem, half)
            for live, copy in copies:
                pl.when(live)(copy.start)
            for live, copy in copies:
                pl.when(live)(copy.wait)
            if want_reduced:
                found_ref[...] = lax.dot_general(
                    held[...], down_ref[...], (((1,), (1,)), ((), ())), preferred_element_type=jnp.float32)
                base = 0
                for b in range(count):
                    row = pl.multiple_of(base * CHUNK, CHUNK)
                    part = found_ref[pl.ds(row, block_len), :]
                    mine = meta_ref[1 + FIELDS * (first + b) + 2] == 1
                    reduced_ref[b * block_len:(b + 1) * block_len, :] = jnp.where(mine, part, 0.0).astype(jnp.bfloat16)
                    base = base + chunks_of(meta_ref, first + b)

        below = 0
        for size in sizes:
            def run(size=size):
                rows_in = held[:size, :]
                gate_out = jnp.dot(rows_in, gate_ref[...], preferred_element_type=jnp.float32)
                up_out = jnp.dot(rows_in, up_ref[...], preferred_element_type=jnp.float32)
                act = gate_out * (0.5 * jnp.tanh(0.5 * gate_out) + 0.5)
                act_ref[:size, :] = act.astype(jnp.bfloat16)
                prod_ref[:size, :] = (act * up_out).astype(jnp.bfloat16)

            pl.when(jnp.logical_and(used > below, used <= size))(run)
            below = size

    weight_spec = pl.BlockSpec((width, TILE), lambda j, m: (0, first_tile + j))
    any_spec = pl.BlockSpec(memory_space=pl.ANY)
    in_specs = [any_spec] * n_pieces
    operands = [meta] + flat
    if want_reduced:
        in_specs.append(pl.BlockSpec((rank, width), lambda j, m: (0, 0)))
        operands.append(down)
    in_specs += [weight_spec, weight_spec] + [any_spec] * len(after)
    operands += [gate_matrix, up_matrix] + list(after)
    out_specs = [pl.BlockSpec((rows, TILE), lambda j, m: (0, j))] * 2
    out_shape = [jax.ShapeDtypeStruct((rows, tiles * TILE), jnp.bfloat16)] * 2
    scratch = [pltpu.VMEM((rows, width), jnp.bfloat16), pltpu.SemaphoreType.DMA((n_copies,))]
    if want_reduced:
        out_specs.append(pl.BlockSpec((rows, rank), lambda j, m: (0, 0)))
        out_shape.append(jax.ShapeDtypeStruct((rows, rank), jnp.bfloat16))
        scratch.append(pltpu.VMEM((rows, rank), jnp.float32))
    return pl.pallas_call(
        kernel,
        grid_spec=pltpu.PrefetchScalarGridSpec(
            num_scalar_prefetch=1, grid=(tiles,), in_specs=in_specs, out_specs=out_specs, scratch_shapes=scratch),
        out_shape=out_shape,
        compiler_params=pltpu.CompilerParams(dimension_semantics=("arbitrary",), vmem_limit_bytes=VMEM_LIMIT),
        cost_estimate=pl.CostEstimate(
            flops=int(share * 4 * rows * width * TILE * tiles),
            bytes_accessed=1024 + int(share * 4 * width * TILE * tiles), transcendentals=0),
    )(*operands)


def kept_call(meta, first, blocks, down, gate_matrix, up_matrix, kept, block_len):
    width = gate_matrix.shape[0]
    rank = down.shape[0]
    fill = kept is None
    count = len(blocks)
    rows = count * block_len
    half = block_len // 2
    flat, places = flatten(blocks)
    n_pieces = len(flat)
    n_copies = rows // CHUNK
    sizes = [m for m in range(block_len, rows + 1, block_len // 2)]

    def kernel(*refs):
        meta_ref = refs[0]
        piece_refs = refs[1:1 + n_pieces]
        rest = refs[1 + n_pieces:]
        if fill:
            down_ref, gate_ref, up_ref = rest[:3]
            rest = rest[3:]
        else:
            rest = rest[2 * KEPT:]
        kept_refs = rest[:2 * KEPT]
        prod_ref, act_ref = rest[2 * KEPT:2 * KEPT + 2]
        rest = rest[2 * KEPT + 2:]
        if fill:
            reduced_ref, held, in_sem, found_ref, kept_sem = rest
        else:
            held, in_sem = rest
        copies = packed_copies(meta_ref, first, places, piece_refs, held, in_sem, half)
        for live, copy in copies:
            pl.when(live)(copy.start)
        loads = []
        if fill:
            for t in range(2 * KEPT):
                source = (gate_ref, up_ref)[t % 2].at[:, t // 2 * TILE:(t // 2 + 1) * TILE]
                loads.append(pltpu.make_async_copy(source, kept_refs[t], kept_sem.at[t]))
            for load in loads:
                load.start()
        total = 0
        for b in range(count):
            total = total + chunks_of(meta_ref, first + b)
        used = total * CHUNK
        for live, copy in copies:
            pl.when(live)(copy.wait)
        if fill:
            found_ref[...] = lax.dot_general(
                held[...], down_ref[...], (((1,), (1,)), ((), ())), preferred_element_type=jnp.float32)
            base = 0
            for b in range(count):
                row = pl.multiple_of(base * CHUNK, CHUNK)
                part = found_ref[pl.ds(row, block_len), :]
                mine = meta_ref[1 + FIELDS * (first + b) + 2] == 1
                reduced_ref[b * block_len:(b + 1) * block_len, :] = jnp.where(mine, part, 0.0).astype(jnp.bfloat16)
                base = base + chunks_of(meta_ref, first + b)
        for t in range(KEPT):
            for load in loads[2 * t:2 * t + 2]:
                load.wait()
            cols = slice(t * TILE, (t + 1) * TILE)
            below = 0
            for size in sizes:
                def run(size=size, t=t, cols=cols):
                    rows_in = held[:size, :]
                    gate_out = jnp.dot(rows_in, kept_refs[2 * t][...], preferred_element_type=jnp.float32)
                    up_out = jnp.dot(rows_in, kept_refs[2 * t + 1][...], preferred_element_type=jnp.float32)
                    act = gate_out * (0.5 * jnp.tanh(0.5 * gate_out) + 0.5)
                    act_ref[:size, cols] = act.astype(jnp.bfloat16)
                    prod_ref[:size, cols] = (act * up_out).astype(jnp.bfloat16)

                pl.when(jnp.logical_and(used > below, used <= size))(run)
                below = size

    any_spec = pl.BlockSpec(memory_space=pl.ANY)
    vmem_spec = pl.BlockSpec(memory_space=pltpu.VMEM)
    in_specs = [any_spec] * n_pieces
    operands = [meta] + flat
    aliases = {}
    if fill:
        in_specs += [vmem_spec, any_spec, any_spec]
        operands += [down, gate_matrix, up_matrix]
    else:
        in_specs += [vmem_spec] * (2 * KEPT)
        aliases = {len(operands) + k: k for k in range(2 * KEPT)}
        operands += list(kept)
    result = jax.ShapeDtypeStruct((rows, KEPT * TILE), jnp.bfloat16)
    out_shape = [pltpu.VMEM((width, TILE), jnp.bfloat16)] * (2 * KEPT) + [result, result]
    scratch = [pltpu.VMEM((rows, width), jnp.bfloat16), pltpu.SemaphoreType.DMA((n_copies,))]
    if fill:
        out_shape.append(jax.ShapeDtypeStruct((rows, rank), jnp.bfloat16))
        scratch += [pltpu.VMEM((rows, rank), jnp.float32), pltpu.SemaphoreType.DMA((2 * KEPT,))]
    return pl.pallas_call(
        kernel,
        grid_spec=pltpu.PrefetchScalarGridSpec(
            num_scalar_prefetch=1, grid=(1,), in_specs=in_specs, out_specs=[vmem_spec] * len(out_shape), scratch_shapes=scratch),
        out_shape=out_shape,
        input_output_aliases=aliases,
        compiler_params=pltpu.CompilerParams(dimension_semantics=("arbitrary",), vmem_limit_bytes=KEPT_LIMIT),
        cost_estimate=pl.CostEstimate(
            flops=0 if fill else 4 * rows * width * TILE * KEPT, bytes_accessed=1024 if fill else 4 * width * TILE * KEPT,
            transcendentals=0),
    )(*operands)


def after_call(values, other):
    any_spec = pl.BlockSpec(memory_space=pl.ANY)

    def kernel(*refs):
        pass

    return pl.pallas_call(
        kernel,
        in_specs=[any_spec] * (len(values) + 1),
        out_specs=[any_spec] * len(values),
        out_shape=[jax.ShapeDtypeStruct(v.shape, v.dtype) for v in values],
        input_output_aliases={k: k for k in range(len(values))},
        compiler_params=pltpu.CompilerParams(vmem_limit_bytes=1024 * 1024),
        cost_estimate=pl.CostEstimate(flops=0, bytes_accessed=0, transcendentals=0),
    )(*values, other)


def table_call(meta, number, pieces, down, owned, row_total, block_len):
    rank, width = down.shape
    half = block_len // 2
    flat, places = flatten([pieces])
    n_pieces = len(flat)
    n_owned = len(owned)
    half_rows = row_total // 2

    def kernel(*refs):
        meta_ref = refs[0]
        piece_refs = refs[1:1 + n_pieces]
        down_ref = refs[1 + n_pieces]
        owned_refs = refs[2 + n_pieces:2 + n_pieces + n_owned]
        mine_ref, other_ref, held, in_sem = refs[2 + n_pieces + n_owned:]
        core = meta_ref[0]
        copies = []
        for k, (_, sibling, offset, length) in enumerate(places):
            side = (1 - core) if sibling else core
            row = pl.multiple_of(side * half + offset, 32)
            copies.append(pltpu.make_async_copy(piece_refs[k], held.at[pl.ds(row, length)], in_sem.at[k]))
        for copy in copies:
            copy.start()

        def put(at, value):
            block = meta_ref[1 + FIELDS * at]
            upper = block // (half_rows // block_len)
            row = pl.multiple_of((block - upper * (half_rows // block_len)) * block_len, block_len)

            @pl.when(upper == core)
            def _():
                mine_ref[pl.ds(row, block_len), :] = value

            @pl.when(upper != core)
            def _():
                other_ref[pl.ds(row, block_len), :] = value

        at = 0
        for ref in owned_refs:
            for b in range(ref.shape[0] // block_len):
                put(at, ref[b * block_len:(b + 1) * block_len, :])
                at += 1
        for copy in copies:
            copy.wait()
        found = lax.dot_general(held[...], down_ref[...], (((1,), (1,)), ((), ())), preferred_element_type=jnp.float32)
        put(number, jnp.where(meta_ref[1 + FIELDS * number + 2] == 1, found, 0.0).astype(jnp.bfloat16))

    whole = pl.BlockSpec(memory_space=pltpu.VMEM)
    return pl.pallas_call(
        kernel,
        in_specs=[pl.BlockSpec(memory_space=pltpu.SMEM)] + [pl.BlockSpec(memory_space=pl.ANY)] * n_pieces + [whole] * (1 + n_owned),
        out_specs=[whole] * 2,
        out_shape=[jax.ShapeDtypeStruct((half_rows, rank), jnp.bfloat16)] * 2,
        scratch_shapes=[pltpu.VMEM((block_len, width), jnp.bfloat16), pltpu.SemaphoreType.DMA((n_pieces,))],
        compiler_params=pltpu.CompilerParams(vmem_limit_bytes=8 * 1024 * 1024),
        cost_estimate=pl.CostEstimate(flops=0, bytes_accessed=1024 * 1024, transcendentals=0),
    )(meta, *flat, down, *owned)


def finish_call(meta, mine, other, lowrank_up, results, row_total, block_len):
    rank, columns = lowrank_up.shape[1:]
    total_blocks = row_total // block_len
    flat = []
    for result in results:
        flat += result[3:]
    n_flat = len(flat)
    per_half = total_blocks // 2

    def kernel(*refs):
        meta_ref, mine_ref, other_ref, map_ref = refs[:4]
        result_refs = refs[4:4 + n_flat]
        out_ref = refs[4 + n_flat]
        k = pl.program_id(0)
        block = meta_ref[1 + FIELDS * k]
        upper = block // per_half
        row = pl.multiple_of((block - upper * per_half) * block_len, block_len)
        at_row = pl.ds(row, block_len)
        reduced = jnp.where(upper == meta_ref[0], mine_ref[at_row, :], other_ref[at_row, :])
        live = meta_ref[1 + FIELDS * k + 1]
        for n, (begun, count, column, prod, _) in enumerate(results):
            def run(n=n, begun=begun, count=count, column=column, prod=prod):
                base = 0
                for b in range(begun, begun + count - 1):
                    base = base + jnp.where(b < k, chunks_of(meta_ref, b), 0)
                at = pl.ds(pl.multiple_of(base * CHUNK, CHUNK), block_len)
                for c in range(0, prod.shape[1], TILE):
                    cols = slice(column + c, column + c + TILE)
                    term = jnp.dot(reduced, map_ref[0, :, cols], preferred_element_type=jnp.float32)
                    prods = result_refs[2 * n][at, c:c + TILE].astype(jnp.float32)
                    acts = result_refs[2 * n + 1][at, c:c + TILE].astype(jnp.float32)
                    sum_of = prods + acts * (lowrank_scale * term)
                    shown = lax.broadcasted_iota(jnp.int32, sum_of.shape, 0) < live
                    out_ref[:, cols] = jnp.where(shown, sum_of, 0.0).astype(jnp.bfloat16)

            pl.when(jnp.logical_and(k >= begun, k < begun + count))(run)

    vmem_spec = pl.BlockSpec(memory_space=pltpu.VMEM)
    return pl.pallas_call(
        kernel,
        grid_spec=pltpu.PrefetchScalarGridSpec(
            num_scalar_prefetch=1,
            grid=(total_blocks,),
            in_specs=[vmem_spec, vmem_spec, pl.BlockSpec((1, rank, columns), lambda k, m: (m[1 + FIELDS * k + 3], 0, 0))]
            + [vmem_spec] * n_flat,
            out_specs=pl.BlockSpec((block_len, columns), lambda k, m: (m[1 + FIELDS * k], 0)),
        ),
        out_shape=jax.ShapeDtypeStruct((row_total, columns), jnp.bfloat16),
        compiler_params=pltpu.CompilerParams(dimension_semantics=("arbitrary",), vmem_limit_bytes=16 * 1024 * 1024),
        cost_estimate=pl.CostEstimate(
            flops=2 * row_total * columns * 256, bytes_accessed=6 * row_total * columns, transcendentals=0),
    )(meta, mine, other, lowrank_up, *flat)


def on_ring(tokens, gate_matrix, up_matrix, lowrank_down, lowrank_up, tenant, adapter_storage_slot, live_count):
    block_count = tenant.shape[0]
    rows_here, width = tokens.shape
    chips = block_count
    block_len = 2 * rows_here
    row_total = block_count * block_len
    columns = gate_matrix.shape[1]
    me = lax.axis_index("tensor")
    core = lax.rem(me, 2)
    chip = me // 2
    place = jnp.where(lax.rem(chip, 2) == 0, chip // 2, chips - 1 - chip // 2)
    order = jnp.array([0, -1, 1, -2, 2, -3, 3, -4], jnp.int32)
    at = lax.rem(place + order + chips, chips)
    numbers = jnp.where(at < chips // 2, 2 * at, 2 * (chips - 1 - at) + 1)
    slots = adapter_storage_slot[tenant][numbers]
    here = (slots == me).astype(jnp.int32)
    fields = jnp.stack([numbers, live_count[numbers], here, slots], axis=1).astype(jnp.int32)
    meta = jnp.concatenate([core[None].astype(jnp.int32), fields.reshape(-1)])

    right, left = ring_pairs(chips, 1), ring_pairs(chips, -1)

    def send(value, pairs):
        return lax.ppermute(value, "tensor", pairs)

    def flip(value, bits):
        return lax.ppermute(value, "tensor", [(d, d ^ bits) for d in range(2 * chips)])

    down = lowrank_down[0]
    weights = (gate_matrix, up_matrix)
    n_tiles = columns // TILE
    from_left, from_right = tokens, tokens
    blocks = [[(tokens, False, 0), (flip(tokens, 1), True, 0)]]
    owned = []
    results = []
    first = 0
    for step in range(3):
        from_left = send(from_left, right)
        from_right = send(from_right, left)
        prod, act, part = pass_call(meta, first, blocks, down, *weights, 0, n_tiles, block_len, True, 0.0)
        results.append((first, len(blocks), 0, prod, act))
        owned.append(part)
        first += len(blocks)
        from_left, from_right = after_call((from_left, from_right), part)
        blocks = [[(v, False, 0), (flip(v, 1), True, 0)] for v in (from_left, from_right)]
    cut = rows_here // 2
    last_low = send(from_left[:cut], right)
    last_high = send(from_right[cut:], left)
    *kept, prod, act, part = kept_call(meta, first, blocks, down, *weights, None, block_len)
    results.append((first, 2, 0, prod, act))
    owned.append(part)
    last_low, last_high = after_call((last_low, last_high), part)
    blocks.append([
        (last_low, False, 0), (flip(last_low, 1), True, 0),
        (last_high, False, cut), (flip(last_high, 1), True, cut),
    ])
    mine, other = table_call(meta, first + 2, blocks[2], down, owned, row_total, block_len)
    mine = mine + flip(other, 1)
    mine = mine + flip(mine, 2)
    mine = mine + flip(mine, 4) + flip(mine, 8) + flip(mine, 12)
    other = flip(mine, 1)
    *_, prod, act = kept_call(meta, first + 2, blocks[2:], down, *weights, kept, block_len)
    results.append((first + 2, 1, 0, prod, act))
    start = KEPT
    for tiles in last_tiles(n_tiles - KEPT):
        prod, act = pass_call(meta, first, blocks, down, *weights, start, tiles, block_len, False, 1.0, (results[-1][3],))
        results.append((first, 3, start * TILE, prod, act))
        start += tiles
    return finish_call(meta, mine, other, lowrank_up, results, row_total, block_len)


def on_device(
    tokens,
    gate_matrix,
    up_matrix,
    lowrank_down,
    lowrank_up,
    tenant,
    adapter_storage_slot,
    live_count,
):
    my_index = lax.axis_index("tensor")
    gathered = lax.all_gather(tokens, "tensor", axis=0, tiled=True)
    row_total = gathered.shape[0]
    width = gathered.shape[1]
    block_count = tenant.shape[0]
    block_len = row_total // block_count
    hidden_columns = gate_matrix.shape[1]
    gate_out = jnp.dot(gathered, gate_matrix, preferred_element_type=jnp.float32)
    up_output = jnp.dot(gathered, up_matrix, preferred_element_type=jnp.float32)
    slot_numbers = adapter_storage_slot[tenant]
    rows_block = gathered.reshape(block_count, block_len, width)
    per_replica = lowrank_down.shape[0]
    rank_width = lowrank_down.shape[1]
    first_slot = my_index * per_replica
    pieces = []
    for block in range(block_count):
        slot_here = slot_numbers[block]
        mine = jnp.logical_and(slot_here >= first_slot, slot_here < first_slot + per_replica)
        resident_slot = jnp.clip(slot_here - first_slot, 0, per_replica - 1)
        down_matrix = lax.dynamic_index_in_dim(lowrank_down, resident_slot, 0, keepdims=False)
        block_rows = rows_block[block]

        def product_fn(rows_in=block_rows, map_in=down_matrix):
            return lax.dot_general(
                rows_in, map_in, (((1,), (1,)), ((), ())), preferred_element_type=jnp.float32
            )

        def empty_fn():
            return jnp.zeros((block_len, rank_width), jnp.float32)

        pieces.append(lax.cond(mine, product_fn, empty_fn))
    partial_value = jnp.stack(pieces, axis=0)
    reduced_output = lax.psum(partial_value, "tensor").astype(jnp.bfloat16)
    every_slot = jnp.arange(lowrank_up.shape[0], dtype=jnp.int32)
    slot_indicator = (slot_numbers[:, None] == every_slot[None, :]).astype(jnp.bfloat16)
    adapter_up = jnp.einsum(
        "oe,exz->oxz", slot_indicator, lowrank_up, preferred_element_type=jnp.float32
    ).astype(jnp.bfloat16)
    lowrank_term = jnp.einsum(
        "who,wok->whk", reduced_output, adapter_up, preferred_element_type=jnp.float32
    )
    up_output = up_output + lowrank_scale * lowrank_term.reshape(row_total, hidden_columns)
    positions = jnp.arange(block_len, dtype=jnp.int32)
    live_rows = (positions[None, :] < live_count[:, None]).reshape(row_total, 1)
    hidden = jnp.where(live_rows, jax.nn.silu(gate_out) * up_output, 0.0)
    return hidden.astype(jnp.bfloat16)


def solution(mesh):
    placed = (
        P(("groups", "tensor"), None),
        P(None, "tensor"),
        P(None, "tensor"),
        P("tensor", None, None),
        P(None, None, "tensor"),
        P("groups"),
        P(),
        P("groups"),
    )
    run = on_ring if mesh.shape["tensor"] == 16 else on_device
    return jax.shard_map(
        run, mesh=mesh, in_specs=placed, out_specs=P("groups", "tensor"), check_vma=False
    )
```

```python
import jax
import jax.numpy as jnp
from jax import lax
from jax.experimental import pallas as pl
from jax.experimental.pallas import tpu as pltpu
from jax.sharding import PartitionSpec as P

lowrank_scale = 2.0
TILE = 256
CHUNK = 16
KEPT = 3
FETCHED = 2
VMEM_LIMIT = 36 * 1024 * 1024


def chip_at(place, chips):
    half = chips // 2
    if place < half:
        return 2 * place
    return 2 * (chips - 1 - place) + 1


def ring_pairs(chips, step):
    pairs = []
    for place in range(chips):
        for core in range(2):
            pairs.append((2 * chip_at(place, chips) + core, 2 * chip_at((place + step) % chips, chips) + core))
    return pairs


FIELDS = 4


def chunks_of(meta_ref, block):
    return (meta_ref[1 + FIELDS * block + 1] + CHUNK - 1) // CHUNK


def packed_copies(meta_ref, first, places, piece_refs, held, sems, half):
    core = meta_ref[0]
    made = []
    at = 0
    for k, (number, sibling, offset, length) in enumerate(places):
        base = 0
        for before in range(number):
            base = base + chunks_of(meta_ref, first + before)
        live = chunks_of(meta_ref, first + number)
        side = (1 - core) if sibling else core
        for i in range(length // CHUNK):
            chunk = side * (half // CHUNK) + offset // CHUNK + i
            row = pl.multiple_of((base + chunk) * CHUNK, CHUNK)
            copy = pltpu.make_async_copy(
                piece_refs[k].at[pl.ds(i * CHUNK, CHUNK)], held.at[pl.ds(jnp.minimum(row, held.shape[0] - CHUNK), CHUNK)], sems.at[at])
            made.append((chunk < live, copy))
            at += 1
    return made


def flatten(blocks):
    flat, places = [], []
    for number, pieces in enumerate(blocks):
        for piece, sibling, offset in pieces:
            places.append((number, sibling, offset, piece.shape[0]))
            flat.append(piece)
    return flat, places


def pass_call(meta, first, blocks, down, gate_matrix, up_matrix, first_tile, tiles, block_len, want_reduced, share, after=()):
    width = gate_matrix.shape[0]
    rank = down.shape[0]
    count = len(blocks)
    rows = count * block_len
    half = block_len // 2
    flat, places = flatten(blocks)
    n_pieces = len(flat)
    n_copies = rows // CHUNK
    sizes = [m for m in range(block_len, rows + 1, block_len // 2)]

    def kernel(*refs):
        meta_ref = refs[0]
        piece_refs = refs[1:1 + n_pieces]
        rest = refs[1 + n_pieces:]
        if want_reduced:
            down_ref = rest[0]
            rest = rest[1:]
        gate_ref, up_ref = rest[:2]
        prod_ref, act_ref = rest[2 + len(after):4 + len(after)]
        rest = rest[4 + len(after):]
        if want_reduced:
            reduced_ref, held, in_sem, found_ref = rest
        else:
            held, in_sem = rest
        total = 0
        for b in range(count):
            total = total + chunks_of(meta_ref, first + b)
        used = total * CHUNK

        @pl.when(pl.program_id(0) == 0)
        def _():
            copies = packed_copies(meta_ref, first, places, piece_refs, held, in_sem, half)
            for live, copy in copies:
                pl.when(live)(copy.start)
            for live, copy in copies:
                pl.when(live)(copy.wait)
            if want_reduced:
                found_ref[...] = lax.dot_general(
                    held[...], down_ref[...], (((1,), (1,)), ((), ())), preferred_element_type=jnp.float32)
                base = 0
                for b in range(count):
                    row = pl.multiple_of(base * CHUNK, CHUNK)
                    part = found_ref[pl.ds(row, block_len), :]
                    mine = meta_ref[1 + FIELDS * (first + b) + 2] == 1
                    reduced_ref[b * block_len:(b + 1) * block_len, :] = jnp.where(mine, part, 0.0).astype(jnp.bfloat16)
                    base = base + chunks_of(meta_ref, first + b)

        below = 0
        for size in sizes:
            def run(size=size):
                rows_in = held[:size, :]
                gate_out = jnp.dot(rows_in, gate_ref[...], preferred_element_type=jnp.float32)
                up_out = jnp.dot(rows_in, up_ref[...], preferred_element_type=jnp.float32)
                act = gate_out * (0.5 * jnp.tanh(0.5 * gate_out) + 0.5)
                act_ref[:size, :] = act.astype(jnp.bfloat16)
                prod_ref[:size, :] = (act * up_out).astype(jnp.bfloat16)

            pl.when(jnp.logical_and(used > below, used <= size))(run)
            below = size

    weight_spec = pl.BlockSpec((width, TILE), lambda j, m: (0, first_tile + j))
    any_spec = pl.BlockSpec(memory_space=pl.ANY)
    in_specs = [any_spec] * n_pieces
    operands = [meta] + flat
    if want_reduced:
        in_specs.append(pl.BlockSpec((rank, width), lambda j, m: (0, 0)))
        operands.append(down)
    in_specs += [weight_spec, weight_spec] + [any_spec] * len(after)
    operands += [gate_matrix, up_matrix] + list(after)
    out_specs = [pl.BlockSpec((rows, TILE), lambda j, m: (0, j))] * 2
    out_shape = [jax.ShapeDtypeStruct((rows, tiles * TILE), jnp.bfloat16)] * 2
    scratch = [pltpu.VMEM((rows, width), jnp.bfloat16), pltpu.SemaphoreType.DMA((n_copies,))]
    if want_reduced:
        out_specs.append(pl.BlockSpec((rows, rank), lambda j, m: (0, 0)))
        out_shape.append(jax.ShapeDtypeStruct((rows, rank), jnp.bfloat16))
        scratch.append(pltpu.VMEM((rows, rank), jnp.float32))
    return pl.pallas_call(
        kernel,
        grid_spec=pltpu.PrefetchScalarGridSpec(
            num_scalar_prefetch=1, grid=(tiles,), in_specs=in_specs, out_specs=out_specs, scratch_shapes=scratch),
        out_shape=out_shape,
        compiler_params=pltpu.CompilerParams(dimension_semantics=("arbitrary",), vmem_limit_bytes=VMEM_LIMIT),
        cost_estimate=pl.CostEstimate(
            flops=int(share * 4 * rows * width * TILE * tiles),
            bytes_accessed=1024 + int(share * 4 * width * TILE * tiles), transcendentals=0),
    )(*operands)


def tile_call(meta, first, blocks, down, gate_matrix, up_matrix, given, fetch, compute, block_len, want_reduced, share, keep=True):
    width = gate_matrix.shape[0]
    rank = down.shape[0]
    count = len(blocks)
    rows = count * block_len
    half = block_len // 2
    flat, places = flatten(blocks)
    n_pieces = len(flat)
    n_copies = rows // CHUNK
    sizes = [m for m in range(block_len, rows + 1, block_len // 2)]
    held_tiles = list(given)
    order = held_tiles + list(fetch)
    n_given = 2 * len(held_tiles)
    n_out = 2 * len(order) if keep else n_given

    def kernel(*refs):
        meta_ref = refs[0]
        piece_refs = refs[1:1 + n_pieces]
        rest = refs[1 + n_pieces:]
        if want_reduced:
            down_ref = rest[0]
            rest = rest[1:]
        gate_ref, up_ref = rest[:2]
        rest = rest[2 + n_given:]
        tile_refs = list(rest[:n_out])
        prod_ref, act_ref = rest[n_out:n_out + 2]
        rest = rest[n_out + 2:]
        if not keep:
            tile_refs += rest[-2 * len(fetch):]
            rest = rest[:-2 * len(fetch)]
        if want_reduced:
            reduced_ref, held, in_sem, tile_sem, found_ref = rest
        else:
            held, in_sem, tile_sem = rest
        copies = packed_copies(meta_ref, first, places, piece_refs, held, in_sem, half)
        for live, copy in copies:
            pl.when(live)(copy.start)
        loads = {}
        for n, t in enumerate(fetch):
            at = len(held_tiles) + n
            loads[t] = [
                pltpu.make_async_copy(ref.at[:, t * TILE:(t + 1) * TILE], tile_refs[2 * at + side], tile_sem.at[2 * n + side])
                for side, ref in enumerate((gate_ref, up_ref))
            ]
            for load in loads[t]:
                load.start()
        total = 0
        for b in range(count):
            total = total + chunks_of(meta_ref, first + b)
        used = total * CHUNK
        for live, copy in copies:
            pl.when(live)(copy.wait)
        if want_reduced:
            found_ref[...] = lax.dot_general(
                held[...], down_ref[...], (((1,), (1,)), ((), ())), preferred_element_type=jnp.float32)
            base = 0
            for b in range(count):
                row = pl.multiple_of(base * CHUNK, CHUNK)
                part = found_ref[pl.ds(row, block_len), :]
                mine = meta_ref[1 + FIELDS * (first + b) + 2] == 1
                reduced_ref[b * block_len:(b + 1) * block_len, :] = jnp.where(mine, part, 0.0).astype(jnp.bfloat16)
                base = base + chunks_of(meta_ref, first + b)
        for n, t in enumerate(compute):
            for load in loads.pop(t, []):
                load.wait()
            at = order.index(t)
            cols = slice(n * TILE, (n + 1) * TILE)
            below = 0
            for size in sizes:
                def run(size=size, at=at, cols=cols):
                    rows_in = held[:size, :]
                    gate_out = jnp.dot(rows_in, tile_refs[2 * at][...], preferred_element_type=jnp.float32)
                    up_out = jnp.dot(rows_in, tile_refs[2 * at + 1][...], preferred_element_type=jnp.float32)
                    act = gate_out * (0.5 * jnp.tanh(0.5 * gate_out) + 0.5)
                    act_ref[:size, cols] = act.astype(jnp.bfloat16)
                    prod_ref[:size, cols] = (act * up_out).astype(jnp.bfloat16)

                pl.when(jnp.logical_and(used > below, used <= size))(run)
                below = size
        for t in list(loads):
            for load in loads[t]:
                load.wait()

    any_spec = pl.BlockSpec(memory_space=pl.ANY)
    vmem_spec = pl.BlockSpec(memory_space=pltpu.VMEM)
    in_specs = [any_spec] * n_pieces
    operands = [meta] + flat
    if want_reduced:
        in_specs.append(vmem_spec)
        operands.append(down)
    in_specs += [any_spec, any_spec] + [vmem_spec] * n_given
    operands += [gate_matrix, up_matrix]
    aliases = {len(operands) + k: k for k in range(n_given)}
    for t in held_tiles:
        operands += list(given[t])
    result = jax.ShapeDtypeStruct((rows, len(compute) * TILE), jnp.bfloat16)
    out_shape = [pltpu.VMEM((width, TILE), jnp.bfloat16)] * n_out + [result, result]
    scratch = [
        pltpu.VMEM((rows, width), jnp.bfloat16),
        pltpu.SemaphoreType.DMA((n_copies,)),
        pltpu.SemaphoreType.DMA((max(1, 2 * len(fetch)),)),
    ]
    if want_reduced:
        out_shape.append(jax.ShapeDtypeStruct((rows, rank), jnp.bfloat16))
        scratch.append(pltpu.VMEM((rows, rank), jnp.float32))
    limit = rows * 32 * 1024 + 4 * 1024 * 1024
    if not keep:
        scratch += [pltpu.VMEM((width, TILE), jnp.bfloat16)] * (2 * len(fetch))
        limit += 4 * width * TILE * len(fetch)
    out = pl.pallas_call(
        kernel,
        grid_spec=pltpu.PrefetchScalarGridSpec(
            num_scalar_prefetch=1, grid=(1,), in_specs=in_specs, out_specs=[vmem_spec] * len(out_shape), scratch_shapes=scratch),
        out_shape=out_shape,
        input_output_aliases=aliases,
        compiler_params=pltpu.CompilerParams(dimension_semantics=("arbitrary",), vmem_limit_bytes=limit),
        cost_estimate=pl.CostEstimate(
            flops=int(share * 4 * rows * width * TILE * len(compute)),
            bytes_accessed=1024 + int(share * 4 * width * TILE * len(compute)), transcendentals=0),
    )(*operands)
    tiles = {t: (out[2 * n], out[2 * n + 1]) for n, t in enumerate(order[:n_out // 2])}
    return tiles, out[n_out:]


def after_call(values, other):
    any_spec = pl.BlockSpec(memory_space=pl.ANY)

    def kernel(*refs):
        pass

    return pl.pallas_call(
        kernel,
        in_specs=[any_spec] * (len(values) + 1),
        out_specs=[any_spec] * len(values),
        out_shape=[jax.ShapeDtypeStruct(v.shape, v.dtype) for v in values],
        input_output_aliases={k: k for k in range(len(values))},
        compiler_params=pltpu.CompilerParams(vmem_limit_bytes=1024 * 1024),
        cost_estimate=pl.CostEstimate(flops=0, bytes_accessed=0, transcendentals=0),
    )(*values, other)


def quarter_of(block, row_total, block_len):
    per_quarter = row_total // block_len // 4
    quarter = block // per_quarter
    return quarter, pl.multiple_of((block - quarter * per_quarter) * block_len, block_len)


def table_call(meta, number, pieces, down, owned, row_total, block_len):
    rank, width = down.shape
    half = block_len // 2
    flat, places = flatten([pieces])
    n_pieces = len(flat)
    n_owned = len(owned)

    def kernel(*refs):
        meta_ref = refs[0]
        piece_refs = refs[1:1 + n_pieces]
        down_ref = refs[1 + n_pieces]
        owned_refs = refs[2 + n_pieces:2 + n_pieces + n_owned]
        mine_ref, other_ref, held, in_sem = refs[2 + n_pieces + n_owned:]
        core = meta_ref[0]
        copies = []
        for k, (_, sibling, offset, length) in enumerate(places):
            side = (1 - core) if sibling else core
            row = pl.multiple_of(side * half + offset, 32)
            copies.append(pltpu.make_async_copy(piece_refs[k], held.at[pl.ds(row, length)], in_sem.at[k]))
        for copy in copies:
            copy.start()

        def put(at, value):
            quarter, row = quarter_of(meta_ref[1 + FIELDS * at], row_total, block_len)
            for q in range(4):
                @pl.when(quarter == q)
                def _(q=q):
                    lanes = slice(q % 2 * rank, (q % 2 + 1) * rank)

                    @pl.when(core == q // 2)
                    def _():
                        mine_ref[pl.ds(row, block_len), lanes] = value

                    @pl.when(core != q // 2)
                    def _():
                        other_ref[pl.ds(row, block_len), lanes] = value

        at = 0
        for ref in owned_refs:
            for b in range(ref.shape[0] // block_len):
                put(at, ref[b * block_len:(b + 1) * block_len, :])
                at += 1
        for copy in copies:
            copy.wait()
        found = lax.dot_general(held[...], down_ref[...], (((1,), (1,)), ((), ())), preferred_element_type=jnp.float32)
        put(number, jnp.where(meta_ref[1 + FIELDS * number + 2] == 1, found, 0.0).astype(jnp.bfloat16))

    whole = pl.BlockSpec(memory_space=pltpu.VMEM)
    return pl.pallas_call(
        kernel,
        in_specs=[pl.BlockSpec(memory_space=pltpu.SMEM)] + [pl.BlockSpec(memory_space=pl.ANY)] * n_pieces + [whole] * (1 + n_owned),
        out_specs=[whole] * 2,
        out_shape=[jax.ShapeDtypeStruct((row_total // 4, 2 * rank), jnp.bfloat16)] * 2,
        scratch_shapes=[pltpu.VMEM((block_len, width), jnp.bfloat16), pltpu.SemaphoreType.DMA((n_pieces,))],
        compiler_params=pltpu.CompilerParams(vmem_limit_bytes=8 * 1024 * 1024),
        cost_estimate=pl.CostEstimate(flops=0, bytes_accessed=1024 * 1024, transcendentals=0),
    )(meta, *flat, down, *owned)


def finish_call(meta, mine, other, lowrank_up, results, row_total, block_len):
    rank, columns = lowrank_up.shape[1:]
    total_blocks = row_total // block_len
    flat = []
    for result in results:
        flat += result[3:]
    n_flat = len(flat)

    def kernel(*refs):
        meta_ref, mine_ref, other_ref, map_ref = refs[:4]
        result_refs = refs[4:4 + n_flat]
        out_ref = refs[4 + n_flat]
        k = pl.program_id(0)
        quarter, row = quarter_of(meta_ref[1 + FIELDS * k], row_total, block_len)
        at_row = pl.ds(row, block_len)
        both = jnp.where(quarter // 2 == meta_ref[0], mine_ref[at_row, :], other_ref[at_row, :])
        reduced = jnp.where(lax.rem(quarter, 2) == 0, both[:, :rank], both[:, rank:])
        live = meta_ref[1 + FIELDS * k + 1]
        for n, (begun, count, column, prod, _) in enumerate(results):
            def run(n=n, begun=begun, count=count, column=column, prod=prod):
                base = 0
                for b in range(begun, begun + count - 1):
                    base = base + jnp.where(b < k, chunks_of(meta_ref, b), 0)
                at = pl.ds(pl.multiple_of(base * CHUNK, CHUNK), block_len)
                for c in range(0, prod.shape[1], TILE):
                    cols = slice(column + c, column + c + TILE)
                    term = jnp.dot(reduced, map_ref[0, :, cols], preferred_element_type=jnp.float32)
                    prods = result_refs[2 * n][at, c:c + TILE].astype(jnp.float32)
                    acts = result_refs[2 * n + 1][at, c:c + TILE].astype(jnp.float32)
                    sum_of = prods + acts * (lowrank_scale * term)
                    shown = lax.broadcasted_iota(jnp.int32, sum_of.shape, 0) < live
                    out_ref[:, cols] = jnp.where(shown, sum_of, 0.0).astype(jnp.bfloat16)

            pl.when(jnp.logical_and(k >= begun, k < begun + count))(run)

    vmem_spec = pl.BlockSpec(memory_space=pltpu.VMEM)
    return pl.pallas_call(
        kernel,
        grid_spec=pltpu.PrefetchScalarGridSpec(
            num_scalar_prefetch=1,
            grid=(total_blocks,),
            in_specs=[vmem_spec, vmem_spec, pl.BlockSpec((1, rank, columns), lambda k, m: (m[1 + FIELDS * k + 3], 0, 0))]
            + [vmem_spec] * n_flat,
            out_specs=pl.BlockSpec((block_len, columns), lambda k, m: (m[1 + FIELDS * k], 0)),
        ),
        out_shape=jax.ShapeDtypeStruct((row_total, columns), jnp.bfloat16),
        compiler_params=pltpu.CompilerParams(dimension_semantics=("arbitrary",), vmem_limit_bytes=16 * 1024 * 1024),
        cost_estimate=pl.CostEstimate(
            flops=2 * row_total * columns * 256, bytes_accessed=6 * row_total * columns, transcendentals=0),
    )(meta, mine, other, lowrank_up, *flat)


def on_ring(tokens, gate_matrix, up_matrix, lowrank_down, lowrank_up, tenant, adapter_storage_slot, live_count):
    block_count = tenant.shape[0]
    rows_here, width = tokens.shape
    chips = block_count
    block_len = 2 * rows_here
    row_total = block_count * block_len
    columns = gate_matrix.shape[1]
    me = lax.axis_index("tensor")
    core = lax.rem(me, 2)
    chip = me // 2
    place = jnp.where(lax.rem(chip, 2) == 0, chip // 2, chips - 1 - chip // 2)
    order = jnp.array([0, -1, 1, -2, 2, -3, 3, -4], jnp.int32)
    at = lax.rem(place + order + chips, chips)
    numbers = jnp.where(at < chips // 2, 2 * at, 2 * (chips - 1 - at) + 1)
    slots = adapter_storage_slot[tenant][numbers]
    here = (slots == me).astype(jnp.int32)
    fields = jnp.stack([numbers, live_count[numbers], here, slots], axis=1).astype(jnp.int32)
    meta = jnp.concatenate([core[None].astype(jnp.int32), fields.reshape(-1)])

    right, left = ring_pairs(chips, 1), ring_pairs(chips, -1)

    def send(value, pairs):
        return lax.ppermute(value, "tensor", pairs)

    def flip(value, bits):
        return lax.ppermute(value, "tensor", [(d, d ^ bits) for d in range(2 * chips)])

    down = lowrank_down[0]
    weights = (gate_matrix, up_matrix)
    n_tiles = columns // TILE
    from_left, from_right = tokens, tokens
    blocks = [[(tokens, False, 0), (flip(tokens, 1), True, 0)]]
    owned = []
    results = []
    first = 0
    for step in range(3):
        from_left = send(from_left, right)
        from_right = send(from_right, left)
        prod, act, part = pass_call(meta, first, blocks, down, *weights, 0, n_tiles, block_len, True, 0.0)
        results.append((first, len(blocks), 0, prod, act))
        owned.append(part)
        first += len(blocks)
        from_left, from_right = after_call((from_left, from_right), part)
        blocks = [[(v, False, 0), (flip(v, 1), True, 0)] for v in (from_left, from_right)]
    cut = rows_here // 2
    last_low = send(from_left[:cut], right)
    last_high = send(from_right[cut:], left)
    tiles, (prod, act, part) = tile_call(
        meta, first, blocks, down, *weights, {}, range(KEPT), range(KEPT), block_len, True, 0.0)
    results.append((first, 2, 0, prod, act))
    owned.append(part)
    last_low, last_high = after_call((last_low, last_high), part)
    blocks.append([
        (last_low, False, 0), (flip(last_low, 1), True, 0),
        (last_high, False, cut), (flip(last_high, 1), True, cut),
    ])
    mine, other = table_call(meta, first + 2, blocks[2], down, owned, row_total, block_len)
    mine = mine + flip(other, 1) + flip(mine, 2) + flip(other, 3)
    mine = mine + flip(mine, 4) + flip(mine, 8) + flip(mine, 12)
    other = flip(mine, 1)
    more = range(KEPT, KEPT + FETCHED)
    tiles, (prod, act) = tile_call(
        meta, first + 2, blocks[2:], down, *weights, tiles, more, range(KEPT), block_len, False, 1.0)
    results.append((first + 2, 1, 0, prod, act))
    _, (prod, act) = tile_call(
        meta, first, blocks, down, *weights, {t: tiles[t] for t in more}, range(KEPT + FETCHED, n_tiles),
        range(KEPT, n_tiles), block_len, False, 1.0, False)
    results.append((first, 3, KEPT * TILE, prod, act))
    return finish_call(meta, mine, other, lowrank_up, results, row_total, block_len)


def on_device(
    tokens,
    gate_matrix,
    up_matrix,
    lowrank_down,
    lowrank_up,
    tenant,
    adapter_storage_slot,
    live_count,
):
    my_index = lax.axis_index("tensor")
    gathered = lax.all_gather(tokens, "tensor", axis=0, tiled=True)
    row_total = gathered.shape[0]
    width = gathered.shape[1]
    block_count = tenant.shape[0]
    block_len = row_total // block_count
    hidden_columns = gate_matrix.shape[1]
    gate_out = jnp.dot(gathered, gate_matrix, preferred_element_type=jnp.float32)
    up_output = jnp.dot(gathered, up_matrix, preferred_element_type=jnp.float32)
    slot_numbers = adapter_storage_slot[tenant]
    rows_block = gathered.reshape(block_count, block_len, width)
    per_replica = lowrank_down.shape[0]
    rank_width = lowrank_down.shape[1]
    first_slot = my_index * per_replica
    pieces = []
    for block in range(block_count):
        slot_here = slot_numbers[block]
        mine = jnp.logical_and(slot_here >= first_slot, slot_here < first_slot + per_replica)
        resident_slot = jnp.clip(slot_here - first_slot, 0, per_replica - 1)
        down_matrix = lax.dynamic_index_in_dim(lowrank_down, resident_slot, 0, keepdims=False)
        block_rows = rows_block[block]

        def product_fn(rows_in=block_rows, map_in=down_matrix):
            return lax.dot_general(
                rows_in, map_in, (((1,), (1,)), ((), ())), preferred_element_type=jnp.float32
            )

        def empty_fn():
            return jnp.zeros((block_len, rank_width), jnp.float32)

        pieces.append(lax.cond(mine, product_fn, empty_fn))
    partial_value = jnp.stack(pieces, axis=0)
    reduced_output = lax.psum(partial_value, "tensor").astype(jnp.bfloat16)
    every_slot = jnp.arange(lowrank_up.shape[0], dtype=jnp.int32)
    slot_indicator = (slot_numbers[:, None] == every_slot[None, :]).astype(jnp.bfloat16)
    adapter_up = jnp.einsum(
        "oe,exz->oxz", slot_indicator, lowrank_up, preferred_element_type=jnp.float32
    ).astype(jnp.bfloat16)
    lowrank_term = jnp.einsum(
        "who,wok->whk", reduced_output, adapter_up, preferred_element_type=jnp.float32
    )
    up_output = up_output + lowrank_scale * lowrank_term.reshape(row_total, hidden_columns)
    positions = jnp.arange(block_len, dtype=jnp.int32)
    live_rows = (positions[None, :] < live_count[:, None]).reshape(row_total, 1)
    hidden = jnp.where(live_rows, jax.nn.silu(gate_out) * up_output, 0.0)
    return hidden.astype(jnp.bfloat16)


def solution(mesh):
    placed = (
        P(("groups", "tensor"), None),
        P(None, "tensor"),
        P(None, "tensor"),
        P("tensor", None, None),
        P(None, None, "tensor"),
        P("groups"),
        P(),
        P("groups"),
    )
    run = on_ring if mesh.shape["tensor"] == 16 else on_device
    return jax.shard_map(
        run, mesh=mesh, in_specs=placed, out_specs=P("groups", "tensor"), check_vma=False
    )
```

```python
import jax
import jax.numpy as jnp
from jax import lax
from jax.experimental import pallas as pl
from jax.experimental.pallas import tpu as pltpu
from jax.sharding import PartitionSpec as P

lowrank_scale = 2.0
TILE = 256
CHUNK = 16
KEPT = 3
FETCHED = 2
VMEM_LIMIT = 36 * 1024 * 1024


def chip_at(place, chips):
    half = chips // 2
    if place < half:
        return 2 * place
    return 2 * (chips - 1 - place) + 1


def ring_pairs(chips, step):
    pairs = []
    for place in range(chips):
        for core in range(2):
            pairs.append((2 * chip_at(place, chips) + core, 2 * chip_at((place + step) % chips, chips) + core))
    return pairs


FIELDS = 4


def chunks_of(meta_ref, block):
    return (meta_ref[1 + FIELDS * block + 1] + CHUNK - 1) // CHUNK


def packed_copies(meta_ref, first, places, piece_refs, held, sems, half):
    core = meta_ref[0]
    made = []
    at = 0
    for k, (number, sibling, offset, length) in enumerate(places):
        base = 0
        for before in range(number):
            base = base + chunks_of(meta_ref, first + before)
        live = chunks_of(meta_ref, first + number)
        side = (1 - core) if sibling else core
        for i in range(length // CHUNK):
            chunk = side * (half // CHUNK) + offset // CHUNK + i
            row = pl.multiple_of((base + chunk) * CHUNK, CHUNK)
            copy = pltpu.make_async_copy(
                piece_refs[k].at[pl.ds(i * CHUNK, CHUNK)], held.at[pl.ds(jnp.minimum(row, held.shape[0] - CHUNK), CHUNK)], sems.at[at])
            made.append((chunk < live, copy))
            at += 1
    return made


def flatten(blocks):
    flat, places = [], []
    for number, pieces in enumerate(blocks):
        for piece, sibling, offset in pieces:
            places.append((number, sibling, offset, piece.shape[0]))
            flat.append(piece)
    return flat, places


def pass_call(meta, first, blocks, down, gate_matrix, up_matrix, first_tile, tiles, block_len, want_reduced, share, after=()):
    width = gate_matrix.shape[0]
    rank = down.shape[0]
    count = len(blocks)
    rows = count * block_len
    half = block_len // 2
    flat, places = flatten(blocks)
    n_pieces = len(flat)
    n_copies = rows // CHUNK
    row_blocks = [slice(m, m + block_len) for m in range(0, rows, block_len)]

    def kernel(*refs):
        meta_ref = refs[0]
        piece_refs = refs[1:1 + n_pieces]
        rest = refs[1 + n_pieces:]
        if want_reduced:
            down_ref = rest[0]
            rest = rest[1:]
        gate_ref, up_ref = rest[:2]
        prod_ref, act_ref = rest[2 + len(after):4 + len(after)]
        rest = rest[4 + len(after):]
        if want_reduced:
            reduced_ref, held, in_sem, found_ref, down_held, down_sem = rest
        else:
            held, in_sem = rest
        total = 0
        for b in range(count):
            total = total + chunks_of(meta_ref, first + b)
        used = total * CHUNK

        @pl.when(pl.program_id(0) == 0)
        def _():
            copies = packed_copies(meta_ref, first, places, piece_refs, held, in_sem, half)
            for live, copy in copies:
                pl.when(live)(copy.start)
            if want_reduced:
                down_copy = pltpu.make_async_copy(down_ref, down_held, down_sem)
                down_copy.start()
            for live, copy in copies:
                pl.when(live)(copy.wait)
            if want_reduced:
                down_copy.wait()
                found_ref[...] = lax.dot_general(
                    held[...], down_held[...], (((1,), (1,)), ((), ())), preferred_element_type=jnp.float32)
                base = 0
                for b in range(count):
                    row = pl.multiple_of(base * CHUNK, CHUNK)
                    part = found_ref[pl.ds(row, block_len), :]
                    mine = meta_ref[1 + FIELDS * (first + b) + 2] == 1
                    reduced_ref[b * block_len:(b + 1) * block_len, :] = jnp.where(mine, part, 0.0).astype(jnp.bfloat16)
                    base = base + chunks_of(meta_ref, first + b)

        for some in row_blocks:
            def run(some=some):
                rows_in = held[some, :]
                gate_out = jnp.dot(rows_in, gate_ref[...], preferred_element_type=jnp.float32)
                up_out = jnp.dot(rows_in, up_ref[...], preferred_element_type=jnp.float32)
                act = gate_out * (0.5 * jnp.tanh(0.5 * gate_out) + 0.5)
                act_ref[some, :] = act.astype(jnp.bfloat16)
                prod_ref[some, :] = (act * up_out).astype(jnp.bfloat16)

            pl.when(used > some.start)(run)

    weight_spec = pl.BlockSpec((width, TILE), lambda j, m: (0, first_tile + j))
    any_spec = pl.BlockSpec(memory_space=pl.ANY)
    hbm_spec = pl.BlockSpec(memory_space=pltpu.HBM)
    in_specs = [hbm_spec if first == 0 else any_spec] * n_pieces
    operands = [meta] + flat
    if want_reduced:
        in_specs.append(hbm_spec)
        operands.append(down)
    in_specs += [weight_spec, weight_spec] + [any_spec] * len(after)
    operands += [gate_matrix, up_matrix] + list(after)
    out_specs = [pl.BlockSpec((rows, TILE), lambda j, m: (0, j))] * 2
    out_shape = [jax.ShapeDtypeStruct((rows, tiles * TILE), jnp.bfloat16)] * 2
    scratch = [pltpu.VMEM((rows, width), jnp.bfloat16), pltpu.SemaphoreType.DMA((n_copies,))]
    if want_reduced:
        out_specs.append(pl.BlockSpec((rows, rank), lambda j, m: (0, 0)))
        out_shape.append(jax.ShapeDtypeStruct((rows, rank), jnp.bfloat16))
        scratch += [
            pltpu.VMEM((rows, rank), jnp.float32),
            pltpu.VMEM((rank, width), jnp.bfloat16),
            pltpu.SemaphoreType.DMA(()),
        ]
    return pl.pallas_call(
        kernel,
        grid_spec=pltpu.PrefetchScalarGridSpec(
            num_scalar_prefetch=1, grid=(tiles,), in_specs=in_specs, out_specs=out_specs, scratch_shapes=scratch),
        out_shape=out_shape,
        compiler_params=pltpu.CompilerParams(dimension_semantics=("arbitrary",), vmem_limit_bytes=VMEM_LIMIT),
        cost_estimate=pl.CostEstimate(
            flops=int(share * 4 * rows * width * TILE * tiles),
            bytes_accessed=1024 + int(share * 4 * width * TILE * tiles), transcendentals=0),
    )(*operands)


def tile_call(meta, first, blocks, down, gate_matrix, up_matrix, given, fetch, compute, block_len, want_reduced, share, keep=True):
    width = gate_matrix.shape[0]
    rank = down.shape[0]
    count = len(blocks)
    rows = count * block_len
    half = block_len // 2
    flat, places = flatten(blocks)
    n_pieces = len(flat)
    n_copies = rows // CHUNK
    row_blocks = [slice(m, m + block_len) for m in range(0, rows, block_len)]
    held_tiles = list(given)
    order = held_tiles + list(fetch)
    n_given = 2 * len(held_tiles)
    n_out = 2 * len(order) if keep else n_given

    def kernel(*refs):
        meta_ref = refs[0]
        piece_refs = refs[1:1 + n_pieces]
        rest = refs[1 + n_pieces:]
        if want_reduced:
            down_ref = rest[0]
            rest = rest[1:]
        gate_ref, up_ref = rest[:2]
        rest = rest[2 + n_given:]
        tile_refs = list(rest[:n_out])
        prod_ref, act_ref = rest[n_out:n_out + 2]
        rest = rest[n_out + 2:]
        if not keep:
            tile_refs += rest[-2 * len(fetch):]
            rest = rest[:-2 * len(fetch)]
        if want_reduced:
            reduced_ref, held, in_sem, tile_sem, found_ref = rest
        else:
            held, in_sem, tile_sem = rest
        copies = packed_copies(meta_ref, first, places, piece_refs, held, in_sem, half)
        for live, copy in copies:
            pl.when(live)(copy.start)
        loads = {}
        for n, t in enumerate(fetch):
            at = len(held_tiles) + n
            loads[t] = [
                pltpu.make_async_copy(ref.at[:, t * TILE:(t + 1) * TILE], tile_refs[2 * at + side], tile_sem.at[2 * n + side])
                for side, ref in enumerate((gate_ref, up_ref))
            ]
            for load in loads[t]:
                load.start()
        total = 0
        for b in range(count):
            total = total + chunks_of(meta_ref, first + b)
        used = total * CHUNK
        for live, copy in copies:
            pl.when(live)(copy.wait)
        if want_reduced:
            found_ref[...] = lax.dot_general(
                held[...], down_ref[...], (((1,), (1,)), ((), ())), preferred_element_type=jnp.float32)
            base = 0
            for b in range(count):
                row = pl.multiple_of(base * CHUNK, CHUNK)
                part = found_ref[pl.ds(row, block_len), :]
                mine = meta_ref[1 + FIELDS * (first + b) + 2] == 1
                reduced_ref[b * block_len:(b + 1) * block_len, :] = jnp.where(mine, part, 0.0).astype(jnp.bfloat16)
                base = base + chunks_of(meta_ref, first + b)
        for n, t in enumerate(compute):
            for load in loads.pop(t, []):
                load.wait()
            at = order.index(t)
            cols = slice(n * TILE, (n + 1) * TILE)
            for some in row_blocks:
                def run(some=some, at=at, cols=cols):
                    rows_in = held[some, :]
                    gate_out = jnp.dot(rows_in, tile_refs[2 * at][...], preferred_element_type=jnp.float32)
                    up_out = jnp.dot(rows_in, tile_refs[2 * at + 1][...], preferred_element_type=jnp.float32)
                    act = gate_out * (0.5 * jnp.tanh(0.5 * gate_out) + 0.5)
                    act_ref[some, cols] = act.astype(jnp.bfloat16)
                    prod_ref[some, cols] = (act * up_out).astype(jnp.bfloat16)

                pl.when(used > some.start)(run)
        for t in list(loads):
            for load in loads[t]:
                load.wait()

    any_spec = pl.BlockSpec(memory_space=pl.ANY)
    vmem_spec = pl.BlockSpec(memory_space=pltpu.VMEM)
    in_specs = [any_spec] * n_pieces
    operands = [meta] + flat
    if want_reduced:
        in_specs.append(vmem_spec)
        operands.append(down)
    in_specs += [any_spec, any_spec] + [vmem_spec] * n_given
    operands += [gate_matrix, up_matrix]
    aliases = {len(operands) + k: k for k in range(n_given)}
    for t in held_tiles:
        operands += list(given[t])
    result = jax.ShapeDtypeStruct((rows, len(compute) * TILE), jnp.bfloat16)
    out_shape = [pltpu.VMEM((width, TILE), jnp.bfloat16)] * n_out + [result, result]
    scratch = [
        pltpu.VMEM((rows, width), jnp.bfloat16),
        pltpu.SemaphoreType.DMA((n_copies,)),
        pltpu.SemaphoreType.DMA((max(1, 2 * len(fetch)),)),
    ]
    if want_reduced:
        out_shape.append(jax.ShapeDtypeStruct((rows, rank), jnp.bfloat16))
        scratch.append(pltpu.VMEM((rows, rank), jnp.float32))
    limit = rows * 32 * 1024 + 4 * 1024 * 1024
    if not keep:
        scratch += [pltpu.VMEM((width, TILE), jnp.bfloat16)] * (2 * len(fetch))
        limit += 4 * width * TILE * len(fetch)
    out = pl.pallas_call(
        kernel,
        grid_spec=pltpu.PrefetchScalarGridSpec(
            num_scalar_prefetch=1, grid=(1,), in_specs=in_specs, out_specs=[vmem_spec] * len(out_shape), scratch_shapes=scratch),
        out_shape=out_shape,
        input_output_aliases=aliases,
        compiler_params=pltpu.CompilerParams(dimension_semantics=("arbitrary",), vmem_limit_bytes=limit),
        cost_estimate=pl.CostEstimate(
            flops=int(share * 4 * rows * width * TILE * len(compute)),
            bytes_accessed=1024 + int(share * 4 * width * TILE * len(compute)), transcendentals=0),
    )(*operands)
    tiles = {t: (out[2 * n], out[2 * n + 1]) for n, t in enumerate(order[:n_out // 2])}
    return tiles, out[n_out:]


def after_call(values, other):
    any_spec = pl.BlockSpec(memory_space=pl.ANY)

    def kernel(*refs):
        pass

    return pl.pallas_call(
        kernel,
        in_specs=[any_spec] * (len(values) + 1),
        out_specs=[any_spec] * len(values),
        out_shape=[jax.ShapeDtypeStruct(v.shape, v.dtype) for v in values],
        input_output_aliases={k: k for k in range(len(values))},
        compiler_params=pltpu.CompilerParams(vmem_limit_bytes=1024 * 1024),
        cost_estimate=pl.CostEstimate(flops=0, bytes_accessed=0, transcendentals=0),
    )(*values, other)


def quarter_of(block, row_total, block_len):
    per_quarter = row_total // block_len // 4
    quarter = block // per_quarter
    return quarter, pl.multiple_of((block - quarter * per_quarter) * block_len, block_len)


def table_call(meta, number, pieces, down, owned, row_total, block_len):
    rank, width = down.shape
    half = block_len // 2
    flat, places = flatten([pieces])
    n_pieces = len(flat)
    n_owned = len(owned)

    def kernel(*refs):
        meta_ref = refs[0]
        piece_refs = refs[1:1 + n_pieces]
        down_ref = refs[1 + n_pieces]
        owned_refs = refs[2 + n_pieces:2 + n_pieces + n_owned]
        mine_ref, other_ref, held, in_sem = refs[2 + n_pieces + n_owned:]
        core = meta_ref[0]
        copies = []
        for k, (_, sibling, offset, length) in enumerate(places):
            side = (1 - core) if sibling else core
            row = pl.multiple_of(side * half + offset, 32)
            copies.append(pltpu.make_async_copy(piece_refs[k], held.at[pl.ds(row, length)], in_sem.at[k]))
        for copy in copies:
            copy.start()

        def put(at, value):
            quarter, row = quarter_of(meta_ref[1 + FIELDS * at], row_total, block_len)
            for q in range(4):
                @pl.when(quarter == q)
                def _(q=q):
                    lanes = slice(q % 2 * rank, (q % 2 + 1) * rank)

                    @pl.when(core == q // 2)
                    def _():
                        mine_ref[pl.ds(row, block_len), lanes] = value

                    @pl.when(core != q // 2)
                    def _():
                        other_ref[pl.ds(row, block_len), lanes] = value

        at = 0
        for ref in owned_refs:
            for b in range(ref.shape[0] // block_len):
                put(at, ref[b * block_len:(b + 1) * block_len, :])
                at += 1
        for copy in copies:
            copy.wait()
        found = lax.dot_general(held[...], down_ref[...], (((1,), (1,)), ((), ())), preferred_element_type=jnp.float32)
        put(number, jnp.where(meta_ref[1 + FIELDS * number + 2] == 1, found, 0.0).astype(jnp.bfloat16))

    whole = pl.BlockSpec(memory_space=pltpu.VMEM)
    return pl.pallas_call(
        kernel,
        in_specs=[pl.BlockSpec(memory_space=pltpu.SMEM)] + [pl.BlockSpec(memory_space=pl.ANY)] * n_pieces + [whole] * (1 + n_owned),
        out_specs=[whole] * 2,
        out_shape=[jax.ShapeDtypeStruct((row_total // 4, 2 * rank), jnp.bfloat16)] * 2,
        scratch_shapes=[pltpu.VMEM((block_len, width), jnp.bfloat16), pltpu.SemaphoreType.DMA((n_pieces,))],
        compiler_params=pltpu.CompilerParams(vmem_limit_bytes=8 * 1024 * 1024),
        cost_estimate=pl.CostEstimate(flops=0, bytes_accessed=1024 * 1024, transcendentals=0),
    )(meta, *flat, down, *owned)


def finish_call(meta, mine, other, lowrank_up, results, row_total, block_len):
    rank, columns = lowrank_up.shape[1:]
    total_blocks = row_total // block_len
    flat = []
    for result in results:
        flat += result[3:]
    n_flat = len(flat)

    def kernel(*refs):
        meta_ref, mine_ref, other_ref, map_ref = refs[:4]
        result_refs = refs[4:4 + n_flat]
        out_ref, maps, map_sem = refs[4 + n_flat:]
        k = pl.program_id(0)

        def map_copy(at):
            return pltpu.make_async_copy(map_ref.at[meta_ref[1 + FIELDS * at + 3]], maps.at[at], map_sem.at[at])

        @pl.when(k == 0)
        def _():
            for at in range(total_blocks):
                map_copy(at).start()

        map_copy(k).wait()
        quarter, row = quarter_of(meta_ref[1 + FIELDS * k], row_total, block_len)
        at_row = pl.ds(row, block_len)
        both = jnp.where(quarter // 2 == meta_ref[0], mine_ref[at_row, :], other_ref[at_row, :])
        reduced = jnp.where(lax.rem(quarter, 2) == 0, both[:, :rank], both[:, rank:])
        live = meta_ref[1 + FIELDS * k + 1]
        for n, (begun, count, column, prod, _) in enumerate(results):
            def run(n=n, begun=begun, count=count, column=column, prod=prod):
                base = 0
                for b in range(begun, begun + count - 1):
                    base = base + jnp.where(b < k, chunks_of(meta_ref, b), 0)
                at = pl.ds(pl.multiple_of(base * CHUNK, CHUNK), block_len)
                for c in range(0, prod.shape[1], TILE):
                    cols = slice(column + c, column + c + TILE)
                    term = jnp.dot(reduced, maps[k, :, cols], preferred_element_type=jnp.float32)
                    prods = result_refs[2 * n][at, c:c + TILE].astype(jnp.float32)
                    acts = result_refs[2 * n + 1][at, c:c + TILE].astype(jnp.float32)
                    sum_of = prods + acts * (lowrank_scale * term)
                    shown = lax.broadcasted_iota(jnp.int32, sum_of.shape, 0) < live
                    out_ref[:, cols] = jnp.where(shown, sum_of, 0.0).astype(jnp.bfloat16)

            pl.when(jnp.logical_and(k >= begun, k < begun + count))(run)

    vmem_spec = pl.BlockSpec(memory_space=pltpu.VMEM)
    return pl.pallas_call(
        kernel,
        grid_spec=pltpu.PrefetchScalarGridSpec(
            num_scalar_prefetch=1,
            grid=(total_blocks,),
            in_specs=[vmem_spec, vmem_spec, pl.BlockSpec(memory_space=pltpu.HBM)]
            + [vmem_spec] * n_flat,
            out_specs=pl.BlockSpec((block_len, columns), lambda k, m: (m[1 + FIELDS * k], 0)),
            scratch_shapes=[
                pltpu.VMEM((total_blocks, rank, columns), jnp.bfloat16),
                pltpu.SemaphoreType.DMA((total_blocks,)),
            ],
        ),
        out_shape=jax.ShapeDtypeStruct((row_total, columns), jnp.bfloat16),
        compiler_params=pltpu.CompilerParams(dimension_semantics=("arbitrary",), vmem_limit_bytes=16 * 1024 * 1024),
        cost_estimate=pl.CostEstimate(
            flops=2 * row_total * columns * 256, bytes_accessed=6 * row_total * columns, transcendentals=0),
    )(meta, mine, other, lowrank_up, *flat)


def on_ring(tokens, gate_matrix, up_matrix, lowrank_down, lowrank_up, tenant, adapter_storage_slot, live_count):
    block_count = tenant.shape[0]
    rows_here, width = tokens.shape
    chips = block_count
    block_len = 2 * rows_here
    row_total = block_count * block_len
    columns = gate_matrix.shape[1]
    me = lax.axis_index("tensor")
    core = lax.rem(me, 2)
    chip = me // 2
    place = jnp.where(lax.rem(chip, 2) == 0, chip // 2, chips - 1 - chip // 2)
    order = jnp.array([0, -1, 1, -2, 2, -3, 3, -4], jnp.int32)
    at = lax.rem(place + order + chips, chips)
    numbers = jnp.where(at < chips // 2, 2 * at, 2 * (chips - 1 - at) + 1)
    slots = adapter_storage_slot[tenant][numbers]
    here = (slots == me).astype(jnp.int32)
    fields = jnp.stack([numbers, live_count[numbers], here, slots], axis=1).astype(jnp.int32)
    meta = jnp.concatenate([core[None].astype(jnp.int32), fields.reshape(-1)])

    right, left = ring_pairs(chips, 1), ring_pairs(chips, -1)

    def send(value, pairs):
        return lax.ppermute(value, "tensor", pairs)

    def flip(value, bits):
        return lax.ppermute(value, "tensor", [(d, d ^ bits) for d in range(2 * chips)])

    down = lowrank_down[0]
    weights = (gate_matrix, up_matrix)
    n_tiles = columns // TILE
    from_left, from_right = tokens, tokens
    blocks = [[(tokens, False, 0), (flip(tokens, 1), True, 0)]]
    owned = []
    results = []
    first = 0
    for step in range(3):
        from_left = send(from_left, right)
        from_right = send(from_right, left)
        prod, act, part = pass_call(meta, first, blocks, down, *weights, 0, n_tiles, block_len, True, 0.0)
        results.append((first, len(blocks), 0, prod, act))
        owned.append(part)
        first += len(blocks)
        from_left, from_right = after_call((from_left, from_right), part)
        blocks = [[(v, False, 0), (flip(v, 1), True, 0)] for v in (from_left, from_right)]
    cut = rows_here // 2
    last_low = send(from_left[:cut], right)
    last_high = send(from_right[cut:], left)
    tiles, (prod, act, part) = tile_call(
        meta, first, blocks, down, *weights, {}, range(KEPT), range(KEPT), block_len, True, 0.0)
    results.append((first, 2, 0, prod, act))
    owned.append(part)
    last_low, last_high = after_call((last_low, last_high), part)
    blocks.append([
        (last_low, False, 0), (flip(last_low, 1), True, 0),
        (last_high, False, cut), (flip(last_high, 1), True, cut),
    ])
    mine, other = table_call(meta, first + 2, blocks[2], down, owned, row_total, block_len)
    mine = mine + flip(other, 1) + flip(mine, 2) + flip(other, 3)
    mine = mine + flip(mine, 4) + flip(mine, 8) + flip(mine, 12)
    other = flip(mine, 1)
    more = range(KEPT, KEPT + FETCHED)
    tiles, (prod, act) = tile_call(
        meta, first + 2, blocks[2:], down, *weights, tiles, more, range(KEPT), block_len, False, 1.0)
    results.append((first + 2, 1, 0, prod, act))
    _, (prod, act) = tile_call(
        meta, first, blocks, down, *weights, {t: tiles[t] for t in more}, range(KEPT + FETCHED, n_tiles),
        range(KEPT, n_tiles), block_len, False, 1.0, False)
    results.append((first, 3, KEPT * TILE, prod, act))
    return finish_call(meta, mine, other, lowrank_up, results, row_total, block_len)


def on_device(
    tokens,
    gate_matrix,
    up_matrix,
    lowrank_down,
    lowrank_up,
    tenant,
    adapter_storage_slot,
    live_count,
):
    my_index = lax.axis_index("tensor")
    gathered = lax.all_gather(tokens, "tensor", axis=0, tiled=True)
    row_total = gathered.shape[0]
    width = gathered.shape[1]
    block_count = tenant.shape[0]
    block_len = row_total // block_count
    hidden_columns = gate_matrix.shape[1]
    gate_out = jnp.dot(gathered, gate_matrix, preferred_element_type=jnp.float32)
    up_output = jnp.dot(gathered, up_matrix, preferred_element_type=jnp.float32)
    slot_numbers = adapter_storage_slot[tenant]
    rows_block = gathered.reshape(block_count, block_len, width)
    per_replica = lowrank_down.shape[0]
    rank_width = lowrank_down.shape[1]
    first_slot = my_index * per_replica
    pieces = []
    for block in range(block_count):
        slot_here = slot_numbers[block]
        mine = jnp.logical_and(slot_here >= first_slot, slot_here < first_slot + per_replica)
        resident_slot = jnp.clip(slot_here - first_slot, 0, per_replica - 1)
        down_matrix = lax.dynamic_index_in_dim(lowrank_down, resident_slot, 0, keepdims=False)
        block_rows = rows_block[block]

        def product_fn(rows_in=block_rows, map_in=down_matrix):
            return lax.dot_general(
                rows_in, map_in, (((1,), (1,)), ((), ())), preferred_element_type=jnp.float32
            )

        def empty_fn():
            return jnp.zeros((block_len, rank_width), jnp.float32)

        pieces.append(lax.cond(mine, product_fn, empty_fn))
    partial_value = jnp.stack(pieces, axis=0)
    reduced_output = lax.psum(partial_value, "tensor").astype(jnp.bfloat16)
    every_slot = jnp.arange(lowrank_up.shape[0], dtype=jnp.int32)
    slot_indicator = (slot_numbers[:, None] == every_slot[None, :]).astype(jnp.bfloat16)
    adapter_up = jnp.einsum(
        "oe,exz->oxz", slot_indicator, lowrank_up, preferred_element_type=jnp.float32
    ).astype(jnp.bfloat16)
    lowrank_term = jnp.einsum(
        "who,wok->whk", reduced_output, adapter_up, preferred_element_type=jnp.float32
    )
    up_output = up_output + lowrank_scale * lowrank_term.reshape(row_total, hidden_columns)
    positions = jnp.arange(block_len, dtype=jnp.int32)
    live_rows = (positions[None, :] < live_count[:, None]).reshape(row_total, 1)
    hidden = jnp.where(live_rows, jax.nn.silu(gate_out) * up_output, 0.0)
    return hidden.astype(jnp.bfloat16)


def solution(mesh):
    placed = (
        P(("groups", "tensor"), None),
        P(None, "tensor"),
        P(None, "tensor"),
        P("tensor", None, None),
        P(None, None, "tensor"),
        P("groups"),
        P(),
        P("groups"),
    )
    run = on_ring if mesh.shape["tensor"] == 16 else on_device
    return jax.shard_map(
        run, mesh=mesh, in_specs=placed, out_specs=P("groups", "tensor"), check_vma=False
    )
```

```python
import jax
import jax.numpy as jnp
from jax import lax
from jax.experimental import pallas as pl
from jax.experimental.pallas import tpu as pltpu
from jax.sharding import PartitionSpec as P

lowrank_scale = 2.0
TILE = 256
CHUNK = 16
KEPT = 4
FETCHED = 1
VMEM_LIMIT = 36 * 1024 * 1024


def chip_at(place, chips):
    half = chips // 2
    if place < half:
        return 2 * place
    return 2 * (chips - 1 - place) + 1


def ring_pairs(chips, step):
    pairs = []
    for place in range(chips):
        for core in range(2):
            pairs.append((2 * chip_at(place, chips) + core, 2 * chip_at((place + step) % chips, chips) + core))
    return pairs


FIELDS = 4


def chunks_of(meta_ref, block):
    return (meta_ref[1 + FIELDS * block + 1] + CHUNK - 1) // CHUNK


def packed_copies(meta_ref, first, places, piece_refs, held, sems, half):
    core = meta_ref[0]
    made = []
    at = 0
    for k, (number, sibling, offset, length) in enumerate(places):
        base = 0
        for before in range(number):
            base = base + chunks_of(meta_ref, first + before)
        live = chunks_of(meta_ref, first + number)
        side = (1 - core) if sibling else core
        for i in range(length // CHUNK):
            chunk = side * (half // CHUNK) + offset // CHUNK + i
            row = pl.multiple_of((base + chunk) * CHUNK, CHUNK)
            copy = pltpu.make_async_copy(
                piece_refs[k].at[pl.ds(i * CHUNK, CHUNK)], held.at[pl.ds(jnp.minimum(row, held.shape[0] - CHUNK), CHUNK)], sems.at[at])
            made.append((chunk < live, copy))
            at += 1
    return made


def flatten(blocks):
    flat, places = [], []
    for number, pieces in enumerate(blocks):
        for piece, sibling, offset in pieces:
            places.append((number, sibling, offset, piece.shape[0]))
            flat.append(piece)
    return flat, places


def pass_call(meta, first, blocks, down, gate_matrix, up_matrix, first_tile, tiles, block_len, want_reduced, share, after=()):
    width = gate_matrix.shape[0]
    rank = down.shape[0]
    count = len(blocks)
    rows = count * block_len
    half = block_len // 2
    flat, places = flatten(blocks)
    n_pieces = len(flat)
    n_copies = rows // CHUNK
    sizes = [m for m in range(block_len, rows + 1, block_len // 2)]

    def kernel(*refs):
        meta_ref = refs[0]
        piece_refs = refs[1:1 + n_pieces]
        rest = refs[1 + n_pieces:]
        if want_reduced:
            down_ref = rest[0]
            rest = rest[1:]
        gate_ref, up_ref = rest[:2]
        prod_ref, act_ref = rest[2 + len(after):4 + len(after)]
        rest = rest[4 + len(after):]
        if want_reduced:
            reduced_ref, held, in_sem, found_ref = rest
        else:
            held, in_sem = rest
        total = 0
        for b in range(count):
            total = total + chunks_of(meta_ref, first + b)
        used = total * CHUNK

        @pl.when(pl.program_id(0) == 0)
        def _():
            copies = packed_copies(meta_ref, first, places, piece_refs, held, in_sem, half)
            for live, copy in copies:
                pl.when(live)(copy.start)
            for live, copy in copies:
                pl.when(live)(copy.wait)
            if want_reduced:
                found_ref[...] = lax.dot_general(
                    held[...], down_ref[...], (((1,), (1,)), ((), ())), preferred_element_type=jnp.float32)
                base = 0
                for b in range(count):
                    row = pl.multiple_of(base * CHUNK, CHUNK)
                    part = found_ref[pl.ds(row, block_len), :]
                    mine = meta_ref[1 + FIELDS * (first + b) + 2] == 1
                    reduced_ref[b * block_len:(b + 1) * block_len, :] = jnp.where(mine, part, 0.0).astype(jnp.bfloat16)
                    base = base + chunks_of(meta_ref, first + b)

        below = 0
        for size in sizes:
            def run(size=size):
                rows_in = held[:size, :]
                gate_out = jnp.dot(rows_in, gate_ref[...], preferred_element_type=jnp.float32)
                up_out = jnp.dot(rows_in, up_ref[...], preferred_element_type=jnp.float32)
                act = gate_out * (0.5 * jnp.tanh(0.5 * gate_out) + 0.5)
                act_ref[:size, :] = act.astype(jnp.bfloat16)
                prod_ref[:size, :] = (act * up_out).astype(jnp.bfloat16)

            pl.when(jnp.logical_and(used > below, used <= size))(run)
            below = size

    weight_spec = pl.BlockSpec((width, TILE), lambda j, m: (0, first_tile + j))
    any_spec = pl.BlockSpec(memory_space=pl.ANY)
    in_specs = [any_spec] * n_pieces
    operands = [meta] + flat
    if want_reduced:
        in_specs.append(pl.BlockSpec((rank, width), lambda j, m: (0, 0)))
        operands.append(down)
    in_specs += [weight_spec, weight_spec] + [any_spec] * len(after)
    operands += [gate_matrix, up_matrix] + list(after)
    out_specs = [pl.BlockSpec((rows, TILE), lambda j, m: (0, j))] * 2
    out_shape = [jax.ShapeDtypeStruct((rows, tiles * TILE), jnp.bfloat16)] * 2
    scratch = [pltpu.VMEM((rows, width), jnp.bfloat16), pltpu.SemaphoreType.DMA((n_copies,))]
    if want_reduced:
        out_specs.append(pl.BlockSpec((rows, rank), lambda j, m: (0, 0)))
        out_shape.append(jax.ShapeDtypeStruct((rows, rank), jnp.bfloat16))
        scratch.append(pltpu.VMEM((rows, rank), jnp.float32))
    return pl.pallas_call(
        kernel,
        grid_spec=pltpu.PrefetchScalarGridSpec(
            num_scalar_prefetch=1, grid=(tiles,), in_specs=in_specs, out_specs=out_specs, scratch_shapes=scratch),
        out_shape=out_shape,
        compiler_params=pltpu.CompilerParams(dimension_semantics=("arbitrary",), vmem_limit_bytes=VMEM_LIMIT),
        cost_estimate=pl.CostEstimate(
            flops=int(share * 4 * rows * width * TILE * tiles),
            bytes_accessed=1024 + int(share * 4 * width * TILE * tiles), transcendentals=0),
    )(*operands)


def tile_call(meta, first, blocks, down, gate_matrix, up_matrix, given, fetch, compute, block_len, want_reduced, share, keep=True):
    width = gate_matrix.shape[0]
    rank = down.shape[0]
    count = len(blocks)
    rows = count * block_len
    half = block_len // 2
    flat, places = flatten(blocks)
    n_pieces = len(flat)
    n_copies = rows // CHUNK
    row_blocks = [slice(m, m + block_len) for m in range(0, rows, block_len)]
    held_tiles = list(given)
    order = held_tiles + list(fetch)
    n_given = 2 * len(held_tiles)
    n_out = 2 * len(order) if keep else n_given

    def kernel(*refs):
        meta_ref = refs[0]
        piece_refs = refs[1:1 + n_pieces]
        rest = refs[1 + n_pieces:]
        if want_reduced:
            down_ref = rest[0]
            rest = rest[1:]
        gate_ref, up_ref = rest[:2]
        rest = rest[2 + n_given:]
        tile_refs = list(rest[:n_out])
        prod_ref, act_ref = rest[n_out:n_out + 2]
        rest = rest[n_out + 2:]
        if not keep:
            tile_refs += rest[-2 * len(fetch):]
            rest = rest[:-2 * len(fetch)]
        if want_reduced:
            reduced_ref, held, in_sem, tile_sem, found_ref = rest
        else:
            held, in_sem, tile_sem = rest
        copies = packed_copies(meta_ref, first, places, piece_refs, held, in_sem, half)
        for live, copy in copies:
            pl.when(live)(copy.start)
        loads = {}
        for n, t in enumerate(fetch):
            at = len(held_tiles) + n
            loads[t] = [
                pltpu.make_async_copy(ref.at[:, t * TILE:(t + 1) * TILE], tile_refs[2 * at + side], tile_sem.at[2 * n + side])
                for side, ref in enumerate((gate_ref, up_ref))
            ]
            for load in loads[t]:
                load.start()
        total = 0
        for b in range(count):
            total = total + chunks_of(meta_ref, first + b)
        used = total * CHUNK
        for live, copy in copies:
            pl.when(live)(copy.wait)
        if want_reduced:
            found_ref[...] = lax.dot_general(
                held[...], down_ref[...], (((1,), (1,)), ((), ())), preferred_element_type=jnp.float32)
            base = 0
            for b in range(count):
                row = pl.multiple_of(base * CHUNK, CHUNK)
                part = found_ref[pl.ds(row, block_len), :]
                mine = meta_ref[1 + FIELDS * (first + b) + 2] == 1
                reduced_ref[b * block_len:(b + 1) * block_len, :] = jnp.where(mine, part, 0.0).astype(jnp.bfloat16)
                base = base + chunks_of(meta_ref, first + b)
        for n, t in enumerate(compute):
            for load in loads.pop(t, []):
                load.wait()
            at = order.index(t)
            cols = slice(n * TILE, (n + 1) * TILE)
            for some in row_blocks:
                def run(some=some, at=at, cols=cols):
                    rows_in = held[some, :]
                    gate_out = jnp.dot(rows_in, tile_refs[2 * at][...], preferred_element_type=jnp.float32)
                    up_out = jnp.dot(rows_in, tile_refs[2 * at + 1][...], preferred_element_type=jnp.float32)
                    act = gate_out * (0.5 * jnp.tanh(0.5 * gate_out) + 0.5)
                    act_ref[some, cols] = act.astype(jnp.bfloat16)
                    prod_ref[some, cols] = (act * up_out).astype(jnp.bfloat16)

                pl.when(used > some.start)(run)
        for t in list(loads):
            for load in loads[t]:
                load.wait()

    any_spec = pl.BlockSpec(memory_space=pl.ANY)
    vmem_spec = pl.BlockSpec(memory_space=pltpu.VMEM)
    in_specs = [any_spec] * n_pieces
    operands = [meta] + flat
    if want_reduced:
        in_specs.append(vmem_spec)
        operands.append(down)
    in_specs += [any_spec, any_spec] + [vmem_spec] * n_given
    operands += [gate_matrix, up_matrix]
    aliases = {len(operands) + k: k for k in range(n_given)}
    for t in held_tiles:
        operands += list(given[t])
    result = jax.ShapeDtypeStruct((rows, len(compute) * TILE), jnp.bfloat16)
    out_shape = [pltpu.VMEM((width, TILE), jnp.bfloat16)] * n_out + [result, result]
    scratch = [
        pltpu.VMEM((rows, width), jnp.bfloat16),
        pltpu.SemaphoreType.DMA((n_copies,)),
        pltpu.SemaphoreType.DMA((max(1, 2 * len(fetch)),)),
    ]
    if want_reduced:
        out_shape.append(jax.ShapeDtypeStruct((rows, rank), jnp.bfloat16))
        scratch.append(pltpu.VMEM((rows, rank), jnp.float32))
    limit = rows * 20 * 1024 + 2 * 1024 * 1024
    if not keep:
        scratch += [pltpu.VMEM((width, TILE), jnp.bfloat16)] * (2 * len(fetch))
        limit += 4 * width * TILE * len(fetch)
    out = pl.pallas_call(
        kernel,
        grid_spec=pltpu.PrefetchScalarGridSpec(
            num_scalar_prefetch=1, grid=(1,), in_specs=in_specs, out_specs=[vmem_spec] * len(out_shape), scratch_shapes=scratch),
        out_shape=out_shape,
        input_output_aliases=aliases,
        compiler_params=pltpu.CompilerParams(dimension_semantics=("arbitrary",), vmem_limit_bytes=limit),
        cost_estimate=pl.CostEstimate(
            flops=int(share * 4 * rows * width * TILE * len(compute)),
            bytes_accessed=1024 + int(share * 4 * width * TILE * len(compute)), transcendentals=0),
    )(*operands)
    tiles = {t: (out[2 * n], out[2 * n + 1]) for n, t in enumerate(order[:n_out // 2])}
    return tiles, out[n_out:]


def after_call(values, other):
    any_spec = pl.BlockSpec(memory_space=pl.ANY)

    def kernel(*refs):
        pass

    return pl.pallas_call(
        kernel,
        in_specs=[any_spec] * (len(values) + 1),
        out_specs=[any_spec] * len(values),
        out_shape=[jax.ShapeDtypeStruct(v.shape, v.dtype) for v in values],
        input_output_aliases={k: k for k in range(len(values))},
        compiler_params=pltpu.CompilerParams(vmem_limit_bytes=1024 * 1024),
        cost_estimate=pl.CostEstimate(flops=0, bytes_accessed=0, transcendentals=0),
    )(*values, other)


def quarter_of(block, row_total, block_len):
    per_quarter = row_total // block_len // 4
    quarter = block // per_quarter
    return quarter, pl.multiple_of((block - quarter * per_quarter) * block_len, block_len)


def table_call(meta, number, pieces, down, owned, row_total, block_len):
    rank, width = down.shape
    half = block_len // 2
    flat, places = flatten([pieces])
    n_pieces = len(flat)
    n_owned = len(owned)

    def kernel(*refs):
        meta_ref = refs[0]
        piece_refs = refs[1:1 + n_pieces]
        down_ref = refs[1 + n_pieces]
        owned_refs = refs[2 + n_pieces:2 + n_pieces + n_owned]
        mine_ref, other_ref, held, in_sem = refs[2 + n_pieces + n_owned:]
        core = meta_ref[0]
        copies = []
        for k, (_, sibling, offset, length) in enumerate(places):
            side = (1 - core) if sibling else core
            row = pl.multiple_of(side * half + offset, 32)
            copies.append(pltpu.make_async_copy(piece_refs[k], held.at[pl.ds(row, length)], in_sem.at[k]))
        for copy in copies:
            copy.start()

        def put(at, value):
            quarter, row = quarter_of(meta_ref[1 + FIELDS * at], row_total, block_len)
            for q in range(4):
                @pl.when(quarter == q)
                def _(q=q):
                    lanes = slice(q % 2 * rank, (q % 2 + 1) * rank)

                    @pl.when(core == q // 2)
                    def _():
                        mine_ref[pl.ds(row, block_len), lanes] = value

                    @pl.when(core != q // 2)
                    def _():
                        other_ref[pl.ds(row, block_len), lanes] = value

        at = 0
        for ref in owned_refs:
            for b in range(ref.shape[0] // block_len):
                put(at, ref[b * block_len:(b + 1) * block_len, :])
                at += 1
        for copy in copies:
            copy.wait()
        found = lax.dot_general(held[...], down_ref[...], (((1,), (1,)), ((), ())), preferred_element_type=jnp.float32)
        put(number, jnp.where(meta_ref[1 + FIELDS * number + 2] == 1, found, 0.0).astype(jnp.bfloat16))

    whole = pl.BlockSpec(memory_space=pltpu.VMEM)
    return pl.pallas_call(
        kernel,
        in_specs=[pl.BlockSpec(memory_space=pltpu.SMEM)] + [pl.BlockSpec(memory_space=pl.ANY)] * n_pieces + [whole] * (1 + n_owned),
        out_specs=[whole] * 2,
        out_shape=[jax.ShapeDtypeStruct((row_total // 4, 2 * rank), jnp.bfloat16)] * 2,
        scratch_shapes=[pltpu.VMEM((block_len, width), jnp.bfloat16), pltpu.SemaphoreType.DMA((n_pieces,))],
        compiler_params=pltpu.CompilerParams(vmem_limit_bytes=8 * 1024 * 1024),
        cost_estimate=pl.CostEstimate(flops=0, bytes_accessed=1024 * 1024, transcendentals=0),
    )(meta, *flat, down, *owned)


def add_call(values, other):
    vmem_spec = pl.BlockSpec(memory_space=pltpu.VMEM)

    def kernel(*refs):
        total = refs[0][...]
        for ref in refs[1:len(values)]:
            total = total + ref[...]
        refs[-1][...] = total

    return pl.pallas_call(
        kernel,
        in_specs=[vmem_spec] * len(values) + [pl.BlockSpec(memory_space=pl.ANY)],
        out_specs=vmem_spec,
        out_shape=jax.ShapeDtypeStruct(values[0].shape, values[0].dtype),
        compiler_params=pltpu.CompilerParams(vmem_limit_bytes=2 * 1024 * 1024),
        cost_estimate=pl.CostEstimate(flops=0, bytes_accessed=1024, transcendentals=0),
    )(*values, other)


def finish_call(meta, mine, other, lowrank_up, results, row_total, block_len):
    rank, columns = lowrank_up.shape[1:]
    total_blocks = row_total // block_len
    flat = []
    for result in results:
        flat += result[3:]
    n_flat = len(flat)

    def kernel(*refs):
        meta_ref, mine_ref, other_ref, map_ref = refs[:4]
        result_refs = refs[4:4 + n_flat]
        out_ref = refs[4 + n_flat]
        k = pl.program_id(0)
        quarter, row = quarter_of(meta_ref[1 + FIELDS * k], row_total, block_len)
        at_row = pl.ds(row, block_len)
        both = jnp.where(quarter // 2 == meta_ref[0], mine_ref[at_row, :], other_ref[at_row, :])
        reduced = jnp.where(lax.rem(quarter, 2) == 0, both[:, :rank], both[:, rank:])
        live = meta_ref[1 + FIELDS * k + 1]
        for n, (begun, count, column, prod, _) in enumerate(results):
            def run(n=n, begun=begun, count=count, column=column, prod=prod):
                base = 0
                for b in range(begun, begun + count - 1):
                    base = base + jnp.where(b < k, chunks_of(meta_ref, b), 0)
                at = pl.ds(pl.multiple_of(base * CHUNK, CHUNK), block_len)
                for c in range(0, prod.shape[1], TILE):
                    cols = slice(column + c, column + c + TILE)
                    term = jnp.dot(reduced, map_ref[0, :, cols], preferred_element_type=jnp.float32)
                    prods = result_refs[2 * n][at, c:c + TILE].astype(jnp.float32)
                    acts = result_refs[2 * n + 1][at, c:c + TILE].astype(jnp.float32)
                    sum_of = prods + acts * (lowrank_scale * term)
                    shown = lax.broadcasted_iota(jnp.int32, sum_of.shape, 0) < live
                    out_ref[:, cols] = jnp.where(shown, sum_of, 0.0).astype(jnp.bfloat16)

            pl.when(jnp.logical_and(k >= begun, k < begun + count))(run)

    vmem_spec = pl.BlockSpec(memory_space=pltpu.VMEM)
    return pl.pallas_call(
        kernel,
        grid_spec=pltpu.PrefetchScalarGridSpec(
            num_scalar_prefetch=1,
            grid=(total_blocks,),
            in_specs=[vmem_spec, vmem_spec, pl.BlockSpec((1, rank, columns), lambda k, m: (m[1 + FIELDS * k + 3], 0, 0))]
            + [vmem_spec] * n_flat,
            out_specs=pl.BlockSpec((block_len, columns), lambda k, m: (m[1 + FIELDS * k], 0)),
        ),
        out_shape=jax.ShapeDtypeStruct((row_total, columns), jnp.bfloat16),
        compiler_params=pltpu.CompilerParams(dimension_semantics=("arbitrary",), vmem_limit_bytes=16 * 1024 * 1024),
        cost_estimate=pl.CostEstimate(
            flops=2 * row_total * columns * 256, bytes_accessed=6 * row_total * columns, transcendentals=0),
    )(meta, mine, other, lowrank_up, *flat)


def on_ring(tokens, gate_matrix, up_matrix, lowrank_down, lowrank_up, tenant, adapter_storage_slot, live_count):
    block_count = tenant.shape[0]
    rows_here, width = tokens.shape
    chips = block_count
    block_len = 2 * rows_here
    row_total = block_count * block_len
    columns = gate_matrix.shape[1]
    me = lax.axis_index("tensor")
    core = lax.rem(me, 2)
    chip = me // 2
    place = jnp.where(lax.rem(chip, 2) == 0, chip // 2, chips - 1 - chip // 2)
    order = jnp.array([0, -1, 1, -2, 2, -3, 3, -4], jnp.int32)
    at = lax.rem(place + order + chips, chips)
    numbers = jnp.where(at < chips // 2, 2 * at, 2 * (chips - 1 - at) + 1)
    slots = adapter_storage_slot[tenant][numbers]
    here = (slots == me).astype(jnp.int32)
    fields = jnp.stack([numbers, live_count[numbers], here, slots], axis=1).astype(jnp.int32)
    meta = jnp.concatenate([core[None].astype(jnp.int32), fields.reshape(-1)])

    right, left = ring_pairs(chips, 1), ring_pairs(chips, -1)

    def send(value, pairs):
        return lax.ppermute(value, "tensor", pairs)

    def flip(value, bits):
        return lax.ppermute(value, "tensor", [(d, d ^ bits) for d in range(2 * chips)])

    down = lowrank_down[0]
    weights = (gate_matrix, up_matrix)
    n_tiles = columns // TILE
    from_left, from_right = tokens, tokens
    blocks = [[(tokens, False, 0), (flip(tokens, 1), True, 0)]]
    owned = []
    results = []
    first = 0
    for step in range(3):
        from_left = send(from_left, right)
        from_right = send(from_right, left)
        prod, act, part = pass_call(meta, first, blocks, down, *weights, 0, n_tiles, block_len, True, 0.0)
        results.append((first, len(blocks), 0, prod, act))
        owned.append(part)
        first += len(blocks)
        from_left, from_right = after_call((from_left, from_right), part)
        blocks = [[(v, False, 0), (flip(v, 1), True, 0)] for v in (from_left, from_right)]
    cut = rows_here // 2
    last_low = send(from_left[:cut], right)
    last_high = send(from_right[cut:], left)
    tiles, (prod, act, part) = tile_call(
        meta, first, blocks, down, *weights, {}, range(KEPT), range(KEPT), block_len, True, 0.0)
    results.append((first, 2, 0, prod, act))
    owned.append(part)
    last_low, last_high = after_call((last_low, last_high), part)
    blocks.append([
        (last_low, False, 0), (flip(last_low, 1), True, 0),
        (last_high, False, cut), (flip(last_high, 1), True, cut),
    ])
    mine, other = table_call(meta, first + 2, blocks[2], down, owned, row_total, block_len)
    more = range(KEPT, KEPT + FETCHED)
    tiles, (prod, act) = tile_call(
        meta, first + 2, blocks[2:], down, *weights, tiles, more, range(KEPT), block_len, False, 1.0)
    results.append((first + 2, 1, 0, prod, act))
    mine = add_call([mine, flip(other, 1), flip(mine, 2), flip(other, 3)], prod)
    met = [mine] + [flip(mine, 4 * k) for k in range(1, chips // 2)]
    _, (prod, act) = tile_call(
        meta, first, blocks, down, *weights, {t: tiles[t] for t in more}, range(KEPT + FETCHED, n_tiles),
        range(KEPT, n_tiles), block_len, False, 1.0, False)
    results.append((first, 3, KEPT * TILE, prod, act))
    mine = add_call(met, prod)
    other = flip(mine, 1)
    return finish_call(meta, mine, other, lowrank_up, results, row_total, block_len)


def on_device(
    tokens,
    gate_matrix,
    up_matrix,
    lowrank_down,
    lowrank_up,
    tenant,
    adapter_storage_slot,
    live_count,
):
    my_index = lax.axis_index("tensor")
    gathered = lax.all_gather(tokens, "tensor", axis=0, tiled=True)
    row_total = gathered.shape[0]
    width = gathered.shape[1]
    block_count = tenant.shape[0]
    block_len = row_total // block_count
    hidden_columns = gate_matrix.shape[1]
    gate_out = jnp.dot(gathered, gate_matrix, preferred_element_type=jnp.float32)
    up_output = jnp.dot(gathered, up_matrix, preferred_element_type=jnp.float32)
    slot_numbers = adapter_storage_slot[tenant]
    rows_block = gathered.reshape(block_count, block_len, width)
    per_replica = lowrank_down.shape[0]
    rank_width = lowrank_down.shape[1]
    first_slot = my_index * per_replica
    pieces = []
    for block in range(block_count):
        slot_here = slot_numbers[block]
        mine = jnp.logical_and(slot_here >= first_slot, slot_here < first_slot + per_replica)
        resident_slot = jnp.clip(slot_here - first_slot, 0, per_replica - 1)
        down_matrix = lax.dynamic_index_in_dim(lowrank_down, resident_slot, 0, keepdims=False)
        block_rows = rows_block[block]

        def product_fn(rows_in=block_rows, map_in=down_matrix):
            return lax.dot_general(
                rows_in, map_in, (((1,), (1,)), ((), ())), preferred_element_type=jnp.float32
            )

        def empty_fn():
            return jnp.zeros((block_len, rank_width), jnp.float32)

        pieces.append(lax.cond(mine, product_fn, empty_fn))
    partial_value = jnp.stack(pieces, axis=0)
    reduced_output = lax.psum(partial_value, "tensor").astype(jnp.bfloat16)
    every_slot = jnp.arange(lowrank_up.shape[0], dtype=jnp.int32)
    slot_indicator = (slot_numbers[:, None] == every_slot[None, :]).astype(jnp.bfloat16)
    adapter_up = jnp.einsum(
        "oe,exz->oxz", slot_indicator, lowrank_up, preferred_element_type=jnp.float32
    ).astype(jnp.bfloat16)
    lowrank_term = jnp.einsum(
        "who,wok->whk", reduced_output, adapter_up, preferred_element_type=jnp.float32
    )
    up_output = up_output + lowrank_scale * lowrank_term.reshape(row_total, hidden_columns)
    positions = jnp.arange(block_len, dtype=jnp.int32)
    live_rows = (positions[None, :] < live_count[:, None]).reshape(row_total, 1)
    hidden = jnp.where(live_rows, jax.nn.silu(gate_out) * up_output, 0.0)
    return hidden.astype(jnp.bfloat16)


def solution(mesh):
    placed = (
        P(("groups", "tensor"), None),
        P(None, "tensor"),
        P(None, "tensor"),
        P("tensor", None, None),
        P(None, None, "tensor"),
        P("groups"),
        P(),
        P("groups"),
    )
    run = on_ring if mesh.shape["tensor"] == 16 else on_device
    return jax.shard_map(
        run, mesh=mesh, in_specs=placed, out_specs=P("groups", "tensor"), check_vma=False
    )
```

```python
import jax
import jax.numpy as jnp
from jax import lax
from jax.experimental import pallas as pl
from jax.experimental.pallas import tpu as pltpu
from jax.sharding import PartitionSpec as P

lowrank_scale = 2.0
TILE = 256
CHUNK = 16
KEPT = 4
FETCHED = 0
VMEM_LIMIT = 36 * 1024 * 1024


def chip_at(place, chips):
    half = chips // 2
    if place < half:
        return 2 * place
    return 2 * (chips - 1 - place) + 1


def ring_pairs(chips, step):
    pairs = []
    for place in range(chips):
        for core in range(2):
            pairs.append((2 * chip_at(place, chips) + core, 2 * chip_at((place + step) % chips, chips) + core))
    return pairs


FIELDS = 4


def chunks_of(meta_ref, block):
    return (meta_ref[1 + FIELDS * block + 1] + CHUNK - 1) // CHUNK


def packed_copies(meta_ref, first, places, piece_refs, held, sems, half):
    core = meta_ref[0]
    made = []
    at = 0
    for k, (number, sibling, offset, length) in enumerate(places):
        base = 0
        for before in range(number):
            base = base + chunks_of(meta_ref, first + before)
        live = chunks_of(meta_ref, first + number)
        side = (1 - core) if sibling else core
        for i in range(length // CHUNK):
            chunk = side * (half // CHUNK) + offset // CHUNK + i
            row = pl.multiple_of((base + chunk) * CHUNK, CHUNK)
            copy = pltpu.make_async_copy(
                piece_refs[k].at[pl.ds(i * CHUNK, CHUNK)], held.at[pl.ds(jnp.minimum(row, held.shape[0] - CHUNK), CHUNK)], sems.at[at])
            made.append((chunk < live, copy))
            at += 1
    return made


def flatten(blocks):
    flat, places = [], []
    for number, pieces in enumerate(blocks):
        for piece, sibling, offset in pieces:
            places.append((number, sibling, offset, piece.shape[0]))
            flat.append(piece)
    return flat, places


def pass_call(meta, first, blocks, down, gate_matrix, up_matrix, first_tile, tiles, block_len, want_reduced, share, after=()):
    width = gate_matrix.shape[0]
    rank = down.shape[0]
    count = len(blocks)
    rows = count * block_len
    half = block_len // 2
    flat, places = flatten(blocks)
    n_pieces = len(flat)
    n_copies = rows // CHUNK
    sizes = [m for m in range(block_len, rows + 1, block_len // 2)]

    def kernel(*refs):
        meta_ref = refs[0]
        piece_refs = refs[1:1 + n_pieces]
        rest = refs[1 + n_pieces:]
        if want_reduced:
            down_ref = rest[0]
            rest = rest[1:]
        gate_ref, up_ref = rest[:2]
        prod_ref, act_ref = rest[2 + len(after):4 + len(after)]
        rest = rest[4 + len(after):]
        if want_reduced:
            reduced_ref, held, in_sem, found_ref = rest
        else:
            held, in_sem = rest
        total = 0
        for b in range(count):
            total = total + chunks_of(meta_ref, first + b)
        used = total * CHUNK

        @pl.when(pl.program_id(0) == 0)
        def _():
            copies = packed_copies(meta_ref, first, places, piece_refs, held, in_sem, half)
            for live, copy in copies:
                pl.when(live)(copy.start)
            for live, copy in copies:
                pl.when(live)(copy.wait)
            if want_reduced:
                found_ref[...] = lax.dot_general(
                    held[...], down_ref[...], (((1,), (1,)), ((), ())), preferred_element_type=jnp.float32)
                base = 0
                for b in range(count):
                    row = pl.multiple_of(base * CHUNK, CHUNK)
                    part = found_ref[pl.ds(row, block_len), :]
                    mine = meta_ref[1 + FIELDS * (first + b) + 2] == 1
                    reduced_ref[b * block_len:(b + 1) * block_len, :] = jnp.where(mine, part, 0.0).astype(jnp.bfloat16)
                    base = base + chunks_of(meta_ref, first + b)

        below = 0
        for size in sizes:
            def run(size=size):
                rows_in = held[:size, :]
                gate_out = jnp.dot(rows_in, gate_ref[...], preferred_element_type=jnp.float32)
                up_out = jnp.dot(rows_in, up_ref[...], preferred_element_type=jnp.float32)
                act = gate_out * (0.5 * jnp.tanh(0.5 * gate_out) + 0.5)
                act_ref[:size, :] = act.astype(jnp.bfloat16)
                prod_ref[:size, :] = (act * up_out).astype(jnp.bfloat16)

            pl.when(jnp.logical_and(used > below, used <= size))(run)
            below = size

    weight_spec = pl.BlockSpec((width, TILE), lambda j, m: (0, first_tile + j))
    any_spec = pl.BlockSpec(memory_space=pl.ANY)
    in_specs = [any_spec] * n_pieces
    operands = [meta] + flat
    if want_reduced:
        in_specs.append(pl.BlockSpec((rank, width), lambda j, m: (0, 0)))
        operands.append(down)
    in_specs += [weight_spec, weight_spec] + [any_spec] * len(after)
    operands += [gate_matrix, up_matrix] + list(after)
    out_specs = [pl.BlockSpec((rows, TILE), lambda j, m: (0, j))] * 2
    out_shape = [jax.ShapeDtypeStruct((rows, tiles * TILE), jnp.bfloat16)] * 2
    scratch = [pltpu.VMEM((rows, width), jnp.bfloat16), pltpu.SemaphoreType.DMA((n_copies,))]
    if want_reduced:
        out_specs.append(pl.BlockSpec((rows, rank), lambda j, m: (0, 0)))
        out_shape.append(jax.ShapeDtypeStruct((rows, rank), jnp.bfloat16))
        scratch.append(pltpu.VMEM((rows, rank), jnp.float32))
    return pl.pallas_call(
        kernel,
        grid_spec=pltpu.PrefetchScalarGridSpec(
            num_scalar_prefetch=1, grid=(tiles,), in_specs=in_specs, out_specs=out_specs, scratch_shapes=scratch),
        out_shape=out_shape,
        compiler_params=pltpu.CompilerParams(dimension_semantics=("arbitrary",), vmem_limit_bytes=VMEM_LIMIT),
        cost_estimate=pl.CostEstimate(
            flops=int(share * 4 * rows * width * TILE * tiles),
            bytes_accessed=1024 + int(share * 4 * width * TILE * tiles), transcendentals=0),
    )(*operands)


def tile_call(meta, first, blocks, down, gate_matrix, up_matrix, given, fetch, compute, block_len, want_reduced, share, keep=True):
    width = gate_matrix.shape[0]
    rank = down.shape[0]
    count = len(blocks)
    rows = count * block_len
    half = block_len // 2
    flat, places = flatten(blocks)
    n_pieces = len(flat)
    n_copies = rows // CHUNK
    row_blocks = [slice(m, m + block_len) for m in range(0, rows, block_len)]
    held_tiles = list(given)
    order = held_tiles + list(fetch)
    n_given = 2 * len(held_tiles)
    n_out = 2 * len(order) if keep else n_given

    def kernel(*refs):
        meta_ref = refs[0]
        piece_refs = refs[1:1 + n_pieces]
        rest = refs[1 + n_pieces:]
        if want_reduced:
            down_ref = rest[0]
            rest = rest[1:]
        gate_ref, up_ref = rest[:2]
        rest = rest[2 + n_given:]
        tile_refs = list(rest[:n_out])
        prod_ref, act_ref = rest[n_out:n_out + 2]
        rest = rest[n_out + 2:]
        if not keep:
            tile_refs += rest[-2 * len(fetch):]
            rest = rest[:-2 * len(fetch)]
        if want_reduced:
            reduced_ref, held, in_sem, tile_sem, found_ref = rest
        else:
            held, in_sem, tile_sem = rest
        copies = packed_copies(meta_ref, first, places, piece_refs, held, in_sem, half)
        for live, copy in copies:
            pl.when(live)(copy.start)
        loads = {}
        for n, t in enumerate(fetch):
            at = len(held_tiles) + n
            loads[t] = [
                pltpu.make_async_copy(ref.at[:, t * TILE:(t + 1) * TILE], tile_refs[2 * at + side], tile_sem.at[2 * n + side])
                for side, ref in enumerate((gate_ref, up_ref))
            ]
            for load in loads[t]:
                load.start()
        total = 0
        for b in range(count):
            total = total + chunks_of(meta_ref, first + b)
        used = total * CHUNK
        for live, copy in copies:
            pl.when(live)(copy.wait)
        if want_reduced:
            found_ref[...] = lax.dot_general(
                held[...], down_ref[...], (((1,), (1,)), ((), ())), preferred_element_type=jnp.float32)
            base = 0
            for b in range(count):
                row = pl.multiple_of(base * CHUNK, CHUNK)
                part = found_ref[pl.ds(row, block_len), :]
                mine = meta_ref[1 + FIELDS * (first + b) + 2] == 1
                reduced_ref[b * block_len:(b + 1) * block_len, :] = jnp.where(mine, part, 0.0).astype(jnp.bfloat16)
                base = base + chunks_of(meta_ref, first + b)
        for n, t in enumerate(compute):
            for load in loads.pop(t, []):
                load.wait()
            at = order.index(t)
            cols = slice(n * TILE, (n + 1) * TILE)
            for some in row_blocks:
                def run(some=some, at=at, cols=cols):
                    rows_in = held[some, :]
                    gate_out = jnp.dot(rows_in, tile_refs[2 * at][...], preferred_element_type=jnp.float32)
                    up_out = jnp.dot(rows_in, tile_refs[2 * at + 1][...], preferred_element_type=jnp.float32)
                    act = gate_out * (0.5 * jnp.tanh(0.5 * gate_out) + 0.5)
                    act_ref[some, cols] = act.astype(jnp.bfloat16)
                    prod_ref[some, cols] = (act * up_out).astype(jnp.bfloat16)

                pl.when(used > some.start)(run)
        for t in list(loads):
            for load in loads[t]:
                load.wait()

    any_spec = pl.BlockSpec(memory_space=pl.ANY)
    vmem_spec = pl.BlockSpec(memory_space=pltpu.VMEM)
    in_specs = [any_spec] * n_pieces
    operands = [meta] + flat
    if want_reduced:
        in_specs.append(vmem_spec)
        operands.append(down)
    in_specs += [any_spec, any_spec] + [vmem_spec] * n_given
    operands += [gate_matrix, up_matrix]
    aliases = {len(operands) + k: k for k in range(n_given)}
    for t in held_tiles:
        operands += list(given[t])
    result = jax.ShapeDtypeStruct((rows, len(compute) * TILE), jnp.bfloat16)
    out_shape = [pltpu.VMEM((width, TILE), jnp.bfloat16)] * n_out + [result, result]
    scratch = [
        pltpu.VMEM((rows, width), jnp.bfloat16),
        pltpu.SemaphoreType.DMA((n_copies,)),
        pltpu.SemaphoreType.DMA((max(1, 2 * len(fetch)),)),
    ]
    if want_reduced:
        out_shape.append(jax.ShapeDtypeStruct((rows, rank), jnp.bfloat16))
        scratch.append(pltpu.VMEM((rows, rank), jnp.float32))
    limit = rows * 20 * 1024 + 2 * 1024 * 1024
    if not keep:
        scratch += [pltpu.VMEM((width, TILE), jnp.bfloat16)] * (2 * len(fetch))
        limit += 4 * width * TILE * len(fetch)
    out = pl.pallas_call(
        kernel,
        grid_spec=pltpu.PrefetchScalarGridSpec(
            num_scalar_prefetch=1, grid=(1,), in_specs=in_specs, out_specs=[vmem_spec] * len(out_shape), scratch_shapes=scratch),
        out_shape=out_shape,
        input_output_aliases=aliases,
        compiler_params=pltpu.CompilerParams(dimension_semantics=("arbitrary",), vmem_limit_bytes=limit),
        cost_estimate=pl.CostEstimate(
            flops=int(share * 4 * rows * width * TILE * len(compute)),
            bytes_accessed=1024 + int(share * 4 * width * TILE * len(compute)), transcendentals=0),
    )(*operands)
    tiles = {t: (out[2 * n], out[2 * n + 1]) for n, t in enumerate(order[:n_out // 2])}
    return tiles, out[n_out:]


def after_call(values, other):
    any_spec = pl.BlockSpec(memory_space=pl.ANY)

    def kernel(*refs):
        pass

    return pl.pallas_call(
        kernel,
        in_specs=[any_spec] * (len(values) + 1),
        out_specs=[any_spec] * len(values),
        out_shape=[jax.ShapeDtypeStruct(v.shape, v.dtype) for v in values],
        input_output_aliases={k: k for k in range(len(values))},
        compiler_params=pltpu.CompilerParams(vmem_limit_bytes=1024 * 1024),
        cost_estimate=pl.CostEstimate(flops=0, bytes_accessed=0, transcendentals=0),
    )(*values, other)


def quarter_of(block, row_total, block_len):
    per_quarter = row_total // block_len // 4
    quarter = block // per_quarter
    return quarter, pl.multiple_of((block - quarter * per_quarter) * block_len, block_len)


def table_call(meta, number, pieces, down, owned, row_total, block_len):
    rank, width = down.shape
    half = block_len // 2
    flat, places = flatten([pieces])
    n_pieces = len(flat)
    n_owned = len(owned)

    def kernel(*refs):
        meta_ref = refs[0]
        piece_refs = refs[1:1 + n_pieces]
        down_ref = refs[1 + n_pieces]
        owned_refs = refs[2 + n_pieces:2 + n_pieces + n_owned]
        mine_ref, other_ref, held, in_sem = refs[2 + n_pieces + n_owned:]
        core = meta_ref[0]
        copies = []
        for k, (_, sibling, offset, length) in enumerate(places):
            side = (1 - core) if sibling else core
            row = pl.multiple_of(side * half + offset, 32)
            copies.append(pltpu.make_async_copy(piece_refs[k], held.at[pl.ds(row, length)], in_sem.at[k]))
        for copy in copies:
            copy.start()

        def put(at, value):
            quarter, row = quarter_of(meta_ref[1 + FIELDS * at], row_total, block_len)
            for q in range(4):
                @pl.when(quarter == q)
                def _(q=q):
                    lanes = slice(q % 2 * rank, (q % 2 + 1) * rank)

                    @pl.when(core == q // 2)
                    def _():
                        mine_ref[pl.ds(row, block_len), lanes] = value

                    @pl.when(core != q // 2)
                    def _():
                        other_ref[pl.ds(row, block_len), lanes] = value

        at = 0
        for ref in owned_refs:
            for b in range(ref.shape[0] // block_len):
                put(at, ref[b * block_len:(b + 1) * block_len, :])
                at += 1
        for copy in copies:
            copy.wait()
        found = lax.dot_general(held[...], down_ref[...], (((1,), (1,)), ((), ())), preferred_element_type=jnp.float32)
        put(number, jnp.where(meta_ref[1 + FIELDS * number + 2] == 1, found, 0.0).astype(jnp.bfloat16))

    whole = pl.BlockSpec(memory_space=pltpu.VMEM)
    return pl.pallas_call(
        kernel,
        in_specs=[pl.BlockSpec(memory_space=pltpu.SMEM)] + [pl.BlockSpec(memory_space=pl.ANY)] * n_pieces + [whole] * (1 + n_owned),
        out_specs=[whole] * 2,
        out_shape=[jax.ShapeDtypeStruct((row_total // 4, 2 * rank), jnp.bfloat16)] * 2,
        scratch_shapes=[pltpu.VMEM((block_len, width), jnp.bfloat16), pltpu.SemaphoreType.DMA((n_pieces,))],
        compiler_params=pltpu.CompilerParams(vmem_limit_bytes=8 * 1024 * 1024),
        cost_estimate=pl.CostEstimate(flops=0, bytes_accessed=1024 * 1024, transcendentals=0),
    )(meta, *flat, down, *owned)


def add_call(values, other):
    vmem_spec = pl.BlockSpec(memory_space=pltpu.VMEM)

    def kernel(*refs):
        total = refs[0][...]
        for ref in refs[1:len(values)]:
            total = total + ref[...]
        refs[-1][...] = total

    return pl.pallas_call(
        kernel,
        in_specs=[vmem_spec] * len(values) + [pl.BlockSpec(memory_space=pl.ANY)],
        out_specs=vmem_spec,
        out_shape=jax.ShapeDtypeStruct(values[0].shape, values[0].dtype),
        compiler_params=pltpu.CompilerParams(vmem_limit_bytes=2 * 1024 * 1024),
        cost_estimate=pl.CostEstimate(flops=0, bytes_accessed=1024, transcendentals=0),
    )(*values, other)


def finish_call(meta, mine, other, lowrank_up, results, row_total, block_len):
    rank, columns = lowrank_up.shape[1:]
    total_blocks = row_total // block_len
    flat = []
    for result in results:
        flat += result[3:]
    n_flat = len(flat)

    def kernel(*refs):
        meta_ref, mine_ref, other_ref, map_ref = refs[:4]
        result_refs = refs[4:4 + n_flat]
        out_ref = refs[4 + n_flat]
        k = pl.program_id(0)
        quarter, row = quarter_of(meta_ref[1 + FIELDS * k], row_total, block_len)
        at_row = pl.ds(row, block_len)
        both = jnp.where(quarter // 2 == meta_ref[0], mine_ref[at_row, :], other_ref[at_row, :])
        reduced = jnp.where(lax.rem(quarter, 2) == 0, both[:, :rank], both[:, rank:])
        live = meta_ref[1 + FIELDS * k + 1]
        for n, (begun, count, column, prod, _) in enumerate(results):
            def run(n=n, begun=begun, count=count, column=column, prod=prod):
                base = 0
                for b in range(begun, begun + count - 1):
                    base = base + jnp.where(b < k, chunks_of(meta_ref, b), 0)
                at = pl.ds(pl.multiple_of(base * CHUNK, CHUNK), block_len)
                for c in range(0, prod.shape[1], TILE):
                    cols = slice(column + c, column + c + TILE)
                    term = jnp.dot(reduced, map_ref[0, :, cols], preferred_element_type=jnp.float32)
                    prods = result_refs[2 * n][at, c:c + TILE].astype(jnp.float32)
                    acts = result_refs[2 * n + 1][at, c:c + TILE].astype(jnp.float32)
                    sum_of = prods + acts * (lowrank_scale * term)
                    shown = lax.broadcasted_iota(jnp.int32, sum_of.shape, 0) < live
                    out_ref[:, cols] = jnp.where(shown, sum_of, 0.0).astype(jnp.bfloat16)

            pl.when(jnp.logical_and(k >= begun, k < begun + count))(run)

    vmem_spec = pl.BlockSpec(memory_space=pltpu.VMEM)
    return pl.pallas_call(
        kernel,
        grid_spec=pltpu.PrefetchScalarGridSpec(
            num_scalar_prefetch=1,
            grid=(total_blocks,),
            in_specs=[vmem_spec, vmem_spec, pl.BlockSpec((1, rank, columns), lambda k, m: (m[1 + FIELDS * k + 3], 0, 0))]
            + [vmem_spec] * n_flat,
            out_specs=pl.BlockSpec((block_len, columns), lambda k, m: (m[1 + FIELDS * k], 0)),
        ),
        out_shape=jax.ShapeDtypeStruct((row_total, columns), jnp.bfloat16),
        compiler_params=pltpu.CompilerParams(dimension_semantics=("arbitrary",), vmem_limit_bytes=16 * 1024 * 1024),
        cost_estimate=pl.CostEstimate(
            flops=2 * row_total * columns * 256, bytes_accessed=6 * row_total * columns, transcendentals=0),
    )(meta, mine, other, lowrank_up, *flat)


def on_ring(tokens, gate_matrix, up_matrix, lowrank_down, lowrank_up, tenant, adapter_storage_slot, live_count):
    block_count = tenant.shape[0]
    rows_here, width = tokens.shape
    chips = block_count
    block_len = 2 * rows_here
    row_total = block_count * block_len
    columns = gate_matrix.shape[1]
    me = lax.axis_index("tensor")
    core = lax.rem(me, 2)
    chip = me // 2
    place = jnp.where(lax.rem(chip, 2) == 0, chip // 2, chips - 1 - chip // 2)
    count = lax.iota(jnp.int32, block_count)
    order = jnp.where(lax.rem(count, 2) == 1, -(count + 1) // 2, count // 2)
    at = lax.rem(place + order + chips, chips)
    numbers = jnp.where(at < chips // 2, 2 * at, 2 * (chips - 1 - at) + 1)

    def pick(values, index):
        chosen = index[:, None] == lax.broadcasted_iota(jnp.int32, (index.shape[0], values.shape[0]), 1)
        return jnp.sum(jnp.where(chosen, values[None, :], 0), axis=1)

    slots = pick(adapter_storage_slot, pick(tenant, numbers))
    here = (slots == me).astype(jnp.int32)
    fields = jnp.stack([numbers, pick(live_count, numbers), here, slots], axis=1).astype(jnp.int32)
    meta = jnp.concatenate([core[None].astype(jnp.int32), fields.reshape(-1)])

    right, left = ring_pairs(chips, 1), ring_pairs(chips, -1)

    def send(value, pairs):
        return lax.ppermute(value, "tensor", pairs)

    def flip(value, bits):
        return lax.ppermute(value, "tensor", [(d, d ^ bits) for d in range(2 * chips)])

    down = lowrank_down[0]
    weights = (gate_matrix, up_matrix)
    n_tiles = columns // TILE
    from_left, from_right = tokens, tokens
    blocks = [[(tokens, False, 0), (flip(tokens, 1), True, 0)]]
    owned = []
    results = []
    first = 0
    for step in range(3):
        from_left = send(from_left, right)
        from_right = send(from_right, left)
        prod, act, part = pass_call(meta, first, blocks, down, *weights, 0, n_tiles, block_len, True, 0.0)
        results.append((first, len(blocks), 0, prod, act))
        owned.append(part)
        first += len(blocks)
        from_left, from_right = after_call((from_left, from_right), part)
        blocks = [[(v, False, 0), (flip(v, 1), True, 0)] for v in (from_left, from_right)]
    cut = rows_here // 2
    last_low = send(from_left[:cut], right)
    last_high = send(from_right[cut:], left)
    tiles, (prod, act, part) = tile_call(
        meta, first, blocks, down, *weights, {}, range(KEPT), range(KEPT), block_len, True, 0.0)
    results.append((first, 2, 0, prod, act))
    owned.append(part)
    last_low, last_high = after_call((last_low, last_high), part)
    blocks.append([
        (last_low, False, 0), (flip(last_low, 1), True, 0),
        (last_high, False, cut), (flip(last_high, 1), True, cut),
    ])
    mine, other = table_call(meta, first + 2, blocks[2], down, owned, row_total, block_len)
    more = range(KEPT, KEPT + FETCHED)
    tiles, (prod, act) = tile_call(
        meta, first + 2, blocks[2:], down, *weights, tiles, more, range(KEPT), block_len, False, 1.0)
    results.append((first + 2, 1, 0, prod, act))
    mine = add_call([mine, flip(other, 1), flip(mine, 2), flip(other, 3)], prod)
    met = [mine] + [flip(mine, 4 * k) for k in range(1, chips // 2)]
    _, (prod, act) = tile_call(
        meta, first, blocks, down, *weights, {t: tiles[t] for t in more}, range(KEPT + FETCHED, n_tiles),
        range(KEPT, n_tiles), block_len, False, 1.0, False)
    results.append((first, 3, KEPT * TILE, prod, act))
    mine = add_call(met, prod)
    other = flip(mine, 1)
    return finish_call(meta, mine, other, lowrank_up, results, row_total, block_len)


def on_device(
    tokens,
    gate_matrix,
    up_matrix,
    lowrank_down,
    lowrank_up,
    tenant,
    adapter_storage_slot,
    live_count,
):
    my_index = lax.axis_index("tensor")
    gathered = lax.all_gather(tokens, "tensor", axis=0, tiled=True)
    row_total = gathered.shape[0]
    width = gathered.shape[1]
    block_count = tenant.shape[0]
    block_len = row_total // block_count
    hidden_columns = gate_matrix.shape[1]
    gate_out = jnp.dot(gathered, gate_matrix, preferred_element_type=jnp.float32)
    up_output = jnp.dot(gathered, up_matrix, preferred_element_type=jnp.float32)
    slot_numbers = adapter_storage_slot[tenant]
    rows_block = gathered.reshape(block_count, block_len, width)
    per_replica = lowrank_down.shape[0]
    rank_width = lowrank_down.shape[1]
    first_slot = my_index * per_replica
    pieces = []
    for block in range(block_count):
        slot_here = slot_numbers[block]
        mine = jnp.logical_and(slot_here >= first_slot, slot_here < first_slot + per_replica)
        resident_slot = jnp.clip(slot_here - first_slot, 0, per_replica - 1)
        down_matrix = lax.dynamic_index_in_dim(lowrank_down, resident_slot, 0, keepdims=False)
        block_rows = rows_block[block]

        def product_fn(rows_in=block_rows, map_in=down_matrix):
            return lax.dot_general(
                rows_in, map_in, (((1,), (1,)), ((), ())), preferred_element_type=jnp.float32
            )

        def empty_fn():
            return jnp.zeros((block_len, rank_width), jnp.float32)

        pieces.append(lax.cond(mine, product_fn, empty_fn))
    partial_value = jnp.stack(pieces, axis=0)
    reduced_output = lax.psum(partial_value, "tensor").astype(jnp.bfloat16)
    every_slot = jnp.arange(lowrank_up.shape[0], dtype=jnp.int32)
    slot_indicator = (slot_numbers[:, None] == every_slot[None, :]).astype(jnp.bfloat16)
    adapter_up = jnp.einsum(
        "oe,exz->oxz", slot_indicator, lowrank_up, preferred_element_type=jnp.float32
    ).astype(jnp.bfloat16)
    lowrank_term = jnp.einsum(
        "who,wok->whk", reduced_output, adapter_up, preferred_element_type=jnp.float32
    )
    up_output = up_output + lowrank_scale * lowrank_term.reshape(row_total, hidden_columns)
    positions = jnp.arange(block_len, dtype=jnp.int32)
    live_rows = (positions[None, :] < live_count[:, None]).reshape(row_total, 1)
    hidden = jnp.where(live_rows, jax.nn.silu(gate_out) * up_output, 0.0)
    return hidden.astype(jnp.bfloat16)


def solution(mesh):
    placed = (
        P(("groups", "tensor"), None),
        P(None, "tensor"),
        P(None, "tensor"),
        P("tensor", None, None),
        P(None, None, "tensor"),
        P("groups"),
        P(),
        P("groups"),
    )
    run = on_ring if mesh.shape["tensor"] == 16 else on_device
    return jax.shard_map(
        run, mesh=mesh, in_specs=placed, out_specs=P("groups", "tensor"), check_vma=False
    )
```

```python
import jax
import jax.numpy as jnp
from jax import lax
from jax.experimental import pallas as pl
from jax.experimental.pallas import tpu as pltpu
from jax.sharding import PartitionSpec as P

lowrank_scale = 2.0
TILE = 256
CHUNK = 16
KEPT = 4
FETCHED = 1
VMEM_LIMIT = 36 * 1024 * 1024


def chip_at(place, chips):
    half = chips // 2
    if place < half:
        return 2 * place
    return 2 * (chips - 1 - place) + 1


def ring_pairs(chips, step):
    pairs = []
    for place in range(chips):
        for core in range(2):
            pairs.append((2 * chip_at(place, chips) + core, 2 * chip_at((place + step) % chips, chips) + core))
    return pairs


FIELDS = 4


def chunks_of(meta_ref, block):
    return (meta_ref[1 + FIELDS * block + 1] + CHUNK - 1) // CHUNK


def packed_copies(meta_ref, first, places, piece_refs, held, sems, half):
    core = meta_ref[0]
    made = []
    at = 0
    for k, (number, sibling, offset, length) in enumerate(places):
        base = 0
        for before in range(number):
            base = base + chunks_of(meta_ref, first + before)
        live = chunks_of(meta_ref, first + number)
        side = (1 - core) if sibling else core
        for i in range(length // CHUNK):
            chunk = side * (half // CHUNK) + offset // CHUNK + i
            row = pl.multiple_of((base + chunk) * CHUNK, CHUNK)
            copy = pltpu.make_async_copy(
                piece_refs[k].at[pl.ds(i * CHUNK, CHUNK)], held.at[pl.ds(jnp.minimum(row, held.shape[0] - CHUNK), CHUNK)], sems.at[at])
            made.append((chunk < live, copy))
            at += 1
    return made


def flatten(blocks):
    flat, places = [], []
    for number, pieces in enumerate(blocks):
        for piece, sibling, offset in pieces:
            places.append((number, sibling, offset, piece.shape[0]))
            flat.append(piece)
    return flat, places


def pass_call(meta, first, blocks, down, gate_matrix, up_matrix, first_tile, tiles, block_len, want_reduced, share, after=()):
    width = gate_matrix.shape[0]
    rank = down.shape[0]
    count = len(blocks)
    rows = count * block_len
    half = block_len // 2
    flat, places = flatten(blocks)
    n_pieces = len(flat)
    n_copies = rows // CHUNK
    sizes = [m for m in range(block_len, rows + 1, block_len // 2)]

    def kernel(*refs):
        meta_ref = refs[0]
        piece_refs = refs[1:1 + n_pieces]
        rest = refs[1 + n_pieces:]
        if want_reduced:
            down_ref = rest[0]
            rest = rest[1:]
        gate_ref, up_ref = rest[:2]
        prod_ref, act_ref = rest[2 + len(after):4 + len(after)]
        rest = rest[4 + len(after):]
        if want_reduced:
            reduced_ref, held, in_sem, found_ref = rest
        else:
            held, in_sem = rest
        total = 0
        for b in range(count):
            total = total + chunks_of(meta_ref, first + b)
        used = total * CHUNK

        @pl.when(pl.program_id(0) == 0)
        def _():
            copies = packed_copies(meta_ref, first, places, piece_refs, held, in_sem, half)
            for live, copy in copies:
                pl.when(live)(copy.start)
            for live, copy in copies:
                pl.when(live)(copy.wait)
            if want_reduced:
                found_ref[...] = lax.dot_general(
                    held[...], down_ref[...], (((1,), (1,)), ((), ())), preferred_element_type=jnp.float32)
                base = 0
                for b in range(count):
                    row = pl.multiple_of(base * CHUNK, CHUNK)
                    part = found_ref[pl.ds(row, block_len), :]
                    mine = meta_ref[1 + FIELDS * (first + b) + 2] == 1
                    reduced_ref[b * block_len:(b + 1) * block_len, :] = jnp.where(mine, part, 0.0).astype(jnp.bfloat16)
                    base = base + chunks_of(meta_ref, first + b)

        below = 0
        for size in sizes:
            def run(size=size):
                rows_in = held[:size, :]
                gate_out = jnp.dot(rows_in, gate_ref[...], preferred_element_type=jnp.float32)
                up_out = jnp.dot(rows_in, up_ref[...], preferred_element_type=jnp.float32)
                act = gate_out * (0.5 * jnp.tanh(0.5 * gate_out) + 0.5)
                act_ref[:size, :] = act.astype(jnp.bfloat16)
                prod_ref[:size, :] = (act * up_out).astype(jnp.bfloat16)

            pl.when(jnp.logical_and(used > below, used <= size))(run)
            below = size

    weight_spec = pl.BlockSpec((width, TILE), lambda j, m: (0, first_tile + j))
    any_spec = pl.BlockSpec(memory_space=pl.ANY)
    in_specs = [any_spec] * n_pieces
    operands = [meta] + flat
    if want_reduced:
        in_specs.append(pl.BlockSpec((rank, width), lambda j, m: (0, 0)))
        operands.append(down)
    in_specs += [weight_spec, weight_spec] + [any_spec] * len(after)
    operands += [gate_matrix, up_matrix] + list(after)
    out_specs = [pl.BlockSpec((rows, TILE), lambda j, m: (0, j))] * 2
    out_shape = [jax.ShapeDtypeStruct((rows, tiles * TILE), jnp.bfloat16)] * 2
    scratch = [pltpu.VMEM((rows, width), jnp.bfloat16), pltpu.SemaphoreType.DMA((n_copies,))]
    if want_reduced:
        out_specs.append(pl.BlockSpec((rows, rank), lambda j, m: (0, 0)))
        out_shape.append(jax.ShapeDtypeStruct((rows, rank), jnp.bfloat16))
        scratch.append(pltpu.VMEM((rows, rank), jnp.float32))
    return pl.pallas_call(
        kernel,
        grid_spec=pltpu.PrefetchScalarGridSpec(
            num_scalar_prefetch=1, grid=(tiles,), in_specs=in_specs, out_specs=out_specs, scratch_shapes=scratch),
        out_shape=out_shape,
        compiler_params=pltpu.CompilerParams(dimension_semantics=("arbitrary",), vmem_limit_bytes=VMEM_LIMIT),
        cost_estimate=pl.CostEstimate(
            flops=int(share * 4 * rows * width * TILE * tiles),
            bytes_accessed=1024 + int(share * 4 * width * TILE * tiles), transcendentals=0),
    )(*operands)


def tile_call(meta, first, blocks, down, gate_matrix, up_matrix, given, fetch, compute, block_len, want_reduced, share, keep=True, reuse=()):
    width = gate_matrix.shape[0]
    rank = down.shape[0]
    count = len(blocks)
    rows = count * block_len
    half = block_len // 2
    flat, places = flatten(blocks)
    n_pieces = len(flat)
    n_copies = rows // CHUNK
    row_blocks = [slice(m, m + block_len) for m in range(0, rows, block_len)]
    held_tiles = list(given)
    order = held_tiles + list(fetch)
    n_given = 2 * len(held_tiles)
    n_out = 2 * len(order) if keep else n_given

    def kernel(*refs):
        meta_ref = refs[0]
        piece_refs = refs[1:1 + n_pieces]
        rest = refs[1 + n_pieces:]
        if want_reduced:
            down_ref = rest[0]
            rest = rest[1:]
        gate_ref, up_ref = rest[:2]
        rest = rest[2 + n_given:]
        tile_refs = list(rest[:n_out])
        prod_ref, act_ref = rest[n_out:n_out + 2]
        rest = rest[n_out + 2:]
        if not keep:
            tile_refs += rest[-2 * len(fetch):]
            rest = rest[:-2 * len(fetch)]
        if want_reduced:
            reduced_ref, held, in_sem, tile_sem, late_sem, found_ref = rest
        else:
            held, in_sem, tile_sem, late_sem = rest
        copies = packed_copies(meta_ref, first, places, piece_refs, held, in_sem, half)
        for live, copy in copies:
            pl.when(live)(copy.start)
        loads = {}
        for n, t in enumerate(fetch):
            at = len(held_tiles) + n
            loads[t] = [
                pltpu.make_async_copy(ref.at[:, t * TILE:(t + 1) * TILE], tile_refs[2 * at + side], tile_sem.at[2 * n + side])
                for side, ref in enumerate((gate_ref, up_ref))
            ]
            for load in loads[t]:
                load.start()
        total = 0
        for b in range(count):
            total = total + chunks_of(meta_ref, first + b)
        used = total * CHUNK
        for live, copy in copies:
            pl.when(live)(copy.wait)
        if want_reduced:
            found_ref[...] = lax.dot_general(
                held[...], down_ref[...], (((1,), (1,)), ((), ())), preferred_element_type=jnp.float32)
            base = 0
            for b in range(count):
                row = pl.multiple_of(base * CHUNK, CHUNK)
                part = found_ref[pl.ds(row, block_len), :]
                mine = meta_ref[1 + FIELDS * (first + b) + 2] == 1
                reduced_ref[b * block_len:(b + 1) * block_len, :] = jnp.where(mine, part, 0.0).astype(jnp.bfloat16)
                base = base + chunks_of(meta_ref, first + b)
        for n, t in enumerate(compute):
            for load in loads.pop(t, []):
                load.wait()
            at = reuse.index(t) if t in reuse else order.index(t)
            cols = slice(n * TILE, (n + 1) * TILE)
            for some in row_blocks:
                def run(some=some, at=at, cols=cols):
                    rows_in = held[some, :]
                    gate_out = jnp.dot(rows_in, tile_refs[2 * at][...], preferred_element_type=jnp.float32)
                    up_out = jnp.dot(rows_in, tile_refs[2 * at + 1][...], preferred_element_type=jnp.float32)
                    act = gate_out * (0.5 * jnp.tanh(0.5 * gate_out) + 0.5)
                    act_ref[some, cols] = act.astype(jnp.bfloat16)
                    prod_ref[some, cols] = (act * up_out).astype(jnp.bfloat16)

                pl.when(used > some.start)(run)
            if t not in reuse and at < len(reuse):
                later = reuse[at]
                loads[later] = [
                    pltpu.make_async_copy(
                        ref.at[:, later * TILE:(later + 1) * TILE], tile_refs[2 * at + side], late_sem.at[2 * at + side])
                    for side, ref in enumerate((gate_ref, up_ref))
                ]
                for load in loads[later]:
                    load.start()
        for t in list(loads):
            for load in loads[t]:
                load.wait()

    any_spec = pl.BlockSpec(memory_space=pl.ANY)
    vmem_spec = pl.BlockSpec(memory_space=pltpu.VMEM)
    in_specs = [any_spec] * n_pieces
    operands = [meta] + flat
    if want_reduced:
        in_specs.append(vmem_spec)
        operands.append(down)
    in_specs += [any_spec, any_spec] + [vmem_spec] * n_given
    operands += [gate_matrix, up_matrix]
    aliases = {len(operands) + k: k for k in range(n_given)}
    for t in held_tiles:
        operands += list(given[t])
    result = jax.ShapeDtypeStruct((rows, len(compute) * TILE), jnp.bfloat16)
    out_shape = [pltpu.VMEM((width, TILE), jnp.bfloat16)] * n_out + [result, result]
    scratch = [
        pltpu.VMEM((rows, width), jnp.bfloat16),
        pltpu.SemaphoreType.DMA((n_copies,)),
        pltpu.SemaphoreType.DMA((max(1, 2 * len(fetch)),)),
        pltpu.SemaphoreType.DMA((max(1, 2 * len(reuse)),)),
    ]
    if want_reduced:
        out_shape.append(jax.ShapeDtypeStruct((rows, rank), jnp.bfloat16))
        scratch.append(pltpu.VMEM((rows, rank), jnp.float32))
    limit = rows * 20 * 1024 + 2 * 1024 * 1024
    if not keep:
        scratch += [pltpu.VMEM((width, TILE), jnp.bfloat16)] * (2 * len(fetch))
        limit += 4 * width * TILE * len(fetch)
    out = pl.pallas_call(
        kernel,
        grid_spec=pltpu.PrefetchScalarGridSpec(
            num_scalar_prefetch=1, grid=(1,), in_specs=in_specs, out_specs=[vmem_spec] * len(out_shape), scratch_shapes=scratch),
        out_shape=out_shape,
        input_output_aliases=aliases,
        compiler_params=pltpu.CompilerParams(dimension_semantics=("arbitrary",), vmem_limit_bytes=limit),
        cost_estimate=pl.CostEstimate(
            flops=int(share * 4 * rows * width * TILE * len(compute)),
            bytes_accessed=1024 + int(share * 4 * width * TILE * len(compute)), transcendentals=0),
    )(*operands)
    tiles = {t: (out[2 * n], out[2 * n + 1]) for n, t in enumerate(order[:n_out // 2])}
    return tiles, out[n_out:]


def after_call(values, other):
    any_spec = pl.BlockSpec(memory_space=pl.ANY)

    def kernel(*refs):
        pass

    return pl.pallas_call(
        kernel,
        in_specs=[any_spec] * (len(values) + 1),
        out_specs=[any_spec] * len(values),
        out_shape=[jax.ShapeDtypeStruct(v.shape, v.dtype) for v in values],
        input_output_aliases={k: k for k in range(len(values))},
        compiler_params=pltpu.CompilerParams(vmem_limit_bytes=1024 * 1024),
        cost_estimate=pl.CostEstimate(flops=0, bytes_accessed=0, transcendentals=0),
    )(*values, other)


def quarter_of(block, row_total, block_len):
    per_quarter = row_total // block_len // 4
    quarter = block // per_quarter
    return quarter, pl.multiple_of((block - quarter * per_quarter) * block_len, block_len)


def table_call(meta, number, pieces, down, owned, row_total, block_len):
    rank, width = down.shape
    half = block_len // 2
    flat, places = flatten([pieces])
    n_pieces = len(flat)
    n_owned = len(owned)

    def kernel(*refs):
        meta_ref = refs[0]
        piece_refs = refs[1:1 + n_pieces]
        down_ref = refs[1 + n_pieces]
        owned_refs = refs[2 + n_pieces:2 + n_pieces + n_owned]
        mine_ref, other_ref, held, in_sem = refs[2 + n_pieces + n_owned:]
        core = meta_ref[0]
        copies = []
        for k, (_, sibling, offset, length) in enumerate(places):
            side = (1 - core) if sibling else core
            row = pl.multiple_of(side * half + offset, 32)
            copies.append(pltpu.make_async_copy(piece_refs[k], held.at[pl.ds(row, length)], in_sem.at[k]))
        for copy in copies:
            copy.start()

        def put(at, value):
            quarter, row = quarter_of(meta_ref[1 + FIELDS * at], row_total, block_len)
            for q in range(4):
                @pl.when(quarter == q)
                def _(q=q):
                    lanes = slice(q % 2 * rank, (q % 2 + 1) * rank)

                    @pl.when(core == q // 2)
                    def _():
                        mine_ref[pl.ds(row, block_len), lanes] = value

                    @pl.when(core != q // 2)
                    def _():
                        other_ref[pl.ds(row, block_len), lanes] = value

        at = 0
        for ref in owned_refs:
            for b in range(ref.shape[0] // block_len):
                put(at, ref[b * block_len:(b + 1) * block_len, :])
                at += 1
        for copy in copies:
            copy.wait()
        found = lax.dot_general(held[...], down_ref[...], (((1,), (1,)), ((), ())), preferred_element_type=jnp.float32)
        put(number, jnp.where(meta_ref[1 + FIELDS * number + 2] == 1, found, 0.0).astype(jnp.bfloat16))

    whole = pl.BlockSpec(memory_space=pltpu.VMEM)
    return pl.pallas_call(
        kernel,
        in_specs=[pl.BlockSpec(memory_space=pltpu.SMEM)] + [pl.BlockSpec(memory_space=pl.ANY)] * n_pieces + [whole] * (1 + n_owned),
        out_specs=[whole] * 2,
        out_shape=[jax.ShapeDtypeStruct((row_total // 4, 2 * rank), jnp.bfloat16)] * 2,
        scratch_shapes=[pltpu.VMEM((block_len, width), jnp.bfloat16), pltpu.SemaphoreType.DMA((n_pieces,))],
        compiler_params=pltpu.CompilerParams(vmem_limit_bytes=8 * 1024 * 1024),
        cost_estimate=pl.CostEstimate(flops=0, bytes_accessed=1024 * 1024, transcendentals=0),
    )(meta, *flat, down, *owned)


def add_call(values, other):
    vmem_spec = pl.BlockSpec(memory_space=pltpu.VMEM)

    def kernel(*refs):
        total = refs[0][...]
        for ref in refs[1:len(values)]:
            total = total + ref[...]
        refs[-1][...] = total

    return pl.pallas_call(
        kernel,
        in_specs=[vmem_spec] * len(values) + [pl.BlockSpec(memory_space=pl.ANY)],
        out_specs=vmem_spec,
        out_shape=jax.ShapeDtypeStruct(values[0].shape, values[0].dtype),
        compiler_params=pltpu.CompilerParams(vmem_limit_bytes=2 * 1024 * 1024),
        cost_estimate=pl.CostEstimate(flops=0, bytes_accessed=1024, transcendentals=0),
    )(*values, other)


def finish_call(meta, mine, other, lowrank_up, results, row_total, block_len):
    rank, columns = lowrank_up.shape[1:]
    total_blocks = row_total // block_len
    flat = []
    for result in results:
        flat += result[3:]
    n_flat = len(flat)

    def kernel(*refs):
        meta_ref, mine_ref, other_ref, map_ref = refs[:4]
        result_refs = refs[4:4 + n_flat]
        out_ref = refs[4 + n_flat]
        k = pl.program_id(0)
        quarter, row = quarter_of(meta_ref[1 + FIELDS * k], row_total, block_len)
        at_row = pl.ds(row, block_len)
        both = jnp.where(quarter // 2 == meta_ref[0], mine_ref[at_row, :], other_ref[at_row, :])
        reduced = jnp.where(lax.rem(quarter, 2) == 0, both[:, :rank], both[:, rank:])
        live = meta_ref[1 + FIELDS * k + 1]
        for n, (begun, count, column, prod, _) in enumerate(results):
            def run(n=n, begun=begun, count=count, column=column, prod=prod):
                base = 0
                for b in range(begun, begun + count - 1):
                    base = base + jnp.where(b < k, chunks_of(meta_ref, b), 0)
                at = pl.ds(pl.multiple_of(base * CHUNK, CHUNK), block_len)
                for c in range(0, prod.shape[1], TILE):
                    cols = slice(column + c, column + c + TILE)
                    term = jnp.dot(reduced, map_ref[0, :, cols], preferred_element_type=jnp.float32)
                    prods = result_refs[2 * n][at, c:c + TILE].astype(jnp.float32)
                    acts = result_refs[2 * n + 1][at, c:c + TILE].astype(jnp.float32)
                    sum_of = prods + acts * (lowrank_scale * term)
                    shown = lax.broadcasted_iota(jnp.int32, sum_of.shape, 0) < live
                    out_ref[:, cols] = jnp.where(shown, sum_of, 0.0).astype(jnp.bfloat16)

            pl.when(jnp.logical_and(k >= begun, k < begun + count))(run)

    vmem_spec = pl.BlockSpec(memory_space=pltpu.VMEM)
    return pl.pallas_call(
        kernel,
        grid_spec=pltpu.PrefetchScalarGridSpec(
            num_scalar_prefetch=1,
            grid=(total_blocks,),
            in_specs=[vmem_spec, vmem_spec, pl.BlockSpec((1, rank, columns), lambda k, m: (m[1 + FIELDS * k + 3], 0, 0))]
            + [vmem_spec] * n_flat,
            out_specs=pl.BlockSpec((block_len, columns), lambda k, m: (m[1 + FIELDS * k], 0)),
        ),
        out_shape=jax.ShapeDtypeStruct((row_total, columns), jnp.bfloat16),
        compiler_params=pltpu.CompilerParams(dimension_semantics=("arbitrary",), vmem_limit_bytes=16 * 1024 * 1024),
        cost_estimate=pl.CostEstimate(
            flops=2 * row_total * columns * 256, bytes_accessed=6 * row_total * columns, transcendentals=0),
    )(meta, mine, other, lowrank_up, *flat)


def on_ring(tokens, gate_matrix, up_matrix, lowrank_down, lowrank_up, tenant, adapter_storage_slot, live_count):
    block_count = tenant.shape[0]
    rows_here, width = tokens.shape
    chips = block_count
    block_len = 2 * rows_here
    row_total = block_count * block_len
    columns = gate_matrix.shape[1]
    me = lax.axis_index("tensor")
    core = lax.rem(me, 2)
    chip = me // 2
    place = jnp.where(lax.rem(chip, 2) == 0, chip // 2, chips - 1 - chip // 2)
    count = lax.iota(jnp.int32, block_count)
    order = jnp.where(lax.rem(count, 2) == 1, -(count + 1) // 2, count // 2)
    at = lax.rem(place + order + chips, chips)
    numbers = jnp.where(at < chips // 2, 2 * at, 2 * (chips - 1 - at) + 1)

    def pick(values, index):
        chosen = index[:, None] == lax.broadcasted_iota(jnp.int32, (index.shape[0], values.shape[0]), 1)
        return jnp.sum(jnp.where(chosen, values[None, :], 0), axis=1)

    slots = pick(adapter_storage_slot, pick(tenant, numbers))
    here = (slots == me).astype(jnp.int32)
    fields = jnp.stack([numbers, pick(live_count, numbers), here, slots], axis=1).astype(jnp.int32)
    meta = jnp.concatenate([core[None].astype(jnp.int32), fields.reshape(-1)])

    right, left = ring_pairs(chips, 1), ring_pairs(chips, -1)

    def send(value, pairs):
        return lax.ppermute(value, "tensor", pairs)

    def flip(value, bits):
        return lax.ppermute(value, "tensor", [(d, d ^ bits) for d in range(2 * chips)])

    down = lowrank_down[0]
    weights = (gate_matrix, up_matrix)
    n_tiles = columns // TILE
    from_left, from_right = tokens, tokens
    blocks = [[(tokens, False, 0), (flip(tokens, 1), True, 0)]]
    owned = []
    results = []
    first = 0
    for step in range(3):
        from_left = send(from_left, right)
        from_right = send(from_right, left)
        prod, act, part = pass_call(meta, first, blocks, down, *weights, 0, n_tiles, block_len, True, 0.0)
        results.append((first, len(blocks), 0, prod, act))
        owned.append(part)
        first += len(blocks)
        from_left, from_right = after_call((from_left, from_right), part)
        blocks = [[(v, False, 0), (flip(v, 1), True, 0)] for v in (from_left, from_right)]
    cut = rows_here // 2
    last_low = send(from_left[:cut], right)
    last_high = send(from_right[cut:], left)
    tiles, (prod, act, part) = tile_call(
        meta, first, blocks, down, *weights, {}, range(KEPT), range(KEPT), block_len, True, 0.0)
    results.append((first, 2, 0, prod, act))
    owned.append(part)
    last_low, last_high = after_call((last_low, last_high), part)
    blocks.append([
        (last_low, False, 0), (flip(last_low, 1), True, 0),
        (last_high, False, cut), (flip(last_high, 1), True, cut),
    ])
    mine, other = table_call(meta, first + 2, blocks[2], down, owned, row_total, block_len)
    more = range(KEPT, KEPT + FETCHED)
    tiles, (prod, act) = tile_call(
        meta, first + 2, blocks[2:], down, *weights, tiles, more, range(KEPT), block_len, False, 1.0)
    results.append((first + 2, 1, 0, prod, act))
    mine = add_call([mine, flip(other, 1), flip(mine, 2), flip(other, 3)], prod)
    met = [mine] + [flip(mine, 4 * k) for k in range(1, chips // 2)]
    _, (prod, act) = tile_call(
        meta, first, blocks, down, *weights, {t: tiles[t] for t in more}, range(KEPT + FETCHED, n_tiles - FETCHED),
        range(KEPT, n_tiles), block_len, False, 1.0, False, range(n_tiles - FETCHED, n_tiles))
    results.append((first, 3, KEPT * TILE, prod, act))
    mine = add_call(met, prod)
    other = flip(mine, 1)
    return finish_call(meta, mine, other, lowrank_up, results, row_total, block_len)


def on_device(
    tokens,
    gate_matrix,
    up_matrix,
    lowrank_down,
    lowrank_up,
    tenant,
    adapter_storage_slot,
    live_count,
):
    my_index = lax.axis_index("tensor")
    gathered = lax.all_gather(tokens, "tensor", axis=0, tiled=True)
    row_total = gathered.shape[0]
    width = gathered.shape[1]
    block_count = tenant.shape[0]
    block_len = row_total // block_count
    hidden_columns = gate_matrix.shape[1]
    gate_out = jnp.dot(gathered, gate_matrix, preferred_element_type=jnp.float32)
    up_output = jnp.dot(gathered, up_matrix, preferred_element_type=jnp.float32)
    slot_numbers = adapter_storage_slot[tenant]
    rows_block = gathered.reshape(block_count, block_len, width)
    per_replica = lowrank_down.shape[0]
    rank_width = lowrank_down.shape[1]
    first_slot = my_index * per_replica
    pieces = []
    for block in range(block_count):
        slot_here = slot_numbers[block]
        mine = jnp.logical_and(slot_here >= first_slot, slot_here < first_slot + per_replica)
        resident_slot = jnp.clip(slot_here - first_slot, 0, per_replica - 1)
        down_matrix = lax.dynamic_index_in_dim(lowrank_down, resident_slot, 0, keepdims=False)
        block_rows = rows_block[block]

        def product_fn(rows_in=block_rows, map_in=down_matrix):
            return lax.dot_general(
                rows_in, map_in, (((1,), (1,)), ((), ())), preferred_element_type=jnp.float32
            )

        def empty_fn():
            return jnp.zeros((block_len, rank_width), jnp.float32)

        pieces.append(lax.cond(mine, product_fn, empty_fn))
    partial_value = jnp.stack(pieces, axis=0)
    reduced_output = lax.psum(partial_value, "tensor").astype(jnp.bfloat16)
    every_slot = jnp.arange(lowrank_up.shape[0], dtype=jnp.int32)
    slot_indicator = (slot_numbers[:, None] == every_slot[None, :]).astype(jnp.bfloat16)
    adapter_up = jnp.einsum(
        "oe,exz->oxz", slot_indicator, lowrank_up, preferred_element_type=jnp.float32
    ).astype(jnp.bfloat16)
    lowrank_term = jnp.einsum(
        "who,wok->whk", reduced_output, adapter_up, preferred_element_type=jnp.float32
    )
    up_output = up_output + lowrank_scale * lowrank_term.reshape(row_total, hidden_columns)
    positions = jnp.arange(block_len, dtype=jnp.int32)
    live_rows = (positions[None, :] < live_count[:, None]).reshape(row_total, 1)
    hidden = jnp.where(live_rows, jax.nn.silu(gate_out) * up_output, 0.0)
    return hidden.astype(jnp.bfloat16)


def solution(mesh):
    placed = (
        P(("groups", "tensor"), None),
        P(None, "tensor"),
        P(None, "tensor"),
        P("tensor", None, None),
        P(None, None, "tensor"),
        P("groups"),
        P(),
        P("groups"),
    )
    run = on_ring if mesh.shape["tensor"] == 16 else on_device
    return jax.shard_map(
        run, mesh=mesh, in_specs=placed, out_specs=P("groups", "tensor"), check_vma=False
    )
```
